256 devices in a mesh: dom: 32 (over y, x, core), chan: 8 (over z).
Axes of the slice: x: 4, y: 4, z: 8, core: 2. Of those that a mesh axis runs over, the one named last changes fastest.
Arguments:
- feats: bfloat16 [131072, 512], P('dom', 'chan'), may hold values from -6 to 6
- block_vals: bfloat16 [1024, 8, 128, 128], P('dom'), may hold values from 0.019897461 to 1
- block_cols: int32 [1024, 8], P('dom'), may hold values from 0 to 159
- block_counts: int32 [1024], P('dom'), may hold values from 4 to 8
- send_list: int32 [32, 32, 4], P('dom'), may hold values from 0 to 31
- w_self: bfloat16 [512, 256], replicated, may hold values from -0.25 to 0.25
- w_neigh: bfloat16 [512, 256], replicated, may hold values from -6 to 6
- bias: float32 [256], replicated, may hold values from -4 to 4
- cotangent: bfloat16 [131072, 256], P(('dom', 'chan')), may hold values from -6 to 6
Outputs:
- out_h: bfloat16 [131072, 256], P(('dom', 'chan'))
- grad_feats: bfloat16 [131072, 512], P('dom', 'chan')
- grad_w_self: float32 [512, 256], P('chan')
- grad_w_neigh: float32 [512, 256], P('chan')
The draws below stay inside these ranges and needn't reach their ends.
All inputs are finite; a program needn't handle non-finite values.
Results may differ from the reference program's by a relative error of at most 0.02.
Values may be sent and summed in bfloat16 or wider, within the bound.
No kernel may reach another device: no remote copies, remote signals or barrier semaphores. Data moves between devices by JAX's collectives and lax.ppermute only.
A program may use at most 128 MiB of HBM per device.

```python
import math
import jax
import jax.numpy as jnp
from jax import lax

F_IN = 512
F_OUT = 256
BS = 128
KB = 8
MINB = 4
BRD = 32
NPART = 32
SLOTS = 4
NBR = 1024
NODES = 131072


def draw_block_cols(key, part):
    perm_keys = jax.random.split(jax.random.fold_in(key, 11), NPART)
    covered = jax.vmap(lambda one_key: jax.random.permutation(one_key, NPART * SLOTS))(perm_keys)
    covered = (covered.astype(jnp.int32) + BRD).reshape(NPART, BRD, MINB)
    further = jax.random.randint(jax.random.fold_in(key, 12), (NPART, BRD, KB - MINB), 0, BRD + NPART * SLOTS, dtype=jnp.int32)
    return jnp.concatenate([covered, further], axis=2).reshape(NBR, KB).astype(jnp.int32)


def draw_block_counts(key, part):
    ceiling = jax.random.randint(jax.random.fold_in(key, 21), (NPART, 1), MINB, KB + 1, dtype=jnp.int32)
    raw_draw = jax.random.randint(jax.random.fold_in(key, 22), (NPART, BRD), 0, 1 << 20, dtype=jnp.int32)
    counts = MINB + raw_draw % (ceiling - MINB + 1)
    return counts.reshape(NBR).at[0].set(KB).astype(jnp.int32)


def touch_ends(entries, own_key, smallest, high):
    spot = [jax.random.randint(jax.random.fold_in(own_key, axis), (), 0, length) for axis, length in enumerate(entries.shape)]
    widest = entries.shape.index(max(entries.shape))
    neighbour = spot[:widest] + [(spot[widest] + 1) % entries.shape[widest]] + spot[widest + 1:]
    return entries.at[tuple(spot)].set(smallest).at[tuple(neighbour)].set(high)


def block_scale(key, dims, cuts, least, top_value):
    def one(position, blocks):
        steps = jax.random.uniform(jax.random.fold_in(jax.random.fold_in(key, 6), position), (blocks,), jnp.float32, least / len(cuts), top_value / len(cuts))
        return jnp.repeat(jnp.exp(steps), dims[position] // blocks).reshape((-1,) + (1,) * (len(dims) - position - 1))

    gain = one(*cuts[0])
    for cut in cuts[1:]:
        gain = gain * one(*cut)
    return gain


def centred(key, shape, width, most, shards=(), kind=jnp.bfloat16):
    loudness = block_scale(key, shape, shards, -0.22, 0.18) if shards else 1.0
    array = jax.random.normal(key, shape, jnp.float32) * width * loudness
    return jnp.minimum(jnp.maximum(array, -most), most).astype(kind)


def setup_inputs(seed: int = 0) -> dict:
    splits = jax.random.split(jax.random.key(seed), 10)
    feats = centred(splits[0], (NODES, F_IN), 1.0, 6.0, ((0, 32), (1, 8)))
    block_vals = jnp.clip(jnp.exp(math.log(1.0) - 3.9171631 * jax.random.uniform(splits[1], (NBR, KB, BS, BS), jnp.float32) ** block_scale(splits[1], (NBR, KB, BS, BS), ((0, 32),), -0.2, 0.2)), 0.019897461, 1.0).astype(jnp.bfloat16)
    block_cols = draw_block_cols(jax.random.fold_in(splits[9], 71), 0)
    block_counts = draw_block_counts(jax.random.fold_in(splits[9], 71), 0)
    send_list = touch_ends(jax.random.randint(splits[4], (NPART, NPART, SLOTS), 0, BRD), jax.random.fold_in(splits[4], 1), 0, BRD - 1).astype(jnp.int32)
    w_self = centred(splits[5], (F_IN, F_OUT), F_IN ** -0.5, 0.25)
    w_neigh = centred(splits[6], (F_IN, F_OUT), (max(1, F_IN // (4 * BS))) ** -0.5, 6.0)
    bias = centred(splits[7], (F_OUT,), 1.0, 4.0, (), jnp.float32)
    cotangent = centred(splits[8], (NODES, F_OUT), 1.0, 6.0, ((0, 256),))
    return dict(feats=feats, block_vals=block_vals, block_cols=block_cols, block_counts=block_counts, send_list=send_list, w_self=w_self, w_neigh=w_neigh, bias=bias, cotangent=cotangent)


def layer_head(preact, cotangent):
    logistic = jax.nn.sigmoid(preact)
    activated = preact * logistic
    slope_value = logistic * (1.0 + preact * (1.0 - logistic))
    rms_value = jnp.sqrt(lax.optimization_barrier(jnp.mean(activated * activated, axis=-1, keepdims=True)) + 1e-06)
    unit_rows = activated / rms_value
    cot_value = cotangent.astype(jnp.float32)
    grad_act = (cot_value - unit_rows * lax.optimization_barrier(jnp.mean(cot_value * unit_rows, axis=-1, keepdims=True))) / rms_value
    return (unit_rows.astype(jnp.bfloat16), (grad_act * slope_value).astype(jnp.bfloat16))

def reference(feats, block_vals, block_cols, block_counts, send_list, w_self, w_neigh, bias, cotangent):
    partitions = NPART
    feat_blocks = feats.reshape(partitions, BRD, BS, F_IN)
    val_blocks = block_vals.reshape(partitions, BRD, KB, BS, BS)
    col_index = block_cols.reshape(partitions, BRD, KB)
    live_mask = (jnp.arange(KB, dtype=jnp.int32)[None, None, :] < block_counts.reshape(partitions, BRD)[:, :, None]).astype(jnp.float32)
    sources = jnp.arange(partitions, dtype=jnp.int32)[:, None]

    def forward_part(part_index):
        remote = feat_blocks[sources, send_list[:, part_index, :]]
        lookup_table = jnp.concatenate([feat_blocks[part_index], remote.reshape(partitions * SLOTS, BS, F_IN)], axis=0)
        picked = lookup_table[col_index[part_index]].astype(jnp.float32)
        blocks = val_blocks[part_index].astype(jnp.float32)
        weights = live_mask[part_index]
        summed = jnp.einsum('rkij,rkjc->ric', blocks * weights[:, :, None, None], picked)
        degree = jnp.einsum('rkij,rk->ri', blocks, weights)
        return (summed, degree)
    summed, degree = lax.map(forward_part, jnp.arange(partitions, dtype=jnp.int32))
    degree = degree.reshape(NODES, 1)
    neighbor_mean = (summed.reshape(NODES, F_IN) / degree).astype(jnp.bfloat16)
    preact = jnp.dot(feats, w_self, preferred_element_type=jnp.float32) + jnp.dot(neighbor_mean, w_neigh, preferred_element_type=jnp.float32) + bias
    out_h, grad_pre = layer_head(preact, cotangent)
    grad_scale = float(NODES) ** (-0.5)
    grad_w_self = jnp.dot(feats.T, grad_pre, preferred_element_type=jnp.float32) * grad_scale
    grad_w_neigh = jnp.dot(neighbor_mean.T, grad_pre, preferred_element_type=jnp.float32) * grad_scale
    grad_self = jnp.dot(grad_pre, w_self.T, preferred_element_type=jnp.float32).astype(jnp.bfloat16)
    grad_mean = jnp.dot(grad_pre, w_neigh.T, preferred_element_type=jnp.float32).astype(jnp.bfloat16)
    grad_scaled = (grad_mean.astype(jnp.float32) / degree).astype(jnp.bfloat16).reshape(partitions, BRD, BS, F_IN)

    def backward_part(grad_total, part_index):
        blocks = val_blocks[part_index].astype(jnp.float32) * live_mask[part_index][:, :, None, None]
        contrib = jnp.einsum('rkij,ric->rkjc', blocks, grad_scaled[part_index].astype(jnp.float32))
        table_grad = jnp.zeros((BRD + partitions * SLOTS, BS, F_IN), jnp.float32).at[col_index[part_index].reshape(-1)].add(contrib.reshape(BRD * KB, BS, F_IN))
        grad_total = grad_total.at[part_index].add(table_grad[:BRD])
        grad_total = grad_total.at[sources, send_list[:, part_index, :]].add(table_grad[BRD:].reshape(partitions, SLOTS, BS, F_IN))
        return (grad_total, None)
    grad_total, _ = lax.scan(backward_part, jnp.zeros((partitions, BRD, BS, F_IN), jnp.float32), jnp.arange(partitions, dtype=jnp.int32))
    grad_feats = (grad_self.astype(jnp.float32) + grad_total.reshape(NODES, F_IN)).astype(jnp.bfloat16)
    return (out_h, grad_feats, grad_w_self, grad_w_neigh)
```

```python
import functools

import jax
import jax.numpy as jnp
from jax import lax
from jax.experimental import pallas as pl
from jax.experimental.pallas import tpu as pltpu
from jax.sharding import PartitionSpec as P

BF = jnp.bfloat16
F32 = jnp.float32
MIB = 1 << 20


def vmem():
    return pl.BlockSpec(memory_space=pltpu.VMEM)


def smem():
    return pl.BlockSpec(memory_space=pltpu.SMEM)


def params(mib):
    return pltpu.CompilerParams(vmem_limit_bytes=mib * MIB)


def cost(flops, nbytes):
    return pl.CostEstimate(flops=flops, bytes_accessed=nbytes, transcendentals=0)


def nt_dot(left, right):
    return lax.dot_general(left, right, (((1,), (1,)), ((), ())), preferred_element_type=F32)


def nn_dot(left, right):
    return lax.dot_general(left, right, (((1,), (0,)), ((), ())), preferred_element_type=F32)


def pack_kernel(send_ref, feats_ref, out_ref):
    dests, slots, _, size = out_ref.shape

    def one(dest, carry):
        for slot in range(slots):
            lane = pl.multiple_of(send_ref[dest, slot] * size, size)
            out_ref[dest, slot] = feats_ref[:, pl.ds(lane, size)]
        return carry

    lax.fori_loop(0, dests, one, 0, unroll=4)


def split_kernel(me_ref, feats_ref, *out_refs):
    chans = len(out_refs)
    width = out_refs[0].shape[1]
    for shift, out_ref in enumerate(out_refs):
        lane = pl.multiple_of(lax.rem(me_ref[0] + shift, chans) * width, width)
        out_ref[...] = feats_ref[:, pl.ds(lane, width)]


def degree_kernel(counts_ref, vals_ref, out_ref):
    rows, depth, size, _ = vals_ref.shape
    ones = jnp.ones((16, size), BF)
    step = pl.program_id(0)
    for row in range(rows):
        count = counts_ref[step * rows + row]
        left = jnp.concatenate([jnp.where(k < count, ones, jnp.zeros_like(ones)) for k in range(depth)], axis=1)
        right = jnp.concatenate([vals_ref[row, k] for k in range(depth)], axis=1)
        total = nt_dot(left, right)
        out_ref[0, :, row * size : (row + 1) * size] = total[:8]


def gather_kernel(me_ref, cols_ref, counts_ref, feats_ref, recv_ref, degree_ref, vals_ref, *out_refs):
    rows, depth, size, _ = vals_ref.shape
    chans = len(out_refs)
    own = feats_ref.shape[1] // size
    step = pl.program_id(0)
    group = lax.rem(me_ref[0] + step, chans)
    parts = []
    for row in range(rows):
        index = group * rows + row
        count = counts_ref[index]
        picked = []
        for k in range(depth):
            col = cols_ref[index, k]
            lane = pl.multiple_of(jnp.minimum(col, own - 1) * size, size)
            near = feats_ref[:, pl.ds(lane, size)]
            far = recv_ref[jnp.maximum(col - own, 0)]
            block = jnp.where(col < own, near, far)
            picked.append(jnp.where(k < count, block, jnp.zeros_like(block)))
        left = jnp.concatenate(picked, axis=1)
        right = jnp.concatenate([vals_ref[row, k] for k in range(depth)], axis=1)
        total = nt_dot(left, right)
        scale = degree_ref[group, 0:1, row * size : (row + 1) * size]
        parts.append((total / scale).astype(BF))
    for shift, out_ref in enumerate(out_refs):

        @pl.when(step == shift)
        def _():
            for row in range(rows):
                out_ref[:, row * size : (row + 1) * size] = parts[row]


def assemble(me_ref, chunk_refs, full_ref):
    chans = len(chunk_refs)
    height = chunk_refs[0].shape[0]
    for shift, chunk_ref in enumerate(chunk_refs):
        start = pl.multiple_of(lax.rem(me_ref[0] + (chans - shift), chans) * height, height)
        full_ref[pl.ds(start, height), :] = chunk_ref[...]


def self_kernel(chans, me_ref, weight_ref, bias_ref, *refs):
    chunk_refs = refs[:chans]
    full_ref, pre_ref = refs[chans:]
    assemble(me_ref, chunk_refs, full_ref)
    pre_ref[...] = nn_dot(weight_ref[...], full_ref[...]) + bias_ref[...]


def head_kernel(chans, me_ref, degree_ref, pre_ref, turned_ref, weight_ref, cot_ref, *refs):
    chunk_refs = refs[:chans]
    mean_ref, out_ref, grad_ref = refs[chans : chans + 3]
    scaled_refs = refs[chans + 3 : 2 * chans + 3]
    (hold_ref,) = refs[2 * chans + 3 :]
    assemble(me_ref, chunk_refs, mean_ref)
    preact = pre_ref[...] + nn_dot(turned_ref[...], mean_ref[...])
    logistic = jax.nn.sigmoid(preact)
    activated = preact * logistic
    slope = logistic * (1.0 + preact * (1.0 - logistic))
    inverse = 1.0 / jnp.sqrt(jnp.mean(activated * activated, axis=0, keepdims=True) + 1e-06)
    unit = activated * inverse
    cot = cot_ref[...].astype(F32)
    grad_act = (cot - unit * jnp.mean(cot * unit, axis=0, keepdims=True)) * inverse
    grad = (grad_act * slope).astype(BF)
    out_ref[...] = unit.astype(BF)
    grad_ref[...] = grad
    mean_grad = nn_dot(weight_ref[...], grad).astype(BF).astype(F32)
    degree = degree_ref[me_ref[0], 0:1, :]
    hold_ref[...] = (mean_grad / degree).astype(BF)
    height = scaled_refs[0].shape[0]
    for shift, scaled_ref in enumerate(scaled_refs):
        start = pl.multiple_of(lax.rem(me_ref[0] + shift, chans) * height, height)
        scaled_ref[...] = hold_ref[pl.ds(start, height), :]


def side_kernel(chans, me_ref, weight_ref, feats_ref, mean_ref, out_ref, grad_ref, *refs):
    turned_ref = refs[0]
    packed_refs = refs[1 : chans + 1]
    (hold_ref,) = refs[chans + 1 :]
    turned_ref[...] = out_ref[...].T
    grad = grad_ref[...]
    nodes = grad.shape[1]
    feature = grad.shape[0]
    hold_ref[:, :nodes] = nn_dot(weight_ref[...], grad).astype(BF)
    hold_ref[:, nodes : nodes + feature] = nt_dot(feats_ref[...], grad).astype(BF)
    hold_ref[:, nodes + feature :] = nt_dot(mean_ref[...], grad).astype(BF)
    height = packed_refs[0].shape[0]
    for shift, packed_ref in enumerate(packed_refs):
        start = pl.multiple_of(lax.rem(me_ref[0] + shift, chans) * height, height)
        packed_ref[...] = hold_ref[pl.ds(start, height), :]


def scatter_kernel(chans, me_ref, cols_ref, counts_ref, vals_ref, *refs):
    chunk_refs = refs[:chans]
    own_ref, far_ref, hold_ref = refs[chans:]
    rows, depth, size, _ = vals_ref.shape
    own = own_ref.shape[0]
    step = pl.program_id(0)
    group = lax.rem(me_ref[0] + (chans - step), chans)

    @pl.when(step == 0)
    def _():
        hold_ref[...] = jnp.zeros_like(hold_ref)

    for shift, chunk_ref in enumerate(chunk_refs):

        @pl.when(step == shift)
        def _():
            for row in range(rows):
                index = group * rows + row
                count = counts_ref[index]
                left = chunk_ref[:, row * size : (row + 1) * size]
                right = jnp.concatenate([vals_ref[row, k] for k in range(depth)], axis=1)
                total = nn_dot(left, right)
                for k in range(depth):
                    col = cols_ref[index, k]
                    part = total[:, k * size : (k + 1) * size]
                    hold_ref[col] += jnp.where(k < count, part, jnp.zeros_like(part))

    @pl.when(step == chans - 1)
    def _():
        own_ref[...] = hold_ref[:own]
        far_ref[...] = hold_ref[own:].astype(BF)


def weight_kernel(*refs):
    packed_refs = refs[:-1]
    out_ref = refs[-1]
    width = out_ref.shape[1]
    total = packed_refs[0][:, width:].astype(F32)
    for packed_ref in packed_refs[1:]:
        total = total + packed_ref[:, width:].astype(F32)
    out_ref[...] = total.astype(BF)


def final_kernel(chans, me_ref, send_ref, own_ref, back_ref, *refs):
    packed_refs = refs[:chans]
    out_ref, hold_ref = refs[chans:]
    dests, slots = send_ref.shape
    blocks, _, size = hold_ref.shape
    rows = blocks // chans
    hold_ref[...] = own_ref[...]

    def one(dest, carry):
        for slot in range(slots):
            hold_ref[send_ref[dest, slot]] += back_ref[dest, slot].astype(F32)
        return carry

    lax.fori_loop(0, dests, one, 0, unroll=4)
    for shift, packed_ref in enumerate(packed_refs):
        group = lax.rem(me_ref[0] + (chans - shift), chans)
        for row in range(rows):
            index = group * rows + row
            total = hold_ref[index] + packed_ref[:, row * size : (row + 1) * size].astype(F32)
            out_ref[:, pl.ds(pl.multiple_of(index * size, size), size)] = total.astype(BF)


def exchange(chunks):
    count = len(chunks)
    return [chunks[0]] + [
        lax.ppermute(chunks[shift], "chan", [(i, (i + shift) % count) for i in range(count)])
        for shift in range(1, count)
    ]


def sds(shape, dtype):
    return jax.ShapeDtypeStruct(shape, dtype)


def per_device(feats, block_vals, block_cols, block_counts, send_list, w_self, w_neigh, bias, cotangent):
    node_count, chan_width = feats.shape
    block_rows, depth, size, _ = block_vals.shape
    parts = lax.axis_size("dom")
    chans = lax.axis_size("chan")
    slots = send_list.shape[2]
    f_in, f_out = w_self.shape
    nodes = node_count // chans
    rows = block_rows // chans
    table = block_rows + parts * slots
    me = lax.axis_index("chan").astype(jnp.int32).reshape(1)
    send = send_list[0]
    feats_t = feats.T
    val_bytes = block_vals.size * 2
    block_flops = 2 * block_rows * depth * size * size * chan_width

    outgoing = pl.pallas_call(
        pack_kernel,
        out_shape=sds((parts, slots, chan_width, size), BF),
        in_specs=[smem(), vmem()],
        out_specs=vmem(),
        compiler_params=params(16),
        cost_estimate=cost(0, 5 * MIB),
        name="pack_outgoing",
    )(send, feats_t)
    incoming = lax.all_to_all(outgoing, "dom", split_axis=0, concat_axis=0, tiled=True)

    feat_chunks = pl.pallas_call(
        split_kernel,
        out_shape=[sds((chan_width, nodes), BF)] * chans,
        in_specs=[smem(), vmem()],
        out_specs=[vmem()] * chans,
        compiler_params=params(16),
        cost_estimate=cost(0, MIB),
        name="split_feats",
    )(me, feats_t)
    feat_chunks = exchange(feat_chunks)
    degree = pl.pallas_call(
        degree_kernel,
        grid_spec=pltpu.PrefetchScalarGridSpec(
            num_scalar_prefetch=1,
            grid=(chans,),
            in_specs=[pl.BlockSpec((rows, depth, size, size), lambda i, *_: (i, 0, 0, 0))],
            out_specs=pl.BlockSpec((1, 8, nodes), lambda i, *_: (i, 0, 0)),
        ),
        out_shape=sds((chans, 8, nodes), F32),
        compiler_params=params(16),
        cost_estimate=cost(block_flops // 4, val_bytes),
        name="degree",
    )(block_counts, block_vals)
    feats_own, pre_self = pl.pallas_call(
        functools.partial(self_kernel, chans),
        out_shape=[sds((f_in, nodes), BF), sds((f_out, nodes), F32)],
        in_specs=[smem(), vmem(), vmem()] + [vmem()] * chans,
        out_specs=[vmem()] * 2,
        compiler_params=params(16),
        cost_estimate=cost(2 * f_in * f_out * nodes, 2 * MIB),
        name="self_part",
    )(me, w_self.T, bias.reshape(f_out, 1), *feat_chunks)

    mean_chunks = pl.pallas_call(
        gather_kernel,
        grid_spec=pltpu.PrefetchScalarGridSpec(
            num_scalar_prefetch=3,
            grid=(chans,),
            in_specs=[
                vmem(),
                vmem(),
                vmem(),
                pl.BlockSpec((rows, depth, size, size), lambda i, me, *_: (lax.rem(me[0] + i, chans), 0, 0, 0)),
            ],
            out_specs=[vmem()] * chans,
        ),
        out_shape=[sds((chan_width, nodes), BF)] * chans,
        compiler_params=params(24),
        cost_estimate=cost(block_flops, val_bytes + 3 * MIB),
        name="neighbour_mean",
    )(me, block_cols, block_counts, feats_t, incoming.reshape(parts * slots, chan_width, size), degree, block_vals)
    mean_chunks = exchange(mean_chunks)

    head = pl.pallas_call(
        functools.partial(head_kernel, chans),
        out_shape=[sds((f_in, nodes), BF), sds((f_out, nodes), BF), sds((f_out, nodes), BF)]
        + [sds((chan_width, nodes), BF)] * chans,
        in_specs=[smem()] + [vmem()] * (5 + chans),
        out_specs=[vmem()] * (3 + chans),
        scratch_shapes=[pltpu.VMEM((f_in, nodes), BF)],
        compiler_params=params(32),
        cost_estimate=cost(4 * f_in * f_out * nodes, 4 * MIB),
        name="layer_head",
    )(me, degree, pre_self, w_neigh.T, w_neigh, cotangent.T, *mean_chunks)
    mean_own, out_t, grad_t = head[:3]
    scaled_chunks = exchange(head[3:])

    side = pl.pallas_call(
        functools.partial(side_kernel, chans),
        out_shape=[sds((nodes, f_out), BF)] + [sds((chan_width, nodes + 2 * f_out), BF)] * chans,
        in_specs=[smem()] + [vmem()] * 5,
        out_specs=[vmem()] * (1 + chans),
        scratch_shapes=[pltpu.VMEM((f_in, nodes + 2 * f_out), BF)],
        compiler_params=params(32),
        cost_estimate=cost(6 * f_in * f_out * nodes, 4 * MIB),
        name="side_grads",
    )(me, w_self, feats_own, mean_own, out_t, grad_t)
    out_h = side[0]

    own_grad, far_grad = pl.pallas_call(
        functools.partial(scatter_kernel, chans),
        grid_spec=pltpu.PrefetchScalarGridSpec(
            num_scalar_prefetch=3,
            grid=(chans,),
            in_specs=[
                pl.BlockSpec(
                    (rows, depth, size, size), lambda i, me, *_: (lax.rem(me[0] + (chans - i), chans), 0, 0, 0)
                ),
            ]
            + [vmem()] * chans,
            out_specs=[vmem()] * 2,
            scratch_shapes=[pltpu.VMEM((table, chan_width, size), F32)],
        ),
        out_shape=[sds((block_rows, chan_width, size), F32), sds((parts * slots, chan_width, size), BF)],
        compiler_params=params(32),
        cost_estimate=cost(block_flops, val_bytes + 4 * MIB),
        name="table_grad",
    )(me, block_cols, block_counts, block_vals, *scaled_chunks)
    back = lax.all_to_all(
        far_grad.reshape(parts, slots, chan_width, size), "dom", split_axis=0, concat_axis=0, tiled=True
    )

    packed = exchange(side[1:])
    weight_sum = pl.pallas_call(
        weight_kernel,
        out_shape=sds((chan_width, 2 * f_out), BF),
        in_specs=[vmem()] * chans,
        out_specs=vmem(),
        compiler_params=params(16),
        cost_estimate=cost(0, MIB),
        name="weight_sum",
    )(*packed)
    flip = 1
    while flip < parts:
        other = lax.ppermute(weight_sum, "dom", [(i, i ^ flip) for i in range(parts)])
        total = weight_sum.astype(F32) + other.astype(F32)
        flip *= 2
        if flip < parts:
            weight_sum = total.astype(BF)
    total = total * (float(node_count * parts) ** (-0.5))
    grad_w_self = total[:, :f_out]
    grad_w_neigh = total[:, f_out:]

    grad_feats = pl.pallas_call(
        functools.partial(final_kernel, chans),
        out_shape=sds((chan_width, node_count), BF),
        in_specs=[smem(), smem()] + [vmem()] * (2 + chans),
        out_specs=vmem(),
        scratch_shapes=[pltpu.VMEM((block_rows, chan_width, size), F32)],
        compiler_params=params(24),
        cost_estimate=cost(0, 6 * MIB),
        name="sum_returned",
    )(me, send, own_grad, back, *packed)
    return (out_h, grad_feats.T, grad_w_self, grad_w_neigh)


def solution(mesh):
    return jax.shard_map(
        per_device,
        mesh=mesh,
        in_specs=(
            P("dom", "chan"),
            P("dom", None, None, None),
            P("dom", None),
            P("dom"),
            P("dom", None, None),
            P(),
            P(),
            P(),
            P(("dom", "chan"), None),
        ),
        out_specs=(P(("dom", "chan"), None), P("dom", "chan"), P("chan", None), P("chan", None)),
        check_vma=False,
    )
```

```python
import functools

import jax
import jax.numpy as jnp
from jax import lax
from jax.experimental import pallas as pl
from jax.experimental.pallas import tpu as pltpu
from jax.sharding import PartitionSpec as P

BF = jnp.bfloat16
F32 = jnp.float32
MIB = 1 << 20
BIG = 8


def vmem():
    return pl.BlockSpec(memory_space=pltpu.VMEM)


def hbm():
    return pl.BlockSpec(memory_space=pltpu.HBM)


def smem():
    return pl.BlockSpec(memory_space=pltpu.SMEM)


def params(mib):
    return pltpu.CompilerParams(vmem_limit_bytes=mib * MIB)


def cost(flops, nbytes):
    return pl.CostEstimate(flops=flops, bytes_accessed=nbytes, transcendentals=0)


def nt_dot(left, right):
    return lax.dot_general(left, right, (((1,), (1,)), ((), ())), preferred_element_type=F32)


def nn_dot(left, right):
    return lax.dot_general(left, right, (((1,), (0,)), ((), ())), preferred_element_type=F32)


def pack_kernel(send_ref, feats_ref, out_ref, hold_ref, sems):
    dests, slots, _, size = hold_ref.shape
    copies = sems.shape[0]
    span = dests // copies
    for copy in range(copies):
        for dest in range(copy * span, (copy + 1) * span):
            for slot in range(slots):
                lane = pl.multiple_of(send_ref[slot, dest] * size, size)
                hold_ref[dest, slot] = feats_ref[:, pl.ds(lane, size)]
        place = pl.ds(copy * span, span)
        pltpu.make_async_copy(hold_ref.at[place], out_ref.at[place], sems.at[copy]).start()
    for copy in range(copies):
        place = pl.ds(copy * span, span)
        pltpu.make_async_copy(hold_ref.at[place], out_ref.at[place], sems.at[copy]).wait()


def split_kernel(me_ref, feats_ref, *out_refs):
    chans = len(out_refs)
    width = out_refs[0].shape[1]
    for shift, out_ref in enumerate(out_refs):
        lane = pl.multiple_of(lax.rem(me_ref[0] + shift, chans) * width, width)
        out_ref[...] = feats_ref[:, pl.ds(lane, width)]


def join_slots(vals_ref, row):
    return jnp.concatenate([vals_ref[row, k] for k in range(vals_ref.shape[1])], axis=1)


def stream_rows(vals_ref, held_ref, sems, body):
    copies = sems.shape[0]
    span = held_ref.shape[0] // copies

    def copy(place):
        rows = pl.ds(place * span, span)
        return pltpu.make_async_copy(vals_ref.at[rows], held_ref.at[rows], sems.at[place])

    for place in range(copies):
        copy(place).start()

    def one(place, carry):
        copy(place).wait()
        for row in range(span):
            body(place * span + row)
        return carry

    lax.fori_loop(0, copies, one, 0)


def gather_kernel(cols_ref, counts_ref, feats_ref, recv_ref, vals_ref, out_ref, degree_ref, held_ref, sems):
    _, depth, size, _ = vals_ref.shape
    width = feats_ref.shape[0]
    rows = out_ref.shape[2] // size
    own = feats_ref.shape[1] // size
    ones = jnp.ones((16, size), BF)

    def body(index):
        count = counts_ref[index]
        picked = []
        for k in range(depth):
            col = cols_ref[k, index]
            lane = pl.multiple_of(jnp.minimum(col, own - 1) * size, size)
            near = feats_ref[:, pl.ds(lane, size)]
            far = recv_ref[jnp.maximum(col - own, 0)]
            block = jnp.concatenate([jnp.where(col < own, near, far), ones], axis=0)
            picked.append(jnp.where(k < count, block, jnp.zeros_like(block)))
        total = nt_dot(join_slots(held_ref, index), jnp.concatenate(picked, axis=1)).T
        group = index // rows
        place = pl.ds(pl.multiple_of(lax.rem(index, rows) * size, size), size)
        degree_ref[group, :, place] = total[width : width + 8]
        out_ref[group, :, place] = (total[:width] / total[width : width + 1]).astype(BF)

    stream_rows(vals_ref, held_ref, sems, body)


def self_kernel(chans, me_ref, weight_ref, bias_ref, neigh_ref, cot_ref, *refs):
    chunk_refs = refs[:chans]
    full_ref, pre_ref, neigh_turned_ref, cot_turned_ref = refs[chans:]
    neigh_turned_ref[...] = neigh_ref[...].T
    cot_turned_ref[...] = cot_ref[...].T
    height = chunk_refs[0].shape[0]
    for shift, chunk_ref in enumerate(chunk_refs):
        start = pl.multiple_of(lax.rem(me_ref[0] + (chans - shift), chans) * height, height)
        full_ref[pl.ds(start, height), :] = chunk_ref[...]
    pre_ref[...] = nn_dot(weight_ref[...].T, full_ref[...]) + bias_ref[...]


def head_kernel(me_ref, degree_ref, pre_ref, turned_ref, weight_ref, cot_ref, mean_ref, out_ref, grad_ref, scaled_ref):
    preact = pre_ref[...] + nn_dot(turned_ref[...], mean_ref[...])
    logistic = jax.nn.sigmoid(preact)
    activated = preact * logistic
    slope = logistic * (1.0 + preact * (1.0 - logistic))
    inverse = 1.0 / jnp.sqrt(jnp.mean(activated * activated, axis=0, keepdims=True) + 1e-06)
    unit = activated * inverse
    cot = cot_ref[...].astype(F32)
    grad_act = (cot - unit * jnp.mean(cot * unit, axis=0, keepdims=True)) * inverse
    grad = (grad_act * slope).astype(BF)
    out_ref[...] = unit.astype(BF)
    grad_ref[...] = grad
    mean_grad = nn_dot(weight_ref[...], grad).astype(BF).astype(F32)
    degree = degree_ref[me_ref[0], 0:1, :]
    scaled_ref[...] = (mean_grad / degree).astype(BF)


def weight_partial_kernel(me_ref, feats_ref, mean_ref, grad_ref, keep_ref, give_ref, hold_ref):
    parts, chans, unit, lanes = hold_ref.shape
    grad = grad_ref[...]
    totals = [nt_dot(feats_ref[...], grad), nt_dot(mean_ref[...], grad)]
    width = totals[0].shape[0] // chans
    halves = totals[0].shape[1] // lanes
    count = width // unit
    for which, total in enumerate(totals):
        for half in range(halves):
            place = (which * halves + half) * count
            for chan in range(chans):
                piece = total[chan * width : (chan + 1) * width, half * lanes : (half + 1) * lanes]
                hold_ref[place : place + count, chan] = piece.reshape(count, unit, lanes)
    half = parts // 2
    bit = me_ref[0]
    keep_ref[...] = hold_ref[pl.ds(bit * half, half)]
    give_ref[...] = hold_ref[pl.ds((1 - bit) * half, half)].astype(BF)


def halve_kernel(me_ref, held_ref, recv_ref, keep_ref, give_ref, hold_ref):
    half = keep_ref.shape[0]
    bit = me_ref[0]
    hold_ref[...] = held_ref[...] + recv_ref[...].astype(F32)
    keep_ref[...] = hold_ref[pl.ds(bit * half, half)]
    give_ref[...] = hold_ref[pl.ds((1 - bit) * half, half)].astype(BF)


def add_round_kernel(held_ref, recv_ref, out_ref):
    out_ref[...] = (held_ref[...] + recv_ref[...].astype(F32)).astype(BF)


def add_pair_kernel(held_ref, recv_ref, out_ref):
    out_ref[...] = (held_ref[...].astype(F32) + recv_ref[...].astype(F32)).astype(BF)


def turn_kernel(out_ref, turned_ref):
    turned_ref[...] = out_ref[...].T


def message_kernel(chans, me_ref, unit_ref, *packed_refs):
    units, _, unit, lanes = unit_ref.shape
    for shift, packed_ref in enumerate(packed_refs):
        dest = lax.rem(me_ref[0] + shift, chans)
        piece = unit_ref[:, dest].astype(F32).reshape(units * unit, lanes)
        packed_ref[...] = piece.astype(BF)


def scatter_kernel(
    cols_ref, counts_ref, vals_ref, scaled_ref, own_ref, far_ref, held_ref, hold_ref, send_ref, val_sems, sems, own_sem
):
    _, depth, size, _ = vals_ref.shape
    rows = scaled_ref.shape[2] // size
    own = own_ref.shape[0]
    hold_ref[...] = jnp.zeros_like(hold_ref)

    def body(index):
        count = counts_ref[index]
        place = pl.ds(pl.multiple_of(lax.rem(index, rows) * size, size), size)
        total = nn_dot(scaled_ref[index // rows, :, place], join_slots(held_ref, index))
        for k in range(depth):
            part = total[:, k * size : (k + 1) * size]
            hold_ref[cols_ref[k, index]] += jnp.where(k < count, part, jnp.zeros_like(part))

    stream_rows(vals_ref, held_ref, val_sems, body)
    copies = sems.shape[0]
    span = far_ref.shape[0] // copies
    for copy in range(copies):
        send_ref[copy * span : (copy + 1) * span] = hold_ref[own + copy * span : own + (copy + 1) * span].astype(BF)
        place = pl.ds(copy * span, span)
        pltpu.make_async_copy(send_ref.at[place], far_ref.at[place], sems.at[copy]).start()
    pltpu.make_async_copy(hold_ref.at[pl.ds(0, own)], own_ref, own_sem).start()
    for copy in range(copies):
        place = pl.ds(copy * span, span)
        pltpu.make_async_copy(send_ref.at[place], far_ref.at[place], sems.at[copy]).wait()
    pltpu.make_async_copy(hold_ref.at[pl.ds(0, own)], own_ref, own_sem).wait()


def unit_kernel(*refs):
    packed_refs = refs[:-1]
    out_ref = refs[-1]
    total = packed_refs[0][...].astype(F32)
    for packed_ref in packed_refs[1:]:
        total = total + packed_ref[...].astype(F32)
    out_ref[...] = total.astype(BF)


def spread_kernel(scale, me_ref, held_ref, self_ref, neigh_ref):
    pieces, rows, lanes = held_ref.shape
    half = pieces // 2
    unit_rows = self_ref.shape[0]
    per = unit_rows // rows
    for place in range(pieces):
        value = held_ref[lax.bitwise_xor(me_ref[0], place)].astype(F32) * scale
        target = self_ref if place < half else neigh_ref
        inside = place % half
        column, row = inside // per, inside % per
        target[row * rows : (row + 1) * rows, column * lanes : (column + 1) * lanes] = value


def near_kernel(me_ref, weight_ref, grad_ref, own_ref, out_ref):
    blocks, width, size = out_ref.shape
    chans, _, nodes = grad_ref.shape
    rows = nodes // size
    weight = weight_ref[pl.ds(pl.multiple_of(me_ref[0] * width, width), width), :]
    for group in range(chans):
        total = nn_dot(weight, grad_ref[group]).astype(BF).astype(F32)
        for row in range(rows):
            index = group * rows + row
            out_ref[index] = own_ref[index] + total[:, row * size : (row + 1) * size]


def final_kernel(send_ref, near_ref, back_ref, out_ref, hold_ref):
    slots, dests = send_ref.shape
    blocks, _, size = hold_ref.shape
    hold_ref[...] = near_ref[...]

    def one(dest, carry):
        for slot in range(slots):
            hold_ref[send_ref[slot, dest]] += back_ref[dest, slot].astype(F32)
        return carry

    lax.fori_loop(0, dests, one, 0, unroll=8)
    for block in range(blocks):
        out_ref[:, block * size : (block + 1) * size] = hold_ref[block].astype(BF)


def exchange(chunks):
    count = len(chunks)
    return [chunks[0]] + [
        lax.ppermute(chunks[shift], "chan", [(i, (i + shift) % count) for i in range(count)])
        for shift in range(1, count)
    ]


def sds(shape, dtype):
    return jax.ShapeDtypeStruct(shape, dtype)


def halving_order(parts):
    count = parts.bit_length() - 1
    return [bit for bit in (0, 1, 3, 2, 4) if bit < count] + list(range(5, count))


def add_round(kernel, left, right):
    return pl.pallas_call(
        kernel,
        out_shape=sds(left.shape, BF),
        in_specs=[vmem()] * 2,
        out_specs=vmem(),
        compiler_params=params(BIG),
        cost_estimate=cost(0, MIB),
        name="weight_add",
    )(left, right)


def per_device(feats, block_vals, block_cols, block_counts, send_list, w_self, w_neigh, bias, cotangent):
    node_count, chan_width = feats.shape
    block_rows, depth, size, _ = block_vals.shape
    parts = lax.axis_size("dom")
    chans = lax.axis_size("chan")
    slots = send_list.shape[2]
    f_in, f_out = w_self.shape
    nodes = node_count // chans
    rows = block_rows // chans
    table = block_rows + parts * slots
    chan = lax.axis_index("chan").astype(jnp.int32)
    part = lax.axis_index("dom").astype(jnp.int32)
    me = chan.reshape(1)
    send = send_list[0].T
    cols = block_cols.T
    feats_t = feats.T
    val_bytes = block_vals.size * 2
    vals = pltpu.with_memory_space_constraint(block_vals, pltpu.HBM)
    block_flops = 2 * block_rows * depth * size * size * chan_width
    layer_flops = 2 * f_in * f_out * nodes
    unit, lanes = 8, 128
    copies, streams = 8, 4

    outgoing = pl.pallas_call(
        pack_kernel,
        out_shape=pltpu.HBM((parts, slots, chan_width, size), BF),
        in_specs=[smem(), vmem()],
        out_specs=hbm(),
        scratch_shapes=[pltpu.VMEM((parts, slots, chan_width, size), BF), pltpu.SemaphoreType.DMA((copies,))],
        compiler_params=params(8),
        cost_estimate=cost(0, 5 * MIB),
        name="pack_outgoing",
    )(send, feats_t)
    incoming = lax.all_to_all(outgoing, "dom", split_axis=0, concat_axis=0, tiled=True)

    feat_chunks = pl.pallas_call(
        split_kernel,
        out_shape=[sds((chan_width, nodes), BF)] * chans,
        in_specs=[smem(), vmem()],
        out_specs=[vmem()] * chans,
        compiler_params=params(BIG),
        cost_estimate=cost(0, MIB),
        name="split_feats",
    )(me, feats_t)
    feat_chunks = exchange(feat_chunks)
    feats_own, pre_self, neigh_turned, cot_turned = pl.pallas_call(
        functools.partial(self_kernel, chans),
        out_shape=[sds((f_in, nodes), BF), sds((f_out, nodes), F32), sds((f_out, f_in), BF), sds((f_out, nodes), BF)],
        in_specs=[smem()] + [vmem()] * (4 + chans),
        out_specs=[vmem()] * 4,
        compiler_params=params(BIG),
        cost_estimate=cost(layer_flops, 2 * MIB),
        name="self_part",
    )(me, w_self, bias.reshape(f_out, 1), w_neigh, cotangent, *feat_chunks)

    incoming, pre_self, feats_own, neigh_turned, cot_turned = lax.optimization_barrier(
        (incoming, pre_self, feats_own, neigh_turned, cot_turned)
    )
    mean, degree = pl.pallas_call(
        gather_kernel,
        out_shape=[sds((chans, chan_width, nodes), BF), sds((chans, 8, nodes), F32)],
        in_specs=[smem(), smem()] + [vmem()] * 2 + [hbm()],
        out_specs=[vmem()] * 2,
        scratch_shapes=[pltpu.VMEM(block_vals.shape, BF), pltpu.SemaphoreType.DMA((streams,))],
        compiler_params=params(16),
        cost_estimate=cost(block_flops, val_bytes + 3 * MIB),
        name="neighbour_mean",
    )(cols, block_counts, feats_t, incoming.reshape(parts * slots, chan_width, size), vals)
    mean = lax.all_to_all(mean, "chan", split_axis=0, concat_axis=0, tiled=True).reshape(f_in, nodes)

    out_t, grad_t, scaled = pl.pallas_call(
        head_kernel,
        out_shape=[sds((f_out, nodes), BF), sds((f_out, nodes), BF), sds((f_in, nodes), BF)],
        in_specs=[smem()] + [vmem()] * 6,
        out_specs=[vmem()] * 3,
        compiler_params=params(BIG),
        cost_estimate=cost(2 * layer_flops, 4 * MIB),
        name="layer_head",
    )(me, degree, pre_self, neigh_turned, w_neigh, cot_turned, mean)
    scaled = lax.all_to_all(
        scaled.reshape(chans, chan_width, nodes), "chan", split_axis=0, concat_axis=0, tiled=True
    )

    order = halving_order(parts)
    halves, wholes = order[:3], order[3:]
    flips = [[(i, i ^ (1 << bit)) for i in range(parts)] for bit in order]
    bits = [((part >> bit) & 1).reshape(1) for bit in order]
    pieces = parts
    keep, give = pl.pallas_call(
        weight_partial_kernel,
        out_shape=[sds((pieces // 2, chans, unit, lanes), F32), sds((pieces // 2, chans, unit, lanes), BF)],
        in_specs=[smem()] + [vmem()] * 3,
        out_specs=[vmem()] * 2,
        scratch_shapes=[pltpu.VMEM((pieces, chans, unit, lanes), F32)],
        compiler_params=params(BIG),
        cost_estimate=cost(2 * layer_flops, 3 * MIB),
        name="weight_partial",
    )(bits[0], feats_own, mean, grad_t)
    pieces //= 2
    for level in range(1, len(halves)):
        got = lax.ppermute(give, "dom", flips[level - 1])
        keep, give = pl.pallas_call(
            halve_kernel,
            out_shape=[sds((pieces // 2, chans, unit, lanes), F32), sds((pieces // 2, chans, unit, lanes), BF)],
            in_specs=[smem()] + [vmem()] * 2,
            out_specs=[vmem()] * 2,
            scratch_shapes=[pltpu.VMEM((pieces, chans, unit, lanes), F32)],
            compiler_params=params(BIG),
            cost_estimate=cost(0, MIB),
            name="weight_halve",
        )(bits[level], keep, got)
        pieces //= 2
    got = lax.ppermute(give, "dom", flips[len(halves) - 1])
    total = add_round(add_round_kernel, keep, got)

    out_h = pl.pallas_call(
        turn_kernel,
        out_shape=sds((nodes, f_out), BF),
        in_specs=[vmem()],
        out_specs=vmem(),
        compiler_params=params(BIG),
        cost_estimate=cost(0, MIB),
        name="turn_out",
    )(out_t)
    grad_all = lax.all_gather(grad_t, "chan", axis=0, tiled=False)

    for level in range(len(halves), len(order) - 1):
        got = lax.ppermute(total, "dom", flips[level])
        total = add_round(add_pair_kernel, total, got)
    scaled, total, out_h = lax.optimization_barrier((scaled, total, out_h))
    got = lax.ppermute(total, "dom", flips[-1])
    own_grad, far_grad = pl.pallas_call(
        scatter_kernel,
        out_shape=[
            pltpu.HBM((block_rows, chan_width, size), F32),
            pltpu.HBM((parts * slots, chan_width, size), BF),
        ],
        in_specs=[smem(), smem(), hbm(), vmem()],
        out_specs=[hbm(), hbm()],
        scratch_shapes=[
            pltpu.VMEM(block_vals.shape, BF),
            pltpu.VMEM((table, chan_width, size), F32),
            pltpu.VMEM((parts * slots, chan_width, size), BF),
            pltpu.SemaphoreType.DMA((streams,)),
            pltpu.SemaphoreType.DMA((copies,)),
            pltpu.SemaphoreType.DMA,
        ],
        compiler_params=params(24),
        cost_estimate=cost(block_flops, val_bytes + 4 * MIB),
        name="table_grad",
    )(cols, block_counts, vals, scaled)
    far_grad, got = lax.optimization_barrier((far_grad, got))
    total = add_round(add_pair_kernel, total, got)
    back = lax.all_to_all(
        far_grad.reshape(parts, slots, chan_width, size), "dom", split_axis=0, concat_axis=0, tiled=True
    )

    packed = pl.pallas_call(
        functools.partial(message_kernel, chans),
        out_shape=[sds((pieces * unit, lanes), BF)] * chans,
        in_specs=[smem(), vmem()],
        out_specs=[vmem()] * chans,
        compiler_params=params(BIG),
        cost_estimate=cost(0, MIB),
        name="pack_messages",
    )(me, total)
    packed = exchange(packed)
    held = pl.pallas_call(
        unit_kernel,
        out_shape=sds((pieces * unit, lanes), BF),
        in_specs=[vmem()] * chans,
        out_specs=vmem(),
        compiler_params=params(BIG),
        cost_estimate=cost(0, MIB),
        name="weight_sum",
    )(*packed).reshape(1, pieces * unit, lanes)
    near = pl.pallas_call(
        near_kernel,
        out_shape=sds((block_rows, chan_width, size), F32),
        in_specs=[smem()] + [vmem()] * 3,
        out_specs=vmem(),
        compiler_params=params(BIG),
        cost_estimate=cost(0, 3 * MIB),
        name="sum_near",
    )(me, w_self, grad_all, own_grad)
    held, near = lax.optimization_barrier((held, near))
    for level in reversed(range(len(halves))):
        held = jnp.concatenate([held, lax.ppermute(held, "dom", flips[level])], axis=0)
    address = jnp.int32(0)
    for level in range(len(halves)):
        address = address * 2 + bits[level][0]
    grad_w_self, grad_w_neigh = pl.pallas_call(
        functools.partial(spread_kernel, float(node_count * parts) ** (-0.5)),
        out_shape=[sds((chan_width, f_out), F32)] * 2,
        in_specs=[smem(), vmem()],
        out_specs=[vmem()] * 2,
        compiler_params=params(BIG),
        cost_estimate=cost(0, MIB),
        name="weight_spread",
    )(address.reshape(1), held)

    grad_feats = pl.pallas_call(
        final_kernel,
        out_shape=sds((chan_width, node_count), BF),
        in_specs=[smem()] + [vmem()] * 2,
        out_specs=vmem(),
        scratch_shapes=[pltpu.VMEM((block_rows, chan_width, size), F32)],
        compiler_params=params(BIG),
        cost_estimate=cost(0, 4 * MIB),
        name="sum_returned",
    )(send, near, back)
    return (out_h, grad_feats.T, grad_w_self, grad_w_neigh)


def solution(mesh):
    return jax.shard_map(
        per_device,
        mesh=mesh,
        in_specs=(
            P("dom", "chan"),
            P("dom", None, None, None),
            P("dom", None),
            P("dom"),
            P("dom", None, None),
            P(),
            P(),
            P(),
            P(("dom", "chan"), None),
        ),
        out_specs=(P(("dom", "chan"), None), P("dom", "chan"), P("chan", None), P("chan", None)),
        check_vma=False,
    )
```

```python
import functools

import jax
import jax.numpy as jnp
from jax import lax
from jax.experimental import pallas as pl
from jax.experimental.pallas import tpu as pltpu
from jax.sharding import PartitionSpec as P

BF = jnp.bfloat16
F32 = jnp.float32
MIB = 1 << 20
BIG = 8


def vmem():
    return pl.BlockSpec(memory_space=pltpu.VMEM)


def hbm():
    return pl.BlockSpec(memory_space=pltpu.HBM)


def smem():
    return pl.BlockSpec(memory_space=pltpu.SMEM)


def params(mib):
    return pltpu.CompilerParams(vmem_limit_bytes=mib * MIB)


def cost(flops, nbytes):
    return pl.CostEstimate(flops=flops, bytes_accessed=nbytes, transcendentals=0)


def nt_dot(left, right):
    return lax.dot_general(left, right, (((1,), (1,)), ((), ())), preferred_element_type=F32)


def nn_dot(left, right):
    return lax.dot_general(left, right, (((1,), (0,)), ((), ())), preferred_element_type=F32)


def pack_kernel(send_ref, feats_ref, out_ref, hold_ref, sems):
    dests, slots, _, size = hold_ref.shape
    copies = sems.shape[0]
    span = dests // copies
    for copy in range(copies):
        for dest in range(copy * span, (copy + 1) * span):
            for slot in range(slots):
                lane = pl.multiple_of(send_ref[slot, dest] * size, size)
                hold_ref[dest, slot] = feats_ref[:, pl.ds(lane, size)]
        place = pl.ds(copy * span, span)
        pltpu.make_async_copy(hold_ref.at[place], out_ref.at[place], sems.at[copy]).start()
    for copy in range(copies):
        place = pl.ds(copy * span, span)
        pltpu.make_async_copy(hold_ref.at[place], out_ref.at[place], sems.at[copy]).wait()


def split_kernel(me_ref, feats_ref, *out_refs):
    chans = len(out_refs)
    width = out_refs[0].shape[1]
    for shift, out_ref in enumerate(out_refs):
        lane = pl.multiple_of(lax.rem(me_ref[0] + shift, chans) * width, width)
        out_ref[...] = feats_ref[:, pl.ds(lane, width)]


def join_slots(vals_ref, row):
    return jnp.concatenate([vals_ref[row, k] for k in range(vals_ref.shape[1])], axis=1)


def stream_rows(vals_ref, held_ref, sems, body, before=None):
    copies = sems.shape[0]
    span = held_ref.shape[0] // copies

    def copy(place):
        rows = pl.ds(place * span, span)
        return pltpu.make_async_copy(vals_ref.at[rows], held_ref.at[rows], sems.at[place])

    for place in range(copies):
        copy(place).start()
    if before is not None:
        before()

    def one(place, carry):
        copy(place).wait()
        for row in range(span):
            body(place * span + row)
        return carry

    lax.fori_loop(0, copies, one, 0)


def gather_kernel(cols_ref, counts_ref, feats_ref, recv_ref, vals_ref, out_ref, degree_ref, held_ref, sems):
    _, depth, size, _ = vals_ref.shape
    width = feats_ref.shape[0]
    rows = out_ref.shape[2] // size
    own = feats_ref.shape[1] // size
    ones = jnp.ones((16, size), BF)

    def body(index):
        count = counts_ref[index]
        picked = []
        for k in range(depth):
            col = cols_ref[k, index]
            lane = pl.multiple_of(jnp.minimum(col, own - 1) * size, size)
            near = feats_ref[:, pl.ds(lane, size)]
            far = recv_ref[jnp.maximum(col - own, 0)]
            block = jnp.concatenate([jnp.where(col < own, near, far), ones], axis=0)
            picked.append(jnp.where(k < count, block, jnp.zeros_like(block)))
        total = nt_dot(join_slots(held_ref, index), jnp.concatenate(picked, axis=1)).T
        group = index // rows
        place = pl.ds(pl.multiple_of(lax.rem(index, rows) * size, size), size)
        degree_ref[group, :, place] = total[width : width + 8]
        out_ref[group, :, place] = (total[:width] / total[width : width + 1]).astype(BF)

    stream_rows(vals_ref, held_ref, sems, body)


def self_kernel(chans, me_ref, weight_ref, bias_ref, neigh_ref, cot_ref, *refs):
    chunk_refs = refs[:chans]
    full_ref, pre_ref, neigh_turned_ref, cot_turned_ref = refs[chans:]
    neigh_turned_ref[...] = neigh_ref[...].T
    cot_turned_ref[...] = cot_ref[...].T
    height = chunk_refs[0].shape[0]
    for shift, chunk_ref in enumerate(chunk_refs):
        start = pl.multiple_of(lax.rem(me_ref[0] + (chans - shift), chans) * height, height)
        full_ref[pl.ds(start, height), :] = chunk_ref[...]
    pre_ref[...] = nn_dot(weight_ref[...].T, full_ref[...]) + bias_ref[...]


def head_kernel(me_ref, degree_ref, pre_ref, turned_ref, weight_ref, cot_ref, mean_ref, out_ref, grad_ref, scaled_ref):
    preact = pre_ref[...] + nn_dot(turned_ref[...], mean_ref[...])
    logistic = jax.nn.sigmoid(preact)
    activated = preact * logistic
    slope = logistic * (1.0 + preact * (1.0 - logistic))
    inverse = 1.0 / jnp.sqrt(jnp.mean(activated * activated, axis=0, keepdims=True) + 1e-06)
    unit = activated * inverse
    cot = cot_ref[...].astype(F32)
    grad_act = (cot - unit * jnp.mean(cot * unit, axis=0, keepdims=True)) * inverse
    grad = (grad_act * slope).astype(BF)
    out_ref[...] = unit.astype(BF)
    grad_ref[...] = grad
    mean_grad = nn_dot(weight_ref[...], grad).astype(BF).astype(F32)
    degree = degree_ref[me_ref[0], 0:1, :]
    scaled_ref[...] = (mean_grad / degree).astype(BF)


def weight_partial_kernel(me_ref, feats_ref, mean_ref, grad_ref, keep_ref, give_ref, hold_ref):
    parts, chans, unit, lanes = hold_ref.shape
    grad = grad_ref[...]
    totals = [nt_dot(feats_ref[...], grad), nt_dot(mean_ref[...], grad)]
    width = totals[0].shape[0] // chans
    halves = totals[0].shape[1] // lanes
    count = width // unit
    for which, total in enumerate(totals):
        for half in range(halves):
            place = (which * halves + half) * count
            for chan in range(chans):
                piece = total[chan * width : (chan + 1) * width, half * lanes : (half + 1) * lanes]
                hold_ref[place : place + count, chan] = piece.reshape(count, unit, lanes)
    half = parts // 2
    bit = me_ref[0]
    keep_ref[...] = hold_ref[pl.ds(bit * half, half)]
    give_ref[...] = hold_ref[pl.ds((1 - bit) * half, half)].astype(BF)


def halve_kernel(me_ref, held_ref, recv_ref, keep_ref, give_ref, hold_ref):
    half = keep_ref.shape[0]
    bit = me_ref[0]
    hold_ref[...] = held_ref[...] + recv_ref[...].astype(F32)
    keep_ref[...] = hold_ref[pl.ds(bit * half, half)]
    give_ref[...] = hold_ref[pl.ds((1 - bit) * half, half)].astype(BF)


def add_round_kernel(held_ref, recv_ref, out_ref):
    out_ref[...] = (held_ref[...] + recv_ref[...].astype(F32)).astype(BF)


def add_pair_kernel(held_ref, recv_ref, out_ref):
    out_ref[...] = (held_ref[...].astype(F32) + recv_ref[...].astype(F32)).astype(BF)


def side_kernel(chans, me_ref, weight_ref, out_ref, grad_ref, turned_ref, *refs):
    self_refs = refs[:chans]
    (hold_ref,) = refs[chans:]
    turned_ref[...] = out_ref[...].T
    hold_ref[...] = nn_dot(weight_ref[...], grad_ref[...]).astype(BF)
    height = self_refs[0].shape[0]
    for shift, self_ref in enumerate(self_refs):
        start = pl.multiple_of(lax.rem(me_ref[0] + shift, chans) * height, height)
        self_ref[...] = hold_ref[pl.ds(start, height), :]


def message_kernel(chans, me_ref, unit_ref, *refs):
    self_refs = refs[:chans]
    packed_refs = refs[chans:]
    nodes = self_refs[0].shape[1]
    units, _, unit, lanes = unit_ref.shape
    for shift, packed_ref in enumerate(packed_refs):
        dest = lax.rem(me_ref[0] + shift, chans)
        piece = unit_ref[:, dest].astype(F32).reshape(units * unit, lanes)
        packed_ref[:, :nodes] = self_refs[shift][...]
        packed_ref[: units * unit, nodes:] = piece.astype(BF)
        packed_ref[units * unit :, nodes:] = jnp.zeros_like(packed_ref[units * unit :, nodes:])


def scatter_kernel(
    cols_ref, counts_ref, vals_ref, scaled_ref, own_ref, far_ref, held_ref, hold_ref, send_ref, val_sems, sems, own_sem
):
    _, depth, size, _ = vals_ref.shape
    rows = scaled_ref.shape[2] // size
    own = own_ref.shape[0]

    def clear():
        hold_ref[...] = jnp.zeros_like(hold_ref)

    def body(index):
        count = counts_ref[index]
        place = pl.ds(pl.multiple_of(lax.rem(index, rows) * size, size), size)
        total = nn_dot(scaled_ref[index // rows, :, place], join_slots(held_ref, index))
        for k in range(depth):
            part = total[:, k * size : (k + 1) * size]
            hold_ref[cols_ref[k, index]] += jnp.where(k < count, part, jnp.zeros_like(part))

    stream_rows(vals_ref, held_ref, val_sems, body, clear)
    copies = sems.shape[0]
    span = far_ref.shape[0] // copies
    for copy in range(copies):
        send_ref[copy * span : (copy + 1) * span] = hold_ref[own + copy * span : own + (copy + 1) * span].astype(BF)
        place = pl.ds(copy * span, span)
        pltpu.make_async_copy(send_ref.at[place], far_ref.at[place], sems.at[copy]).start()
    pltpu.make_async_copy(hold_ref.at[pl.ds(0, own)], own_ref, own_sem).start()
    for copy in range(copies):
        place = pl.ds(copy * span, span)
        pltpu.make_async_copy(send_ref.at[place], far_ref.at[place], sems.at[copy]).wait()
    pltpu.make_async_copy(hold_ref.at[pl.ds(0, own)], own_ref, own_sem).wait()


def unit_kernel(*refs):
    packed_refs = refs[:-1]
    out_ref = refs[-1]
    rows, lanes = out_ref.shape
    total = packed_refs[0][:rows, -lanes:].astype(F32)
    for packed_ref in packed_refs[1:]:
        total = total + packed_ref[:rows, -lanes:].astype(F32)
    out_ref[...] = total.astype(BF)


def spread_kernel(scale, me_ref, held_ref, self_ref, neigh_ref):
    pieces, rows, lanes = held_ref.shape
    half = pieces // 2
    unit_rows = self_ref.shape[0]
    per = unit_rows // rows
    for place in range(pieces):
        value = held_ref[lax.bitwise_xor(me_ref[0], place)].astype(F32) * scale
        target = self_ref if place < half else neigh_ref
        inside = place % half
        column, row = inside // per, inside % per
        target[row * rows : (row + 1) * rows, column * lanes : (column + 1) * lanes] = value


def near_kernel(chans, me_ref, own_ref, *refs):
    packed_refs = refs[:chans]
    (out_ref,) = refs[chans:]
    blocks, _, size = out_ref.shape
    rows = blocks // chans
    for shift, packed_ref in enumerate(packed_refs):
        group = lax.rem(me_ref[0] + (chans - shift), chans)
        for row in range(rows):
            index = group * rows + row
            out_ref[index] = own_ref[index] + packed_ref[:, row * size : (row + 1) * size].astype(F32)


def final_kernel(send_ref, near_ref, back_ref, out_ref, hold_ref):
    slots, dests = send_ref.shape
    blocks, _, size = hold_ref.shape
    hold_ref[...] = near_ref[...]

    def one(dest, carry):
        for slot in range(slots):
            hold_ref[send_ref[slot, dest]] += back_ref[dest, slot].astype(F32)
        return carry

    lax.fori_loop(0, dests, one, 0, unroll=8)
    for block in range(blocks):
        out_ref[:, block * size : (block + 1) * size] = hold_ref[block].astype(BF)


def exchange(chunks):
    count = len(chunks)
    return [chunks[0]] + [
        lax.ppermute(chunks[shift], "chan", [(i, (i + shift) % count) for i in range(count)])
        for shift in range(1, count)
    ]


def sds(shape, dtype):
    return jax.ShapeDtypeStruct(shape, dtype)


def halving_order(parts):
    count = parts.bit_length() - 1
    return [bit for bit in (0, 1, 3, 2, 4) if bit < count] + list(range(5, count))


def add_round(kernel, left, right):
    return pl.pallas_call(
        kernel,
        out_shape=sds(left.shape, BF),
        in_specs=[vmem()] * 2,
        out_specs=vmem(),
        compiler_params=params(BIG),
        cost_estimate=cost(0, MIB),
        name="weight_add",
    )(left, right)


def per_device(feats, block_vals, block_cols, block_counts, send_list, w_self, w_neigh, bias, cotangent):
    node_count, chan_width = feats.shape
    block_rows, depth, size, _ = block_vals.shape
    parts = lax.axis_size("dom")
    chans = lax.axis_size("chan")
    slots = send_list.shape[2]
    f_in, f_out = w_self.shape
    nodes = node_count // chans
    rows = block_rows // chans
    table = block_rows + parts * slots
    chan = lax.axis_index("chan").astype(jnp.int32)
    part = lax.axis_index("dom").astype(jnp.int32)
    me = chan.reshape(1)
    send = send_list[0].T
    cols = block_cols.T
    feats_t = feats.T
    val_bytes = block_vals.size * 2
    vals = pltpu.with_memory_space_constraint(block_vals, pltpu.HBM)
    block_flops = 2 * block_rows * depth * size * size * chan_width
    layer_flops = 2 * f_in * f_out * nodes
    unit, lanes = 8, 128
    copies, streams = 8, 4

    outgoing = pl.pallas_call(
        pack_kernel,
        out_shape=pltpu.HBM((parts, slots, chan_width, size), BF),
        in_specs=[smem(), vmem()],
        out_specs=hbm(),
        scratch_shapes=[pltpu.VMEM((parts, slots, chan_width, size), BF), pltpu.SemaphoreType.DMA((copies,))],
        compiler_params=params(8),
        cost_estimate=cost(0, 5 * MIB),
        name="pack_outgoing",
    )(
        pltpu.with_memory_space_constraint(send, pltpu.HBM),
        pltpu.with_memory_space_constraint(feats_t, pltpu.HBM),
    )
    incoming = lax.all_to_all(outgoing, "dom", split_axis=0, concat_axis=0, tiled=True)

    feat_chunks = pl.pallas_call(
        split_kernel,
        out_shape=[sds((chan_width, nodes), BF)] * chans,
        in_specs=[smem(), vmem()],
        out_specs=[vmem()] * chans,
        compiler_params=params(BIG),
        cost_estimate=cost(0, MIB),
        name="split_feats",
    )(me, feats_t)
    feat_chunks = exchange(feat_chunks)
    feats_own, pre_self, neigh_turned, cot_turned = pl.pallas_call(
        functools.partial(self_kernel, chans),
        out_shape=[sds((f_in, nodes), BF), sds((f_out, nodes), F32), sds((f_out, f_in), BF), sds((f_out, nodes), BF)],
        in_specs=[smem()] + [vmem()] * (4 + chans),
        out_specs=[vmem()] * 4,
        compiler_params=params(BIG),
        cost_estimate=cost(layer_flops, 2 * MIB),
        name="self_part",
    )(me, w_self, bias.reshape(f_out, 1), w_neigh, cotangent, *feat_chunks)

    incoming, pre_self, feats_own, neigh_turned, cot_turned = lax.optimization_barrier(
        (incoming, pre_self, feats_own, neigh_turned, cot_turned)
    )
    mean, degree = pl.pallas_call(
        gather_kernel,
        out_shape=[sds((chans, chan_width, nodes), BF), sds((chans, 8, nodes), F32)],
        in_specs=[smem(), smem()] + [vmem()] * 2 + [hbm()],
        out_specs=[vmem()] * 2,
        scratch_shapes=[pltpu.VMEM(block_vals.shape, BF), pltpu.SemaphoreType.DMA((streams,))],
        compiler_params=params(16),
        cost_estimate=cost(block_flops, val_bytes + 3 * MIB),
        name="neighbour_mean",
    )(cols, block_counts, feats_t, incoming.reshape(parts * slots, chan_width, size), vals)
    mean = lax.all_to_all(mean, "chan", split_axis=0, concat_axis=0, tiled=True).reshape(f_in, nodes)

    out_t, grad_t, scaled = pl.pallas_call(
        head_kernel,
        out_shape=[sds((f_out, nodes), BF), sds((f_out, nodes), BF), sds((f_in, nodes), BF)],
        in_specs=[smem()] + [vmem()] * 6,
        out_specs=[vmem()] * 3,
        compiler_params=params(BIG),
        cost_estimate=cost(2 * layer_flops, 4 * MIB),
        name="layer_head",
    )(me, degree, pre_self, neigh_turned, w_neigh, cot_turned, mean)
    scaled = lax.all_to_all(
        scaled.reshape(chans, chan_width, nodes), "chan", split_axis=0, concat_axis=0, tiled=True
    )

    order = halving_order(parts)
    halves, wholes = order[:3], order[3:]
    flips = [[(i, i ^ (1 << bit)) for i in range(parts)] for bit in order]
    bits = [((part >> bit) & 1).reshape(1) for bit in order]
    pieces = parts
    keep, give = pl.pallas_call(
        weight_partial_kernel,
        out_shape=[sds((pieces // 2, chans, unit, lanes), F32), sds((pieces // 2, chans, unit, lanes), BF)],
        in_specs=[smem()] + [vmem()] * 3,
        out_specs=[vmem()] * 2,
        scratch_shapes=[pltpu.VMEM((pieces, chans, unit, lanes), F32)],
        compiler_params=params(BIG),
        cost_estimate=cost(2 * layer_flops, 3 * MIB),
        name="weight_partial",
    )(bits[0], feats_own, mean, grad_t)
    pieces //= 2
    for level in range(1, len(halves)):
        got = lax.ppermute(give, "dom", flips[level - 1])
        keep, give = pl.pallas_call(
            halve_kernel,
            out_shape=[sds((pieces // 2, chans, unit, lanes), F32), sds((pieces // 2, chans, unit, lanes), BF)],
            in_specs=[smem()] + [vmem()] * 2,
            out_specs=[vmem()] * 2,
            scratch_shapes=[pltpu.VMEM((pieces, chans, unit, lanes), F32)],
            compiler_params=params(BIG),
            cost_estimate=cost(0, MIB),
            name="weight_halve",
        )(bits[level], keep, got)
        pieces //= 2
    got = lax.ppermute(give, "dom", flips[len(halves) - 1])
    total = add_round(add_round_kernel, keep, got)

    side = pl.pallas_call(
        functools.partial(side_kernel, chans),
        out_shape=[sds((nodes, f_out), BF)] + [sds((chan_width, nodes), BF)] * chans,
        in_specs=[smem()] + [vmem()] * 3,
        out_specs=[vmem()] * (1 + chans),
        scratch_shapes=[pltpu.VMEM((f_in, nodes), BF)],
        compiler_params=params(BIG),
        cost_estimate=cost(layer_flops, 3 * MIB),
        name="side_grads",
    )(me, w_self, out_t, grad_t)
    for level in range(len(halves), len(order) - 1):
        got = lax.ppermute(total, "dom", flips[level])
        total = add_round(add_pair_kernel, total, got)
    scaled, total, side = lax.optimization_barrier((scaled, total, side))
    out_h = side[0]
    got = lax.ppermute(total, "dom", flips[-1])
    own_grad, far_grad = pl.pallas_call(
        scatter_kernel,
        out_shape=[
            pltpu.HBM((block_rows, chan_width, size), F32),
            pltpu.HBM((parts * slots, chan_width, size), BF),
        ],
        in_specs=[smem(), smem(), hbm(), vmem()],
        out_specs=[hbm(), hbm()],
        scratch_shapes=[
            pltpu.VMEM(block_vals.shape, BF),
            pltpu.VMEM((table, chan_width, size), F32),
            pltpu.VMEM((parts * slots, chan_width, size), BF),
            pltpu.SemaphoreType.DMA((streams,)),
            pltpu.SemaphoreType.DMA((copies,)),
            pltpu.SemaphoreType.DMA,
        ],
        compiler_params=params(24),
        cost_estimate=cost(block_flops, val_bytes + 4 * MIB),
        name="table_grad",
    )(cols, block_counts, vals, scaled)
    far_grad, got = lax.optimization_barrier((far_grad, got))
    total = add_round(add_pair_kernel, total, got)
    back = lax.all_to_all(
        far_grad.reshape(parts, slots, chan_width, size), "dom", split_axis=0, concat_axis=0, tiled=True
    )

    packed = pl.pallas_call(
        functools.partial(message_kernel, chans),
        out_shape=[sds((chan_width, nodes + lanes), BF)] * chans,
        in_specs=[smem()] + [vmem()] * (1 + chans),
        out_specs=[vmem()] * chans,
        compiler_params=params(BIG),
        cost_estimate=cost(0, MIB),
        name="pack_messages",
    )(me, total, *side[1:])
    packed = exchange(packed)
    held = pl.pallas_call(
        unit_kernel,
        out_shape=sds((pieces * unit, lanes), BF),
        in_specs=[vmem()] * chans,
        out_specs=vmem(),
        compiler_params=params(BIG),
        cost_estimate=cost(0, MIB),
        name="weight_sum",
    )(*packed).reshape(1, pieces * unit, lanes)
    near = pl.pallas_call(
        functools.partial(near_kernel, chans),
        out_shape=sds((block_rows, chan_width, size), F32),
        in_specs=[smem()] + [vmem()] * (1 + chans),
        out_specs=vmem(),
        compiler_params=params(BIG),
        cost_estimate=cost(0, 3 * MIB),
        name="sum_near",
    )(me, own_grad, *packed)
    held, near = lax.optimization_barrier((held, near))
    for level in reversed(range(len(halves))):
        held = jnp.concatenate([held, lax.ppermute(held, "dom", flips[level])], axis=0)
        if level == len(halves) - 1:
            held, back = lax.optimization_barrier((held, back))
    address = jnp.int32(0)
    for level in range(len(halves)):
        address = address * 2 + bits[level][0]
    grad_w_self, grad_w_neigh = pl.pallas_call(
        functools.partial(spread_kernel, float(node_count * parts) ** (-0.5)),
        out_shape=[sds((chan_width, f_out), F32)] * 2,
        in_specs=[smem(), vmem()],
        out_specs=[vmem()] * 2,
        compiler_params=params(BIG),
        cost_estimate=cost(0, MIB),
        name="weight_spread",
    )(address.reshape(1), held)

    grad_feats = pl.pallas_call(
        final_kernel,
        out_shape=sds((chan_width, node_count), BF),
        in_specs=[smem()] + [vmem()] * 2,
        out_specs=vmem(),
        scratch_shapes=[pltpu.VMEM((block_rows, chan_width, size), F32)],
        compiler_params=params(BIG),
        cost_estimate=cost(0, 4 * MIB),
        name="sum_returned",
    )(send, near, back)
    return (out_h, grad_feats.T, grad_w_self, grad_w_neigh)


def solution(mesh):
    return jax.shard_map(
        per_device,
        mesh=mesh,
        in_specs=(
            P("dom", "chan"),
            P("dom", None, None, None),
            P("dom", None),
            P("dom"),
            P("dom", None, None),
            P(),
            P(),
            P(),
            P(("dom", "chan"), None),
        ),
        out_specs=(P(("dom", "chan"), None), P("dom", "chan"), P("chan", None), P("chan", None)),
        check_vma=False,
    )
```

```python
import functools

import jax
import jax.numpy as jnp
from jax import lax
from jax.experimental import pallas as pl
from jax.experimental.pallas import tpu as pltpu
from jax.sharding import PartitionSpec as P

BF = jnp.bfloat16
F32 = jnp.float32
MIB = 1 << 20
BIG = 8


def vmem():
    return pl.BlockSpec(memory_space=pltpu.VMEM)


def hbm():
    return pl.BlockSpec(memory_space=pltpu.HBM)


def smem():
    return pl.BlockSpec(memory_space=pltpu.SMEM)


def params(mib):
    return pltpu.CompilerParams(vmem_limit_bytes=mib * MIB)


def cost(flops, nbytes):
    return pl.CostEstimate(flops=flops, bytes_accessed=nbytes, transcendentals=0)


def nt_dot(left, right):
    return lax.dot_general(left, right, (((1,), (1,)), ((), ())), preferred_element_type=F32)


def nn_dot(left, right):
    return lax.dot_general(left, right, (((1,), (0,)), ((), ())), preferred_element_type=F32)


def pack_kernel(send_ref, feats_ref, out_ref, hold_ref, sems):
    dests, slots, _, size = hold_ref.shape
    copies = sems.shape[0]
    span = dests // copies
    for copy in range(copies):
        for dest in range(copy * span, (copy + 1) * span):
            for slot in range(slots):
                lane = pl.multiple_of(send_ref[slot, dest] * size, size)
                hold_ref[dest, slot] = feats_ref[:, pl.ds(lane, size)]
        place = pl.ds(copy * span, span)
        pltpu.make_async_copy(hold_ref.at[place], out_ref.at[place], sems.at[copy]).start()
    for copy in range(copies):
        place = pl.ds(copy * span, span)
        pltpu.make_async_copy(hold_ref.at[place], out_ref.at[place], sems.at[copy]).wait()


def split_kernel(me_ref, feats_ref, *refs):
    out_refs, sems = refs[:-1], refs[-1]
    chans = len(out_refs)
    width = out_refs[0].shape[1]

    def copy(shift):
        lane = pl.multiple_of(lax.rem(me_ref[0] + shift, chans) * width, width)
        return pltpu.make_async_copy(feats_ref.at[:, pl.ds(lane, width)], out_refs[shift], sems.at[shift])

    for shift in range(chans):
        copy(shift).start()
    for shift in range(chans):
        copy(shift).wait()


def join_slots(vals_ref, row):
    return jnp.concatenate([vals_ref[row, k] for k in range(vals_ref.shape[1])], axis=1)


def stream_rows(vals_ref, held_ref, sems, body, before=None, after=None):
    copies = sems.shape[0]
    span = held_ref.shape[0] // copies

    def copy(place):
        rows = pl.ds(place * span, span)
        return pltpu.make_async_copy(vals_ref.at[rows], held_ref.at[rows], sems.at[place])

    for place in range(copies):
        copy(place).start()
    if before is not None:
        before()

    def one(place, carry):
        copy(place).wait()
        for row in range(span):
            body(place * span + row)
        if after is not None:
            after(place)
        return carry

    lax.fori_loop(0, copies, one, 0)


def gather_kernel(
    cols_ref, counts_ref, feats_ref, recv_ref, vals_ref, out_ref, degree_ref, held_ref, mean_ref, sems, out_sems
):
    _, depth, size, _ = vals_ref.shape
    width = feats_ref.shape[0]
    rows = out_ref.shape[2] // size
    own = feats_ref.shape[1] // size
    ones = jnp.ones((16, size), BF)

    def body(index):
        count = counts_ref[index]
        picked = []
        for k in range(depth):
            col = cols_ref[k, index]
            lane = pl.multiple_of(jnp.minimum(col, own - 1) * size, size)
            near = feats_ref[:, pl.ds(lane, size)]
            far = recv_ref[jnp.maximum(col - own, 0)]
            block = jnp.concatenate([jnp.where(col < own, near, far), ones], axis=0)
            picked.append(jnp.where(k < count, block, jnp.zeros_like(block)))
        total = nt_dot(join_slots(held_ref, index), jnp.concatenate(picked, axis=1)).T
        group = index // rows
        place = pl.ds(pl.multiple_of(lax.rem(index, rows) * size, size), size)
        degree_ref[group, :, place] = total[width : width + 8]
        mean_ref[group, :, place] = (total[:width] / total[width : width + 1]).astype(BF)

    copies = out_sems.shape[0]
    span = mean_ref.shape[0] // copies

    def copy(place):
        groups = pl.ds(place * span, span)
        return pltpu.make_async_copy(mean_ref.at[groups], out_ref.at[groups], out_sems.at[place])

    stream_rows(vals_ref, held_ref, sems, body, after=lambda place: copy(place).start())
    for place in range(copies):
        copy(place).wait()


def self_kernel(chans, me_ref, weight_ref, bias_ref, neigh_ref, cot_ref, *refs):
    chunk_refs = refs[:chans]
    full_ref, pre_ref, neigh_turned_ref, cot_turned_ref = refs[chans:]
    neigh_turned_ref[...] = neigh_ref[...].T
    cot_turned_ref[...] = cot_ref[...].T
    height = chunk_refs[0].shape[0]
    for shift, chunk_ref in enumerate(chunk_refs):
        start = pl.multiple_of(lax.rem(me_ref[0] + (chans - shift), chans) * height, height)
        full_ref[pl.ds(start, height), :] = chunk_ref[...]
    pre_ref[...] = nn_dot(weight_ref[...].T, full_ref[...]) + bias_ref[...]


def head_kernel(me_ref, degree_ref, pre_ref, turned_ref, weight_ref, cot_ref, mean_ref, out_ref, grad_ref, scaled_ref):
    preact = pre_ref[...] + nn_dot(turned_ref[...], mean_ref[...])
    logistic = jax.nn.sigmoid(preact)
    activated = preact * logistic
    slope = logistic * (1.0 + preact * (1.0 - logistic))
    inverse = 1.0 / jnp.sqrt(jnp.mean(activated * activated, axis=0, keepdims=True) + 1e-06)
    unit = activated * inverse
    cot = cot_ref[...].astype(F32)
    grad_act = (cot - unit * jnp.mean(cot * unit, axis=0, keepdims=True)) * inverse
    grad = (grad_act * slope).astype(BF)
    out_ref[...] = unit.astype(BF)
    grad_ref[...] = grad
    mean_grad = nn_dot(weight_ref[...], grad).astype(BF).astype(F32)
    degree = degree_ref[me_ref[0], 0:1, :]
    scaled_ref[...] = (mean_grad / degree).astype(BF)


def weight_partial_kernel(me_ref, feats_ref, mean_ref, grad_ref, keep_ref, give_ref, hold_ref):
    parts, chans, unit, lanes = hold_ref.shape
    grad = grad_ref[...]
    totals = [nt_dot(feats_ref[...], grad), nt_dot(mean_ref[...], grad)]
    width = totals[0].shape[0] // chans
    halves = totals[0].shape[1] // lanes
    count = width // unit
    for which, total in enumerate(totals):
        for half in range(halves):
            place = (which * halves + half) * count
            for chan in range(chans):
                piece = total[chan * width : (chan + 1) * width, half * lanes : (half + 1) * lanes]
                hold_ref[place : place + count, chan] = piece.reshape(count, unit, lanes)
    half = parts // 2
    bit = me_ref[0]
    keep_ref[...] = hold_ref[pl.ds(bit * half, half)]
    give_ref[...] = hold_ref[pl.ds((1 - bit) * half, half)].astype(BF)


def halve_kernel(me_ref, held_ref, recv_ref, keep_ref, give_ref, hold_ref):
    half = keep_ref.shape[0]
    bit = me_ref[0]
    hold_ref[...] = held_ref[...] + recv_ref[...].astype(F32)
    keep_ref[...] = hold_ref[pl.ds(bit * half, half)]
    give_ref[...] = hold_ref[pl.ds((1 - bit) * half, half)].astype(BF)


def add_round_kernel(held_ref, recv_ref, out_ref):
    out_ref[...] = (held_ref[...] + recv_ref[...].astype(F32)).astype(BF)


def add_pair_kernel(held_ref, recv_ref, out_ref):
    out_ref[...] = (held_ref[...].astype(F32) + recv_ref[...].astype(F32)).astype(BF)


def side_kernel(chans, me_ref, weight_ref, out_ref, grad_ref, turned_ref, *refs):
    self_refs = refs[:chans]
    (hold_ref,) = refs[chans:]
    turned_ref[...] = out_ref[...].T
    hold_ref[...] = nn_dot(weight_ref[...], grad_ref[...]).astype(BF)
    height = self_refs[0].shape[0]
    for shift, self_ref in enumerate(self_refs):
        start = pl.multiple_of(lax.rem(me_ref[0] + shift, chans) * height, height)
        self_ref[...] = hold_ref[pl.ds(start, height), :]


def message_kernel(chans, me_ref, unit_ref, *refs):
    self_refs = refs[:chans]
    packed_refs = refs[chans:]
    nodes = self_refs[0].shape[1]
    units, _, unit, lanes = unit_ref.shape
    for shift, packed_ref in enumerate(packed_refs):
        dest = lax.rem(me_ref[0] + shift, chans)
        piece = unit_ref[:, dest].astype(F32).reshape(units * unit, lanes)
        packed_ref[:, :nodes] = self_refs[shift][...]
        packed_ref[: units * unit, nodes:] = piece.astype(BF)
        packed_ref[units * unit :, nodes:] = jnp.zeros_like(packed_ref[units * unit :, nodes:])


def scatter_kernel(
    cols_ref, counts_ref, vals_ref, scaled_ref, own_ref, far_ref, held_ref, hold_ref, send_ref, val_sems, sems, own_sem
):
    _, depth, size, _ = vals_ref.shape
    rows = scaled_ref.shape[2] // size
    own = own_ref.shape[0]

    def clear():
        hold_ref[...] = jnp.zeros_like(hold_ref)

    def body(index):
        count = counts_ref[index]
        place = pl.ds(pl.multiple_of(lax.rem(index, rows) * size, size), size)
        total = nn_dot(scaled_ref[index // rows, :, place], join_slots(held_ref, index))
        for k in range(depth):
            part = total[:, k * size : (k + 1) * size]
            hold_ref[cols_ref[k, index]] += jnp.where(k < count, part, jnp.zeros_like(part))

    stream_rows(vals_ref, held_ref, val_sems, body, clear)
    copies = sems.shape[0]
    span = far_ref.shape[0] // copies
    for copy in range(copies):
        send_ref[copy * span : (copy + 1) * span] = hold_ref[own + copy * span : own + (copy + 1) * span].astype(BF)
        place = pl.ds(copy * span, span)
        pltpu.make_async_copy(send_ref.at[place], far_ref.at[place], sems.at[copy]).start()
    pltpu.make_async_copy(hold_ref.at[pl.ds(0, own)], own_ref, own_sem).start()
    for copy in range(copies):
        place = pl.ds(copy * span, span)
        pltpu.make_async_copy(send_ref.at[place], far_ref.at[place], sems.at[copy]).wait()
    pltpu.make_async_copy(hold_ref.at[pl.ds(0, own)], own_ref, own_sem).wait()


def unit_kernel(*refs):
    packed_refs = refs[:-1]
    out_ref = refs[-1]
    rows, lanes = out_ref.shape
    total = packed_refs[0][:rows, -lanes:].astype(F32)
    for packed_ref in packed_refs[1:]:
        total = total + packed_ref[:rows, -lanes:].astype(F32)
    out_ref[...] = total.astype(BF)


def spread_kernel(scale, me_ref, held_ref, self_ref, neigh_ref):
    pieces, rows, lanes = held_ref.shape
    half = pieces // 2
    unit_rows = self_ref.shape[0]
    per = unit_rows // rows
    for place in range(pieces):
        value = held_ref[lax.bitwise_xor(me_ref[0], place)].astype(F32) * scale
        target = self_ref if place < half else neigh_ref
        inside = place % half
        column, row = inside // per, inside % per
        target[row * rows : (row + 1) * rows, column * lanes : (column + 1) * lanes] = value


def near_kernel(chans, me_ref, own_ref, *refs):
    packed_refs = refs[:chans]
    (out_ref,) = refs[chans:]
    blocks, _, size = out_ref.shape
    rows = blocks // chans
    for shift, packed_ref in enumerate(packed_refs):
        group = lax.rem(me_ref[0] + (chans - shift), chans)
        for row in range(rows):
            index = group * rows + row
            out_ref[index] = own_ref[index] + packed_ref[:, row * size : (row + 1) * size].astype(F32)


def final_kernel(send_ref, near_ref, back_ref, out_ref, hold_ref):
    slots, dests = send_ref.shape
    blocks, _, size = hold_ref.shape
    hold_ref[...] = near_ref[...]

    def one(dest, carry):
        for slot in range(slots):
            hold_ref[send_ref[slot, dest]] += back_ref[dest, slot].astype(F32)
        return carry

    lax.fori_loop(0, dests, one, 0, unroll=8)
    for block in range(blocks):
        out_ref[:, block * size : (block + 1) * size] = hold_ref[block].astype(BF)


def exchange(chunks):
    count = len(chunks)
    return [chunks[0]] + [
        lax.ppermute(chunks[shift], "chan", [(i, (i + shift) % count) for i in range(count)])
        for shift in range(1, count)
    ]


def sds(shape, dtype):
    return jax.ShapeDtypeStruct(shape, dtype)


def halving_order(parts):
    count = parts.bit_length() - 1
    return [bit for bit in (0, 1, 3, 2, 4) if bit < count] + list(range(5, count))


def add_round(kernel, left, right):
    return pl.pallas_call(
        kernel,
        out_shape=sds(left.shape, BF),
        in_specs=[vmem()] * 2,
        out_specs=vmem(),
        compiler_params=params(BIG),
        cost_estimate=cost(0, MIB),
        name="weight_add",
    )(left, right)


def per_device(feats, block_vals, block_cols, block_counts, send_list, w_self, w_neigh, bias, cotangent):
    node_count, chan_width = feats.shape
    block_rows, depth, size, _ = block_vals.shape
    parts = lax.axis_size("dom")
    chans = lax.axis_size("chan")
    slots = send_list.shape[2]
    f_in, f_out = w_self.shape
    nodes = node_count // chans
    rows = block_rows // chans
    table = block_rows + parts * slots
    chan = lax.axis_index("chan").astype(jnp.int32)
    part = lax.axis_index("dom").astype(jnp.int32)
    me = chan.reshape(1)
    send = send_list[0].T
    cols = block_cols.T
    feats_t = feats.T
    val_bytes = block_vals.size * 2
    vals = pltpu.with_memory_space_constraint(block_vals, pltpu.HBM)
    block_flops = 2 * block_rows * depth * size * size * chan_width
    layer_flops = 2 * f_in * f_out * nodes
    unit, lanes = 8, 128
    copies, streams = 8, 4

    outgoing = pl.pallas_call(
        pack_kernel,
        out_shape=pltpu.HBM((parts, slots, chan_width, size), BF),
        in_specs=[smem(), vmem()],
        out_specs=hbm(),
        scratch_shapes=[pltpu.VMEM((parts, slots, chan_width, size), BF), pltpu.SemaphoreType.DMA((copies,))],
        compiler_params=params(8),
        cost_estimate=cost(0, 5 * MIB),
        name="pack_outgoing",
    )(
        pltpu.with_memory_space_constraint(send, pltpu.HBM),
        pltpu.with_memory_space_constraint(feats_t, pltpu.HBM),
    )
    incoming = lax.all_to_all(outgoing, "dom", split_axis=0, concat_axis=0, tiled=True)

    feat_chunks = pl.pallas_call(
        split_kernel,
        out_shape=[pltpu.HBM((chan_width, nodes), BF)] * chans,
        in_specs=[smem(), vmem()],
        out_specs=[hbm()] * chans,
        scratch_shapes=[pltpu.SemaphoreType.DMA((chans,))],
        compiler_params=params(BIG),
        cost_estimate=cost(0, MIB),
        name="split_feats",
    )(me, feats_t)
    incoming, feat_chunks = lax.optimization_barrier((incoming, exchange(feat_chunks)))
    feat_chunks = [pltpu.with_memory_space_constraint(chunk, pltpu.HBM) for chunk in feat_chunks]
    feats_own, pre_self, neigh_turned, cot_turned = pl.pallas_call(
        functools.partial(self_kernel, chans),
        out_shape=[sds((f_in, nodes), BF), sds((f_out, nodes), F32), sds((f_out, f_in), BF), sds((f_out, nodes), BF)],
        in_specs=[smem()] + [vmem()] * (4 + chans),
        out_specs=[vmem()] * 4,
        compiler_params=params(BIG),
        cost_estimate=cost(layer_flops, 2 * MIB),
        name="self_part",
    )(me, w_self, bias.reshape(f_out, 1), w_neigh, cotangent, *feat_chunks)

    mean, degree = pl.pallas_call(
        gather_kernel,
        out_shape=[pltpu.HBM((chans, chan_width, nodes), BF), sds((chans, 8, nodes), F32)],
        in_specs=[smem(), smem()] + [vmem()] * 2 + [hbm()],
        out_specs=[hbm(), vmem()],
        scratch_shapes=[
            pltpu.VMEM(block_vals.shape, BF),
            pltpu.VMEM((chans, chan_width, nodes), BF),
            pltpu.SemaphoreType.DMA((streams,)),
            pltpu.SemaphoreType.DMA((streams,)),
        ],
        compiler_params=params(16),
        cost_estimate=cost(block_flops, val_bytes + 3 * MIB),
        name="neighbour_mean",
    )(cols, block_counts, feats_t, incoming.reshape(parts * slots, chan_width, size), vals)
    mean = lax.all_to_all(mean, "chan", split_axis=0, concat_axis=0, tiled=True).reshape(f_in, nodes)

    out_t, grad_t, scaled = pl.pallas_call(
        head_kernel,
        out_shape=[sds((f_out, nodes), BF), sds((f_out, nodes), BF), sds((f_in, nodes), BF)],
        in_specs=[smem()] + [vmem()] * 6,
        out_specs=[vmem()] * 3,
        compiler_params=params(BIG),
        cost_estimate=cost(2 * layer_flops, 4 * MIB),
        name="layer_head",
    )(me, degree, pre_self, neigh_turned, w_neigh, cot_turned, mean)
    scaled = lax.all_to_all(
        scaled.reshape(chans, chan_width, nodes), "chan", split_axis=0, concat_axis=0, tiled=True
    )

    order = halving_order(parts)
    halves, wholes = order[:3], order[3:]
    flips = [[(i, i ^ (1 << bit)) for i in range(parts)] for bit in order]
    bits = [((part >> bit) & 1).reshape(1) for bit in order]
    pieces = parts
    keep, give = pl.pallas_call(
        weight_partial_kernel,
        out_shape=[sds((pieces // 2, chans, unit, lanes), F32), sds((pieces // 2, chans, unit, lanes), BF)],
        in_specs=[smem()] + [vmem()] * 3,
        out_specs=[vmem()] * 2,
        scratch_shapes=[pltpu.VMEM((pieces, chans, unit, lanes), F32)],
        compiler_params=params(BIG),
        cost_estimate=cost(2 * layer_flops, 3 * MIB),
        name="weight_partial",
    )(bits[0], feats_own, mean, grad_t)
    pieces //= 2
    for level in range(1, len(halves)):
        got = lax.ppermute(give, "dom", flips[level - 1])
        keep, give = pl.pallas_call(
            halve_kernel,
            out_shape=[sds((pieces // 2, chans, unit, lanes), F32), sds((pieces // 2, chans, unit, lanes), BF)],
            in_specs=[smem()] + [vmem()] * 2,
            out_specs=[vmem()] * 2,
            scratch_shapes=[pltpu.VMEM((pieces, chans, unit, lanes), F32)],
            compiler_params=params(BIG),
            cost_estimate=cost(0, MIB),
            name="weight_halve",
        )(bits[level], keep, got)
        pieces //= 2
    got = lax.ppermute(give, "dom", flips[len(halves) - 1])
    total = add_round(add_round_kernel, keep, got)

    side = pl.pallas_call(
        functools.partial(side_kernel, chans),
        out_shape=[sds((nodes, f_out), BF)] + [sds((chan_width, nodes), BF)] * chans,
        in_specs=[smem()] + [vmem()] * 3,
        out_specs=[vmem()] * (1 + chans),
        scratch_shapes=[pltpu.VMEM((f_in, nodes), BF)],
        compiler_params=params(BIG),
        cost_estimate=cost(layer_flops, 3 * MIB),
        name="side_grads",
    )(me, w_self, out_t, grad_t)
    for level in range(len(halves), len(order) - 1):
        got = lax.ppermute(total, "dom", flips[level])
        total = add_round(add_pair_kernel, total, got)
    scaled, total, side = lax.optimization_barrier((scaled, total, side))
    out_h = side[0]
    own_grad, far_grad = pl.pallas_call(
        scatter_kernel,
        out_shape=[
            pltpu.HBM((block_rows, chan_width, size), F32),
            pltpu.HBM((parts * slots, chan_width, size), BF),
        ],
        in_specs=[smem(), smem(), hbm(), vmem()],
        out_specs=[hbm(), hbm()],
        scratch_shapes=[
            pltpu.VMEM(block_vals.shape, BF),
            pltpu.VMEM((table, chan_width, size), F32),
            pltpu.VMEM((parts * slots, chan_width, size), BF),
            pltpu.SemaphoreType.DMA((streams,)),
            pltpu.SemaphoreType.DMA((copies,)),
            pltpu.SemaphoreType.DMA,
        ],
        compiler_params=params(24),
        cost_estimate=cost(block_flops, val_bytes + 4 * MIB),
        name="table_grad",
    )(cols, block_counts, vals, scaled)
    total, far_grad = lax.optimization_barrier((total, far_grad))
    back = lax.all_to_all(
        far_grad.reshape(parts, slots, chan_width, size), "dom", split_axis=0, concat_axis=0, tiled=True
    )

    packed = pl.pallas_call(
        functools.partial(message_kernel, chans),
        out_shape=[sds((chan_width, nodes + lanes), BF)] * chans,
        in_specs=[smem()] + [vmem()] * (1 + chans),
        out_specs=[vmem()] * chans,
        compiler_params=params(BIG),
        cost_estimate=cost(0, MIB),
        name="pack_messages",
    )(me, total, *side[1:])
    packed = exchange(packed)
    held = pl.pallas_call(
        unit_kernel,
        out_shape=sds((pieces * unit, lanes), BF),
        in_specs=[vmem()] * chans,
        out_specs=vmem(),
        compiler_params=params(BIG),
        cost_estimate=cost(0, MIB),
        name="weight_sum",
    )(*packed).reshape(1, pieces * unit, lanes)
    near = pl.pallas_call(
        functools.partial(near_kernel, chans),
        out_shape=sds((block_rows, chan_width, size), F32),
        in_specs=[smem()] + [vmem()] * (1 + chans),
        out_specs=vmem(),
        compiler_params=params(BIG),
        cost_estimate=cost(0, 3 * MIB),
        name="sum_near",
    )(me, own_grad, *packed)
    held, near = lax.optimization_barrier((held, near))
    whole, half = 1 << order[-1], 1 << halves[-1]
    across, beside, both = (
        lax.ppermute(held, "dom", [(i, i ^ flip) for i in range(parts)]) for flip in (whole, half, whole | half)
    )
    mine = held.astype(F32) + across.astype(F32)
    other = beside.astype(F32) + both.astype(F32)
    held = jnp.concatenate([mine, other], axis=0).astype(BF)
    held, back = lax.optimization_barrier((held, back))
    for level in reversed(range(len(halves) - 1)):
        held = jnp.concatenate([held, lax.ppermute(held, "dom", flips[level])], axis=0)
    address = jnp.int32(0)
    for level in range(len(halves)):
        address = address * 2 + bits[level][0]
    grad_w_self, grad_w_neigh = pl.pallas_call(
        functools.partial(spread_kernel, float(node_count * parts) ** (-0.5)),
        out_shape=[sds((chan_width, f_out), F32)] * 2,
        in_specs=[smem(), vmem()],
        out_specs=[vmem()] * 2,
        compiler_params=params(BIG),
        cost_estimate=cost(0, MIB),
        name="weight_spread",
    )(address.reshape(1), held)

    grad_feats = pl.pallas_call(
        final_kernel,
        out_shape=sds((chan_width, node_count), BF),
        in_specs=[smem()] + [vmem()] * 2,
        out_specs=vmem(),
        scratch_shapes=[pltpu.VMEM((block_rows, chan_width, size), F32)],
        compiler_params=params(BIG),
        cost_estimate=cost(0, 4 * MIB),
        name="sum_returned",
    )(send, near, back)
    return (out_h, grad_feats.T, grad_w_self, grad_w_neigh)


def solution(mesh):
    return jax.shard_map(
        per_device,
        mesh=mesh,
        in_specs=(
            P("dom", "chan"),
            P("dom", None, None, None),
            P("dom", None),
            P("dom"),
            P("dom", None, None),
            P(),
            P(),
            P(),
            P(("dom", "chan"), None),
        ),
        out_specs=(P(("dom", "chan"), None), P("dom", "chan"), P("chan", None), P("chan", None)),
        check_vma=False,
    )
```

```python
import functools

import jax
import jax.numpy as jnp
from jax import lax
from jax.experimental import pallas as pl
from jax.experimental.pallas import tpu as pltpu
from jax.sharding import PartitionSpec as P

BF = jnp.bfloat16
F32 = jnp.float32
MIB = 1 << 20
BIG = 8


def vmem():
    return pl.BlockSpec(memory_space=pltpu.VMEM)


def hbm():
    return pl.BlockSpec(memory_space=pltpu.HBM)


def smem():
    return pl.BlockSpec(memory_space=pltpu.SMEM)


def params(mib):
    return pltpu.CompilerParams(vmem_limit_bytes=mib * MIB)


def cost(flops, nbytes):
    return pl.CostEstimate(flops=flops, bytes_accessed=nbytes, transcendentals=0)


def nt_dot(left, right):
    return lax.dot_general(left, right, (((1,), (1,)), ((), ())), preferred_element_type=F32)


def nn_dot(left, right):
    return lax.dot_general(left, right, (((1,), (0,)), ((), ())), preferred_element_type=F32)


def pack_kernel(send_ref, feats_ref, out_ref, hold_ref, sems):
    dests, slots, _, size = hold_ref.shape
    copies = sems.shape[0]
    span = dests // copies
    for copy in range(copies):
        for dest in range(copy * span, (copy + 1) * span):
            for slot in range(slots):
                lane = pl.multiple_of(send_ref[slot, dest] * size, size)
                hold_ref[dest, slot] = feats_ref[:, pl.ds(lane, size)]
        place = pl.ds(copy * span, span)
        pltpu.make_async_copy(hold_ref.at[place], out_ref.at[place], sems.at[copy]).start()
    for copy in range(copies):
        place = pl.ds(copy * span, span)
        pltpu.make_async_copy(hold_ref.at[place], out_ref.at[place], sems.at[copy]).wait()


def split_kernel(me_ref, feats_ref, *refs):
    out_refs, sems = refs[:-1], refs[-1]
    chans = len(out_refs)
    width = out_refs[0].shape[1]

    def copy(shift):
        lane = pl.multiple_of(lax.rem(me_ref[0] + shift, chans) * width, width)
        return pltpu.make_async_copy(feats_ref.at[:, pl.ds(lane, width)], out_refs[shift], sems.at[shift])

    for shift in range(chans):
        copy(shift).start()
    for shift in range(chans):
        copy(shift).wait()


def join_slots(vals_ref, row):
    return jnp.concatenate([vals_ref[row, k] for k in range(vals_ref.shape[1])], axis=1)


def stream_rows(vals_ref, held_ref, sems, body, before=None, after=None):
    copies = sems.shape[0]
    span = held_ref.shape[0] // copies

    def copy(place):
        rows = pl.ds(place * span, span)
        return pltpu.make_async_copy(vals_ref.at[rows], held_ref.at[rows], sems.at[place])

    for place in range(copies):
        copy(place).start()
    if before is not None:
        before()

    def one(place, carry):
        copy(place).wait()
        for row in range(span):
            body(place * span + row)
        if after is not None:
            after(place)
        return carry

    lax.fori_loop(0, copies, one, 0)


def gather_kernel(
    cols_ref, counts_ref, feats_ref, recv_ref, vals_ref, out_ref, degree_ref, held_ref, mean_ref, sems, out_sems
):
    _, depth, size, _ = vals_ref.shape
    width = feats_ref.shape[0]
    rows = out_ref.shape[2] // size
    own = feats_ref.shape[1] // size
    ones = jnp.ones((16, size), BF)

    def body(index):
        count = counts_ref[index]
        picked = []
        for k in range(depth):
            col = cols_ref[k, index]
            lane = pl.multiple_of(jnp.minimum(col, own - 1) * size, size)
            near = feats_ref[:, pl.ds(lane, size)]
            far = recv_ref[jnp.maximum(col - own, 0)]
            block = jnp.concatenate([jnp.where(col < own, near, far), ones], axis=0)
            picked.append(jnp.where(k < count, block, jnp.zeros_like(block)))
        total = nt_dot(join_slots(held_ref, index), jnp.concatenate(picked, axis=1)).T
        group = index // rows
        place = pl.ds(pl.multiple_of(lax.rem(index, rows) * size, size), size)
        degree_ref[group, :, place] = total[width : width + 8]
        mean_ref[group, :, place] = (total[:width] / total[width : width + 1]).astype(BF)

    copies = out_sems.shape[0]
    span = mean_ref.shape[0] // copies

    def copy(place):
        groups = pl.ds(place * span, span)
        return pltpu.make_async_copy(mean_ref.at[groups], out_ref.at[groups], out_sems.at[place])

    stream_rows(vals_ref, held_ref, sems, body, after=lambda place: copy(place).start())
    for place in range(copies):
        copy(place).wait()


def self_kernel(chans, me_ref, weight_ref, bias_ref, neigh_ref, cot_ref, *refs):
    chunk_refs = refs[:chans]
    full_ref, pre_ref, neigh_turned_ref, cot_turned_ref = refs[chans:]
    neigh_turned_ref[...] = neigh_ref[...].T
    cot_turned_ref[...] = cot_ref[...].T
    height = chunk_refs[0].shape[0]
    for shift, chunk_ref in enumerate(chunk_refs):
        start = pl.multiple_of(lax.rem(me_ref[0] + (chans - shift), chans) * height, height)
        full_ref[pl.ds(start, height), :] = chunk_ref[...]
    pre_ref[...] = nn_dot(weight_ref[...].T, full_ref[...]) + bias_ref[...]


def head_kernel(me_ref, degree_ref, pre_ref, turned_ref, weight_ref, cot_ref, mean_ref, out_ref, grad_ref, scaled_ref):
    preact = pre_ref[...] + nn_dot(turned_ref[...], mean_ref[...])
    logistic = jax.nn.sigmoid(preact)
    activated = preact * logistic
    slope = logistic * (1.0 + preact * (1.0 - logistic))
    inverse = 1.0 / jnp.sqrt(jnp.mean(activated * activated, axis=0, keepdims=True) + 1e-06)
    unit = activated * inverse
    cot = cot_ref[...].astype(F32)
    grad_act = (cot - unit * jnp.mean(cot * unit, axis=0, keepdims=True)) * inverse
    grad = (grad_act * slope).astype(BF)
    out_ref[...] = unit.astype(BF)
    grad_ref[...] = grad
    mean_grad = nn_dot(weight_ref[...], grad).astype(BF).astype(F32)
    degree = degree_ref[me_ref[0], 0:1, :]
    scaled_ref[...] = (mean_grad / degree).astype(BF)


def weight_partial_kernel(me_ref, feats_ref, mean_ref, grad_ref, keep_ref, give_ref, hold_ref):
    parts, chans, unit, lanes = hold_ref.shape
    grad = grad_ref[...]
    totals = [nt_dot(feats_ref[...], grad), nt_dot(mean_ref[...], grad)]
    width = totals[0].shape[0] // chans
    halves = totals[0].shape[1] // lanes
    count = width // unit
    for which, total in enumerate(totals):
        for half in range(halves):
            place = (which * halves + half) * count
            for chan in range(chans):
                piece = total[chan * width : (chan + 1) * width, half * lanes : (half + 1) * lanes]
                hold_ref[place : place + count, chan] = piece.reshape(count, unit, lanes)
    half = parts // 2
    bit = me_ref[0]
    keep_ref[...] = hold_ref[pl.ds(bit * half, half)]
    give_ref[...] = hold_ref[pl.ds((1 - bit) * half, half)].astype(BF)


def halve_kernel(me_ref, held_ref, recv_ref, keep_ref, give_ref, hold_ref):
    half = keep_ref.shape[0]
    bit = me_ref[0]
    hold_ref[...] = held_ref[...] + recv_ref[...].astype(F32)
    keep_ref[...] = hold_ref[pl.ds(bit * half, half)]
    give_ref[...] = hold_ref[pl.ds((1 - bit) * half, half)].astype(BF)


def add_round_kernel(held_ref, recv_ref, out_ref):
    out_ref[...] = (held_ref[...] + recv_ref[...].astype(F32)).astype(BF)


def add_pair_kernel(held_ref, recv_ref, out_ref):
    out_ref[...] = (held_ref[...].astype(F32) + recv_ref[...].astype(F32)).astype(BF)


def side_kernel(chans, me_ref, weight_ref, out_ref, grad_ref, turned_ref, *refs):
    self_refs = refs[:chans]
    (hold_ref,) = refs[chans:]
    turned_ref[...] = out_ref[...].T
    hold_ref[...] = nn_dot(weight_ref[...], grad_ref[...]).astype(BF)
    height = self_refs[0].shape[0]
    for shift, self_ref in enumerate(self_refs):
        start = pl.multiple_of(lax.rem(me_ref[0] + shift, chans) * height, height)
        self_ref[...] = hold_ref[pl.ds(start, height), :]


def message_kernel(chans, me_ref, unit_ref, *refs):
    self_refs = refs[:chans]
    packed_refs = refs[chans:]
    nodes = self_refs[0].shape[1]
    units, _, unit, lanes = unit_ref.shape
    for shift, packed_ref in enumerate(packed_refs):
        dest = lax.rem(me_ref[0] + shift, chans)
        piece = unit_ref[:, dest].astype(F32).reshape(units * unit, lanes)
        packed_ref[:, :nodes] = self_refs[shift][...]
        packed_ref[: units * unit, nodes:] = piece.astype(BF)
        packed_ref[units * unit :, nodes:] = jnp.zeros_like(packed_ref[units * unit :, nodes:])


def scatter_kernel(
    cols_ref, counts_ref, vals_ref, scaled_ref, own_ref, far_ref, held_ref, hold_ref, send_ref, val_sems, sems, own_sem
):
    _, depth, size, _ = vals_ref.shape
    rows = scaled_ref.shape[2] // size
    own = own_ref.shape[0]

    def clear():
        hold_ref[...] = jnp.zeros_like(hold_ref)

    def body(index):
        count = counts_ref[index]
        place = pl.ds(pl.multiple_of(lax.rem(index, rows) * size, size), size)
        total = nn_dot(scaled_ref[index // rows, :, place], join_slots(held_ref, index))
        for k in range(depth):
            part = total[:, k * size : (k + 1) * size]
            hold_ref[cols_ref[k, index]] += jnp.where(k < count, part, jnp.zeros_like(part))

    stream_rows(vals_ref, held_ref, val_sems, body, clear)
    copies = sems.shape[0]
    span = far_ref.shape[0] // copies
    for copy in range(copies):
        send_ref[copy * span : (copy + 1) * span] = hold_ref[own + copy * span : own + (copy + 1) * span].astype(BF)
        place = pl.ds(copy * span, span)
        pltpu.make_async_copy(send_ref.at[place], far_ref.at[place], sems.at[copy]).start()
    pltpu.make_async_copy(hold_ref.at[pl.ds(0, own)], own_ref, own_sem).start()
    for copy in range(copies):
        place = pl.ds(copy * span, span)
        pltpu.make_async_copy(send_ref.at[place], far_ref.at[place], sems.at[copy]).wait()
    pltpu.make_async_copy(hold_ref.at[pl.ds(0, own)], own_ref, own_sem).wait()


def unit_kernel(*refs):
    packed_refs = refs[:-1]
    out_ref = refs[-1]
    rows, lanes = out_ref.shape
    total = packed_refs[0][:rows, -lanes:].astype(F32)
    for packed_ref in packed_refs[1:]:
        total = total + packed_ref[:rows, -lanes:].astype(F32)
    out_ref[...] = total.astype(BF)


def spread_kernel(scale, me_ref, held_ref, self_ref, neigh_ref):
    pieces, rows, lanes = held_ref.shape
    half = pieces // 2
    unit_rows = self_ref.shape[0]
    per = unit_rows // rows
    for place in range(pieces):
        value = held_ref[lax.bitwise_xor(me_ref[0], place)].astype(F32) * scale
        target = self_ref if place < half else neigh_ref
        inside = place % half
        column, row = inside // per, inside % per
        target[row * rows : (row + 1) * rows, column * lanes : (column + 1) * lanes] = value


def near_kernel(shifts, me_ref, own_ref, *refs):
    chans = len(shifts)
    packed_refs = refs[:chans]
    (out_ref,) = refs[chans:]
    blocks, _, size = out_ref.shape
    rows = blocks // chans
    for shift, packed_ref in zip(shifts, packed_refs):
        group = lax.rem(me_ref[0] + (chans - shift), chans)
        for row in range(rows):
            index = group * rows + row
            out_ref[index] = own_ref[index] + packed_ref[:, row * size : (row + 1) * size].astype(F32)


def final_kernel(send_ref, near_ref, back_ref, out_ref, hold_ref):
    slots, dests = send_ref.shape
    blocks, _, size = hold_ref.shape
    hold_ref[...] = near_ref[...]

    def one(dest, carry):
        for slot in range(slots):
            hold_ref[send_ref[slot, dest]] += back_ref[dest, slot].astype(F32)
        return carry

    lax.fori_loop(0, dests, one, 0, unroll=8)
    for block in range(blocks):
        out_ref[:, block * size : (block + 1) * size] = hold_ref[block].astype(BF)


def exchange(chunks):
    count = len(chunks)
    received = list(chunks)
    for shift in range(1, count):
        received[shift] = lax.ppermute(chunks[shift], "chan", [(i, (i + shift) % count) for i in range(count)])
    return received


def sds(shape, dtype):
    return jax.ShapeDtypeStruct(shape, dtype)


def halving_order(parts):
    count = parts.bit_length() - 1
    return [bit for bit in (0, 1, 3, 2, 4) if bit < count] + list(range(5, count))


def add_round(kernel, left, right):
    return pl.pallas_call(
        kernel,
        out_shape=sds(left.shape, BF),
        in_specs=[vmem()] * 2,
        out_specs=vmem(),
        compiler_params=params(BIG),
        cost_estimate=cost(0, MIB),
        name="weight_add",
    )(left, right)


def per_device(feats, block_vals, block_cols, block_counts, send_list, w_self, w_neigh, bias, cotangent):
    node_count, chan_width = feats.shape
    block_rows, depth, size, _ = block_vals.shape
    parts = lax.axis_size("dom")
    chans = lax.axis_size("chan")
    slots = send_list.shape[2]
    f_in, f_out = w_self.shape
    nodes = node_count // chans
    rows = block_rows // chans
    table = block_rows + parts * slots
    chan = lax.axis_index("chan").astype(jnp.int32)
    part = lax.axis_index("dom").astype(jnp.int32)
    me = chan.reshape(1)
    send = send_list[0].T
    cols = block_cols.T
    feats_t = feats.T
    val_bytes = block_vals.size * 2
    vals = pltpu.with_memory_space_constraint(block_vals, pltpu.HBM)
    block_flops = 2 * block_rows * depth * size * size * chan_width
    layer_flops = 2 * f_in * f_out * nodes
    unit, lanes = 8, 128
    copies, streams = 8, 4

    outgoing = pl.pallas_call(
        pack_kernel,
        out_shape=pltpu.HBM((parts, slots, chan_width, size), BF),
        in_specs=[smem(), vmem()],
        out_specs=hbm(),
        scratch_shapes=[pltpu.VMEM((parts, slots, chan_width, size), BF), pltpu.SemaphoreType.DMA((copies,))],
        compiler_params=params(8),
        cost_estimate=cost(0, 5 * MIB),
        name="pack_outgoing",
    )(
        pltpu.with_memory_space_constraint(send, pltpu.HBM),
        pltpu.with_memory_space_constraint(feats_t, pltpu.HBM),
    )
    incoming = lax.all_to_all(outgoing, "dom", split_axis=0, concat_axis=0, tiled=True)

    feat_chunks = pl.pallas_call(
        split_kernel,
        out_shape=[pltpu.HBM((chan_width, nodes), BF)] * chans,
        in_specs=[smem(), vmem()],
        out_specs=[hbm()] * chans,
        scratch_shapes=[pltpu.SemaphoreType.DMA((chans,))],
        compiler_params=params(BIG),
        cost_estimate=cost(0, MIB),
        name="split_feats",
    )(me, feats_t)
    incoming, feat_chunks = lax.optimization_barrier((incoming, exchange(feat_chunks)))
    feat_chunks = [pltpu.with_memory_space_constraint(chunk, pltpu.HBM) for chunk in feat_chunks]
    feats_own, pre_self, neigh_turned, cot_turned = pl.pallas_call(
        functools.partial(self_kernel, chans),
        out_shape=[sds((f_in, nodes), BF), sds((f_out, nodes), F32), sds((f_out, f_in), BF), sds((f_out, nodes), BF)],
        in_specs=[smem()] + [vmem()] * (4 + chans),
        out_specs=[vmem()] * 4,
        compiler_params=params(BIG),
        cost_estimate=cost(layer_flops, 2 * MIB),
        name="self_part",
    )(me, w_self, bias.reshape(f_out, 1), w_neigh, cotangent, *feat_chunks)

    mean, degree = pl.pallas_call(
        gather_kernel,
        out_shape=[pltpu.HBM((chans, chan_width, nodes), BF), sds((chans, 8, nodes), F32)],
        in_specs=[smem(), smem()] + [vmem()] * 2 + [hbm()],
        out_specs=[hbm(), vmem()],
        scratch_shapes=[
            pltpu.VMEM(block_vals.shape, BF),
            pltpu.VMEM((chans, chan_width, nodes), BF),
            pltpu.SemaphoreType.DMA((streams,)),
            pltpu.SemaphoreType.DMA((streams,)),
        ],
        compiler_params=params(16),
        cost_estimate=cost(block_flops, val_bytes + 3 * MIB),
        name="neighbour_mean",
    )(cols, block_counts, feats_t, incoming.reshape(parts * slots, chan_width, size), vals)
    mean = lax.all_to_all(mean, "chan", split_axis=0, concat_axis=0, tiled=True).reshape(f_in, nodes)

    out_t, grad_t, scaled = pl.pallas_call(
        head_kernel,
        out_shape=[sds((f_out, nodes), BF), sds((f_out, nodes), BF), sds((f_in, nodes), BF)],
        in_specs=[smem()] + [vmem()] * 6,
        out_specs=[vmem()] * 3,
        compiler_params=params(BIG),
        cost_estimate=cost(2 * layer_flops, 4 * MIB),
        name="layer_head",
    )(me, degree, pre_self, neigh_turned, w_neigh, cot_turned, mean)
    scaled = lax.all_to_all(
        scaled.reshape(chans, chan_width, nodes), "chan", split_axis=0, concat_axis=0, tiled=True
    )

    order = halving_order(parts)
    halves, wholes = order[:3], order[3:]
    flips = [[(i, i ^ (1 << bit)) for i in range(parts)] for bit in order]
    bits = [((part >> bit) & 1).reshape(1) for bit in order]
    pieces = parts
    keep, give = pl.pallas_call(
        weight_partial_kernel,
        out_shape=[sds((pieces // 2, chans, unit, lanes), F32), sds((pieces // 2, chans, unit, lanes), BF)],
        in_specs=[smem()] + [vmem()] * 3,
        out_specs=[vmem()] * 2,
        scratch_shapes=[pltpu.VMEM((pieces, chans, unit, lanes), F32)],
        compiler_params=params(BIG),
        cost_estimate=cost(2 * layer_flops, 3 * MIB),
        name="weight_partial",
    )(bits[0], feats_own, mean, grad_t)
    pieces //= 2
    for level in range(1, len(halves)):
        got = lax.ppermute(give, "dom", flips[level - 1])
        keep, give = pl.pallas_call(
            halve_kernel,
            out_shape=[sds((pieces // 2, chans, unit, lanes), F32), sds((pieces // 2, chans, unit, lanes), BF)],
            in_specs=[smem()] + [vmem()] * 2,
            out_specs=[vmem()] * 2,
            scratch_shapes=[pltpu.VMEM((pieces, chans, unit, lanes), F32)],
            compiler_params=params(BIG),
            cost_estimate=cost(0, MIB),
            name="weight_halve",
        )(bits[level], keep, got)
        pieces //= 2
    got = lax.ppermute(give, "dom", flips[len(halves) - 1])
    total = add_round(add_round_kernel, keep, got)

    side = pl.pallas_call(
        functools.partial(side_kernel, chans),
        out_shape=[sds((nodes, f_out), BF)] + [sds((chan_width, nodes), BF)] * chans,
        in_specs=[smem()] + [vmem()] * 3,
        out_specs=[vmem()] * (1 + chans),
        scratch_shapes=[pltpu.VMEM((f_in, nodes), BF)],
        compiler_params=params(BIG),
        cost_estimate=cost(layer_flops, 3 * MIB),
        name="side_grads",
    )(me, w_self, out_t, grad_t)
    for level in range(len(halves), len(order) - 1):
        got = lax.ppermute(total, "dom", flips[level])
        total = add_round(add_pair_kernel, total, got)
    scaled, total, side = lax.optimization_barrier((scaled, total, side))
    out_h = side[0]
    own_grad, far_grad = pl.pallas_call(
        scatter_kernel,
        out_shape=[
            pltpu.HBM((block_rows, chan_width, size), F32),
            pltpu.HBM((parts * slots, chan_width, size), BF),
        ],
        in_specs=[smem(), smem(), hbm(), vmem()],
        out_specs=[hbm(), hbm()],
        scratch_shapes=[
            pltpu.VMEM(block_vals.shape, BF),
            pltpu.VMEM((table, chan_width, size), F32),
            pltpu.VMEM((parts * slots, chan_width, size), BF),
            pltpu.SemaphoreType.DMA((streams,)),
            pltpu.SemaphoreType.DMA((copies,)),
            pltpu.SemaphoreType.DMA,
        ],
        compiler_params=params(24),
        cost_estimate=cost(block_flops, val_bytes + 4 * MIB),
        name="table_grad",
    )(cols, block_counts, vals, scaled)
    total, far_grad = lax.optimization_barrier((total, far_grad))
    back = lax.all_to_all(
        far_grad.reshape(parts, slots, chan_width, size), "dom", split_axis=0, concat_axis=0, tiled=True
    )

    packed = pl.pallas_call(
        functools.partial(message_kernel, chans),
        out_shape=[sds((chan_width, nodes + lanes), BF)] * chans,
        in_specs=[smem()] + [vmem()] * (1 + chans),
        out_specs=[vmem()] * chans,
        compiler_params=params(BIG),
        cost_estimate=cost(0, MIB),
        name="pack_messages",
    )(me, total, *side[1:])
    packed = exchange(packed)
    shifts = sorted(range(chans), key=lambda shift: -min(shift, chans - shift))
    packed = [packed[shift] for shift in shifts]
    held = pl.pallas_call(
        unit_kernel,
        out_shape=sds((pieces * unit, lanes), BF),
        in_specs=[vmem()] * chans,
        out_specs=vmem(),
        compiler_params=params(BIG),
        cost_estimate=cost(0, MIB),
        name="weight_sum",
    )(*packed).reshape(1, pieces * unit, lanes)
    near = pl.pallas_call(
        functools.partial(near_kernel, shifts),
        out_shape=sds((block_rows, chan_width, size), F32),
        in_specs=[smem()] + [vmem()] * (1 + chans),
        out_specs=vmem(),
        compiler_params=params(BIG),
        cost_estimate=cost(0, 3 * MIB),
        name="sum_near",
    )(me, own_grad, *packed)
    whole, half = 1 << order[-1], 1 << halves[-1]
    across, beside, both = (
        lax.ppermute(held, "dom", [(i, i ^ flip) for i in range(parts)]) for flip in (whole, half, whole | half)
    )
    mine = held.astype(F32) + across.astype(F32)
    other = beside.astype(F32) + both.astype(F32)
    held = jnp.concatenate([mine, other], axis=0).astype(BF)
    held, back, near = lax.optimization_barrier((held, back, near))
    grad_feats = pl.pallas_call(
        final_kernel,
        out_shape=sds((chan_width, node_count), BF),
        in_specs=[smem()] + [vmem()] * 2,
        out_specs=vmem(),
        scratch_shapes=[pltpu.VMEM((block_rows, chan_width, size), F32)],
        compiler_params=params(BIG),
        cost_estimate=cost(0, 4 * MIB),
        name="sum_returned",
    )(send, near, back)
    for level in reversed(range(len(halves) - 1)):
        held = jnp.concatenate([held, lax.ppermute(held, "dom", flips[level])], axis=0)
        if level == len(halves) - 2:
            held, grad_feats = lax.optimization_barrier((held, grad_feats))
    address = jnp.int32(0)
    for level in range(len(halves)):
        address = address * 2 + bits[level][0]
    grad_w_self, grad_w_neigh = pl.pallas_call(
        functools.partial(spread_kernel, float(node_count * parts) ** (-0.5)),
        out_shape=[sds((chan_width, f_out), F32)] * 2,
        in_specs=[smem(), vmem()],
        out_specs=[vmem()] * 2,
        compiler_params=params(BIG),
        cost_estimate=cost(0, MIB),
        name="weight_spread",
    )(address.reshape(1), held)

    return (out_h, grad_feats.T, grad_w_self, grad_w_neigh)


def solution(mesh):
    return jax.shard_map(
        per_device,
        mesh=mesh,
        in_specs=(
            P("dom", "chan"),
            P("dom", None, None, None),
            P("dom", None),
            P("dom"),
            P("dom", None, None),
            P(),
            P(),
            P(),
            P(("dom", "chan"), None),
        ),
        out_specs=(P(("dom", "chan"), None), P("dom", "chan"), P("chan", None), P("chan", None)),
        check_vma=False,
    )
```

```python
import functools

import jax
import jax.numpy as jnp
from jax import lax
from jax.experimental import pallas as pl
from jax.experimental.pallas import tpu as pltpu
from jax.sharding import PartitionSpec as P

BF = jnp.bfloat16
F32 = jnp.float32
MIB = 1 << 20
BIG = 8


def vmem():
    return pl.BlockSpec(memory_space=pltpu.VMEM)


def hbm():
    return pl.BlockSpec(memory_space=pltpu.HBM)


def smem():
    return pl.BlockSpec(memory_space=pltpu.SMEM)


def params(mib):
    return pltpu.CompilerParams(vmem_limit_bytes=mib * MIB)


def cost(flops, nbytes):
    return pl.CostEstimate(flops=flops, bytes_accessed=nbytes, transcendentals=0)


def nt_dot(left, right):
    return lax.dot_general(left, right, (((1,), (1,)), ((), ())), preferred_element_type=F32)


def nn_dot(left, right):
    return lax.dot_general(left, right, (((1,), (0,)), ((), ())), preferred_element_type=F32)


def pack_kernel(send_ref, feats_ref, out_ref, hold_ref, sems):
    dests, slots, _, size = hold_ref.shape
    copies = sems.shape[0]
    span = dests // copies
    for copy in range(copies):
        for dest in range(copy * span, (copy + 1) * span):
            for slot in range(slots):
                lane = pl.multiple_of(send_ref[slot, dest] * size, size)
                hold_ref[dest, slot] = feats_ref[:, pl.ds(lane, size)]
        place = pl.ds(copy * span, span)
        pltpu.make_async_copy(hold_ref.at[place], out_ref.at[place], sems.at[copy]).start()
    for copy in range(copies):
        place = pl.ds(copy * span, span)
        pltpu.make_async_copy(hold_ref.at[place], out_ref.at[place], sems.at[copy]).wait()


def split_kernel(me_ref, feats_ref, *refs):
    out_refs, sems = refs[:-1], refs[-1]
    chans = len(out_refs)
    width = out_refs[0].shape[1]

    def copy(shift):
        lane = pl.multiple_of(lax.rem(me_ref[0] + shift, chans) * width, width)
        return pltpu.make_async_copy(feats_ref.at[:, pl.ds(lane, width)], out_refs[shift], sems.at[shift])

    for shift in range(chans):
        copy(shift).start()
    for shift in range(chans):
        copy(shift).wait()


def join_slots(vals_ref, row):
    return jnp.concatenate([vals_ref[row, k] for k in range(vals_ref.shape[1])], axis=1)


def stream_rows(vals_ref, held_ref, sems, body, before=None, after=None):
    copies = sems.shape[0]
    span = held_ref.shape[0] // copies

    def copy(place):
        rows = pl.ds(place * span, span)
        return pltpu.make_async_copy(vals_ref.at[rows], held_ref.at[rows], sems.at[place])

    for place in range(copies):
        copy(place).start()
    if before is not None:
        before()

    def one(place, carry):
        copy(place).wait()
        for row in range(span):
            body(place * span + row)
        if after is not None:
            after(place)
        return carry

    lax.fori_loop(0, copies, one, 0)


def gather_kernel(
    cols_ref, counts_ref, feats_ref, recv_ref, vals_ref, out_ref, degree_ref, held_ref, mean_ref, sems, out_sems
):
    _, depth, size, _ = vals_ref.shape
    width = feats_ref.shape[0]
    rows = out_ref.shape[2] // size
    own = feats_ref.shape[1] // size
    ones = jnp.ones((16, size), BF)

    def body(index):
        count = counts_ref[index]
        picked = []
        for k in range(depth):
            col = cols_ref[k, index]
            lane = pl.multiple_of(jnp.minimum(col, own - 1) * size, size)
            near = feats_ref[:, pl.ds(lane, size)]
            far = recv_ref[jnp.maximum(col - own, 0)]
            block = jnp.concatenate([jnp.where(col < own, near, far), ones], axis=0)
            picked.append(jnp.where(k < count, block, jnp.zeros_like(block)))
        total = nt_dot(join_slots(held_ref, index), jnp.concatenate(picked, axis=1)).T
        group = index // rows
        place = pl.ds(pl.multiple_of(lax.rem(index, rows) * size, size), size)
        degree_ref[group, :, place] = total[width : width + 8]
        mean_ref[group, :, place] = (total[:width] / total[width : width + 1]).astype(BF)

    copies = out_sems.shape[0]
    span = mean_ref.shape[0] // copies

    def copy(place):
        groups = pl.ds(place * span, span)
        return pltpu.make_async_copy(mean_ref.at[groups], out_ref.at[groups], out_sems.at[place])

    stream_rows(vals_ref, held_ref, sems, body, after=lambda place: copy(place).start())
    for place in range(copies):
        copy(place).wait()


def self_kernel(chans, me_ref, weight_ref, bias_ref, neigh_ref, cot_ref, *refs):
    chunk_refs = refs[:chans]
    full_ref, pre_ref, neigh_turned_ref, cot_turned_ref = refs[chans:]
    neigh_turned_ref[...] = neigh_ref[...].T
    cot_turned_ref[...] = cot_ref[...].T
    height = chunk_refs[0].shape[0]
    for shift, chunk_ref in enumerate(chunk_refs):
        start = pl.multiple_of(lax.rem(me_ref[0] + (chans - shift), chans) * height, height)
        full_ref[pl.ds(start, height), :] = chunk_ref[...]
    pre_ref[...] = nn_dot(weight_ref[...].T, full_ref[...]) + bias_ref[...]


def head_kernel(me_ref, degree_ref, pre_ref, turned_ref, weight_ref, cot_ref, mean_ref, out_ref, grad_ref, scaled_ref):
    preact = pre_ref[...] + nn_dot(turned_ref[...], mean_ref[...])
    logistic = jax.nn.sigmoid(preact)
    activated = preact * logistic
    slope = logistic * (1.0 + preact * (1.0 - logistic))
    inverse = 1.0 / jnp.sqrt(jnp.mean(activated * activated, axis=0, keepdims=True) + 1e-06)
    unit = activated * inverse
    cot = cot_ref[...].astype(F32)
    grad_act = (cot - unit * jnp.mean(cot * unit, axis=0, keepdims=True)) * inverse
    grad = (grad_act * slope).astype(BF)
    out_ref[...] = unit.astype(BF)
    grad_ref[...] = grad
    mean_grad = nn_dot(weight_ref[...], grad).astype(BF).astype(F32)
    degree = degree_ref[me_ref[0], 0:1, :]
    scaled_ref[...] = (mean_grad / degree).astype(BF)


def weight_partial_kernel(me_ref, feats_ref, mean_ref, grad_ref, keep_ref, give_ref, hold_ref):
    parts, chans, unit, lanes = hold_ref.shape
    grad = grad_ref[...]
    totals = [nt_dot(feats_ref[...], grad), nt_dot(mean_ref[...], grad)]
    width = totals[0].shape[0] // chans
    halves = totals[0].shape[1] // lanes
    count = width // unit
    for which, total in enumerate(totals):
        for half in range(halves):
            place = (which * halves + half) * count
            for chan in range(chans):
                piece = total[chan * width : (chan + 1) * width, half * lanes : (half + 1) * lanes]
                hold_ref[place : place + count, chan] = piece.reshape(count, unit, lanes)
    half = parts // 2
    bit = me_ref[0]
    keep_ref[...] = hold_ref[pl.ds(bit * half, half)]
    give_ref[...] = hold_ref[pl.ds((1 - bit) * half, half)].astype(BF)


def halve_kernel(me_ref, held_ref, recv_ref, keep_ref, give_ref, hold_ref):
    half = keep_ref.shape[0]
    bit = me_ref[0]
    hold_ref[...] = held_ref[...] + recv_ref[...].astype(F32)
    keep_ref[...] = hold_ref[pl.ds(bit * half, half)]
    give_ref[...] = hold_ref[pl.ds((1 - bit) * half, half)].astype(BF)


def add_round_kernel(held_ref, recv_ref, out_ref):
    out_ref[...] = (held_ref[...] + recv_ref[...].astype(F32)).astype(BF)


def add_pair_kernel(held_ref, recv_ref, out_ref):
    out_ref[...] = (held_ref[...].astype(F32) + recv_ref[...].astype(F32)).astype(BF)


def side_kernel(chans, me_ref, weight_ref, out_ref, grad_ref, turned_ref, *refs):
    self_refs = refs[:chans]
    (hold_ref,) = refs[chans:]
    turned_ref[...] = out_ref[...].T
    hold_ref[...] = nn_dot(weight_ref[...], grad_ref[...]).astype(BF)
    height = self_refs[0].shape[0]
    for shift, self_ref in enumerate(self_refs):
        start = pl.multiple_of(lax.rem(me_ref[0] + shift, chans) * height, height)
        self_ref[...] = hold_ref[pl.ds(start, height), :]


def message_kernel(chans, me_ref, unit_ref, *refs):
    self_refs = refs[:chans]
    packed_refs = refs[chans:]
    nodes = self_refs[0].shape[1]
    units, _, unit, lanes = unit_ref.shape
    for shift, packed_ref in enumerate(packed_refs):
        dest = lax.rem(me_ref[0] + shift, chans)
        piece = unit_ref[:, dest].astype(F32).reshape(units * unit, lanes)
        packed_ref[:, :nodes] = self_refs[shift][...]
        packed_ref[: units * unit, nodes:] = piece.astype(BF)
        packed_ref[units * unit :, nodes:] = jnp.zeros_like(packed_ref[units * unit :, nodes:])


def scatter_kernel(
    cols_ref, counts_ref, vals_ref, scaled_ref, own_ref, far_ref, held_ref, hold_ref, send_ref, val_sems, sems, own_sem
):
    _, depth, size, _ = vals_ref.shape
    rows = scaled_ref.shape[2] // size
    own = own_ref.shape[0]

    def clear():
        hold_ref[...] = jnp.zeros_like(hold_ref)

    def body(index):
        count = counts_ref[index]
        place = pl.ds(pl.multiple_of(lax.rem(index, rows) * size, size), size)
        total = nn_dot(scaled_ref[index // rows, :, place], join_slots(held_ref, index))
        for k in range(depth):
            part = total[:, k * size : (k + 1) * size]
            hold_ref[cols_ref[k, index]] += jnp.where(k < count, part, jnp.zeros_like(part))

    stream_rows(vals_ref, held_ref, val_sems, body, clear)
    copies = sems.shape[0]
    span = far_ref.shape[0] // copies
    for copy in range(copies):
        send_ref[copy * span : (copy + 1) * span] = hold_ref[own + copy * span : own + (copy + 1) * span].astype(BF)
        place = pl.ds(copy * span, span)
        pltpu.make_async_copy(send_ref.at[place], far_ref.at[place], sems.at[copy]).start()
    pltpu.make_async_copy(hold_ref.at[pl.ds(0, own)], own_ref, own_sem).start()
    for copy in range(copies):
        place = pl.ds(copy * span, span)
        pltpu.make_async_copy(send_ref.at[place], far_ref.at[place], sems.at[copy]).wait()
    pltpu.make_async_copy(hold_ref.at[pl.ds(0, own)], own_ref, own_sem).wait()


def unit_kernel(*refs):
    packed_refs = refs[:-1]
    out_ref = refs[-1]
    rows, lanes = out_ref.shape
    total = packed_refs[0][:rows, -lanes:].astype(F32)
    for packed_ref in packed_refs[1:]:
        total = total + packed_ref[:rows, -lanes:].astype(F32)
    out_ref[...] = total.astype(BF)


def spread_kernel(scale, me_ref, held_ref, self_ref, neigh_ref):
    pieces, rows, lanes = held_ref.shape
    half = pieces // 2
    unit_rows = self_ref.shape[0]
    per = unit_rows // rows
    for place in range(pieces):
        value = held_ref[lax.bitwise_xor(me_ref[0], place)].astype(F32) * scale
        target = self_ref if place < half else neigh_ref
        inside = place % half
        column, row = inside // per, inside % per
        target[row * rows : (row + 1) * rows, column * lanes : (column + 1) * lanes] = value


def near_kernel(shifts, me_ref, own_ref, *refs):
    chans = len(shifts)
    packed_refs = refs[:chans]
    (out_ref,) = refs[chans:]
    blocks, _, size = out_ref.shape
    rows = blocks // chans
    for shift, packed_ref in zip(shifts, packed_refs):
        group = lax.rem(me_ref[0] + (chans - shift), chans)
        for row in range(rows):
            index = group * rows + row
            out_ref[index] = own_ref[index] + packed_ref[:, row * size : (row + 1) * size].astype(F32)


def final_kernel(send_ref, near_ref, back_ref, out_ref, hold_ref):
    slots, dests = send_ref.shape
    blocks, _, size = hold_ref.shape
    hold_ref[...] = near_ref[...]

    def one(dest, carry):
        for slot in range(slots):
            hold_ref[send_ref[slot, dest]] += back_ref[dest, slot].astype(F32)
        return carry

    lax.fori_loop(0, dests, one, 0, unroll=8)
    for block in range(blocks):
        out_ref[:, block * size : (block + 1) * size] = hold_ref[block].astype(BF)


def exchange(chunks):
    count = len(chunks)
    received = list(chunks)
    for shift in range(1, count):
        received[shift] = lax.ppermute(chunks[shift], "chan", [(i, (i + shift) % count) for i in range(count)])
    return received


def sds(shape, dtype):
    return jax.ShapeDtypeStruct(shape, dtype)


def halving_order(parts):
    count = parts.bit_length() - 1
    return [bit for bit in (0, 1, 3, 2, 4) if bit < count] + list(range(5, count))


def add_round(kernel, left, right):
    return pl.pallas_call(
        kernel,
        out_shape=sds(left.shape, BF),
        in_specs=[vmem()] * 2,
        out_specs=vmem(),
        compiler_params=params(BIG),
        cost_estimate=cost(0, MIB),
        name="weight_add",
    )(left, right)


def per_device(feats, block_vals, block_cols, block_counts, send_list, w_self, w_neigh, bias, cotangent):
    node_count, chan_width = feats.shape
    block_rows, depth, size, _ = block_vals.shape
    parts = lax.axis_size("dom")
    chans = lax.axis_size("chan")
    slots = send_list.shape[2]
    f_in, f_out = w_self.shape
    nodes = node_count // chans
    rows = block_rows // chans
    table = block_rows + parts * slots
    chan = lax.axis_index("chan").astype(jnp.int32)
    part = lax.axis_index("dom").astype(jnp.int32)
    me = chan.reshape(1)
    send = send_list[0].T
    cols = block_cols.T
    feats_t = feats.T
    val_bytes = block_vals.size * 2
    vals = pltpu.with_memory_space_constraint(block_vals, pltpu.HBM)
    block_flops = 2 * block_rows * depth * size * size * chan_width
    layer_flops = 2 * f_in * f_out * nodes
    unit, lanes = 8, 128
    copies, streams = 8, 4

    outgoing = pl.pallas_call(
        pack_kernel,
        out_shape=pltpu.HBM((parts, slots, chan_width, size), BF),
        in_specs=[smem(), vmem()],
        out_specs=hbm(),
        scratch_shapes=[pltpu.VMEM((parts, slots, chan_width, size), BF), pltpu.SemaphoreType.DMA((copies,))],
        compiler_params=params(8),
        cost_estimate=cost(0, 5 * MIB),
        name="pack_outgoing",
    )(
        pltpu.with_memory_space_constraint(send, pltpu.HBM),
        pltpu.with_memory_space_constraint(feats_t, pltpu.HBM),
    )
    incoming = lax.all_to_all(outgoing, "dom", split_axis=0, concat_axis=0, tiled=True)

    feat_chunks = pl.pallas_call(
        split_kernel,
        out_shape=[pltpu.HBM((chan_width, nodes), BF)] * chans,
        in_specs=[smem(), vmem()],
        out_specs=[hbm()] * chans,
        scratch_shapes=[pltpu.SemaphoreType.DMA((chans,))],
        compiler_params=params(BIG),
        cost_estimate=cost(0, MIB),
        name="split_feats",
    )(me, feats_t)
    incoming, feat_chunks = lax.optimization_barrier((incoming, exchange(feat_chunks)))
    feat_chunks = [pltpu.with_memory_space_constraint(chunk, pltpu.HBM) for chunk in feat_chunks]
    feats_own, pre_self, neigh_turned, cot_turned = pl.pallas_call(
        functools.partial(self_kernel, chans),
        out_shape=[sds((f_in, nodes), BF), sds((f_out, nodes), F32), sds((f_out, f_in), BF), sds((f_out, nodes), BF)],
        in_specs=[smem()] + [vmem()] * (4 + chans),
        out_specs=[vmem()] * 4,
        compiler_params=params(BIG),
        cost_estimate=cost(layer_flops, 2 * MIB),
        name="self_part",
    )(me, w_self, bias.reshape(f_out, 1), w_neigh, cotangent, *feat_chunks)

    mean, degree = pl.pallas_call(
        gather_kernel,
        out_shape=[pltpu.HBM((chans, chan_width, nodes), BF), sds((chans, 8, nodes), F32)],
        in_specs=[smem(), smem()] + [vmem()] * 2 + [hbm()],
        out_specs=[hbm(), vmem()],
        scratch_shapes=[
            pltpu.VMEM(block_vals.shape, BF),
            pltpu.VMEM((chans, chan_width, nodes), BF),
            pltpu.SemaphoreType.DMA((streams,)),
            pltpu.SemaphoreType.DMA((streams,)),
        ],
        compiler_params=params(16),
        cost_estimate=cost(block_flops, val_bytes + 3 * MIB),
        name="neighbour_mean",
    )(cols, block_counts, feats_t, incoming.reshape(parts * slots, chan_width, size), vals)
    mean = lax.all_to_all(mean, "chan", split_axis=0, concat_axis=0, tiled=True).reshape(f_in, nodes)

    out_t, grad_t, scaled = pl.pallas_call(
        head_kernel,
        out_shape=[sds((f_out, nodes), BF), sds((f_out, nodes), BF), sds((f_in, nodes), BF)],
        in_specs=[smem()] + [vmem()] * 6,
        out_specs=[vmem()] * 3,
        compiler_params=params(BIG),
        cost_estimate=cost(2 * layer_flops, 4 * MIB),
        name="layer_head",
    )(me, degree, pre_self, neigh_turned, w_neigh, cot_turned, mean)
    scaled = lax.all_to_all(
        scaled.reshape(chans, chan_width, nodes), "chan", split_axis=0, concat_axis=0, tiled=True
    )

    order = halving_order(parts)
    halves, wholes = order[:3], order[3:]
    flips = [[(i, i ^ (1 << bit)) for i in range(parts)] for bit in order]
    bits = [((part >> bit) & 1).reshape(1) for bit in order]
    pieces = parts
    keep, give = pl.pallas_call(
        weight_partial_kernel,
        out_shape=[sds((pieces // 2, chans, unit, lanes), F32), sds((pieces // 2, chans, unit, lanes), BF)],
        in_specs=[smem()] + [vmem()] * 3,
        out_specs=[vmem()] * 2,
        scratch_shapes=[pltpu.VMEM((pieces, chans, unit, lanes), F32)],
        compiler_params=params(BIG),
        cost_estimate=cost(2 * layer_flops, 3 * MIB),
        name="weight_partial",
    )(bits[0], feats_own, mean, grad_t)
    pieces //= 2
    for level in range(1, len(halves)):
        got = lax.ppermute(give, "dom", flips[level - 1])
        keep, give = pl.pallas_call(
            halve_kernel,
            out_shape=[sds((pieces // 2, chans, unit, lanes), F32), sds((pieces // 2, chans, unit, lanes), BF)],
            in_specs=[smem()] + [vmem()] * 2,
            out_specs=[vmem()] * 2,
            scratch_shapes=[pltpu.VMEM((pieces, chans, unit, lanes), F32)],
            compiler_params=params(BIG),
            cost_estimate=cost(0, MIB),
            name="weight_halve",
        )(bits[level], keep, got)
        pieces //= 2
    got = lax.ppermute(give, "dom", flips[len(halves) - 1])
    total = add_round(add_round_kernel, keep, got)

    side = pl.pallas_call(
        functools.partial(side_kernel, chans),
        out_shape=[sds((nodes, f_out), BF)] + [sds((chan_width, nodes), BF)] * chans,
        in_specs=[smem()] + [vmem()] * 3,
        out_specs=[vmem()] * (1 + chans),
        scratch_shapes=[pltpu.VMEM((f_in, nodes), BF)],
        compiler_params=params(BIG),
        cost_estimate=cost(layer_flops, 3 * MIB),
        name="side_grads",
    )(me, w_self, out_t, grad_t)
    for level in range(len(halves), len(order) - 1):
        got = lax.ppermute(total, "dom", flips[level])
        total = add_round(add_pair_kernel, total, got)
    scaled, total, side = lax.optimization_barrier((scaled, total, side))
    out_h = side[0]
    own_grad, far_grad = pl.pallas_call(
        scatter_kernel,
        out_shape=[
            pltpu.HBM((block_rows, chan_width, size), F32),
            pltpu.HBM((parts * slots, chan_width, size), BF),
        ],
        in_specs=[smem(), smem(), hbm(), vmem()],
        out_specs=[hbm(), hbm()],
        scratch_shapes=[
            pltpu.VMEM(block_vals.shape, BF),
            pltpu.VMEM((table, chan_width, size), F32),
            pltpu.VMEM((parts * slots, chan_width, size), BF),
            pltpu.SemaphoreType.DMA((streams,)),
            pltpu.SemaphoreType.DMA((copies,)),
            pltpu.SemaphoreType.DMA,
        ],
        compiler_params=params(24),
        cost_estimate=cost(block_flops, val_bytes + 4 * MIB),
        name="table_grad",
    )(cols, block_counts, vals, scaled)
    total, far_grad = lax.optimization_barrier((total, far_grad))
    back = lax.all_to_all(
        far_grad.reshape(parts, slots, chan_width, size), "dom", split_axis=0, concat_axis=0, tiled=True
    )

    packed = pl.pallas_call(
        functools.partial(message_kernel, chans),
        out_shape=[sds((chan_width, nodes + lanes), BF)] * chans,
        in_specs=[smem()] + [vmem()] * (1 + chans),
        out_specs=[vmem()] * chans,
        compiler_params=params(BIG),
        cost_estimate=cost(0, MIB),
        name="pack_messages",
    )(me, total, *side[1:])
    packed = exchange(packed)
    shifts = sorted(range(chans), key=lambda shift: -min(shift, chans - shift))
    packed = [packed[shift] for shift in shifts]
    held = pl.pallas_call(
        unit_kernel,
        out_shape=sds((pieces * unit, lanes), BF),
        in_specs=[vmem()] * chans,
        out_specs=vmem(),
        compiler_params=params(BIG),
        cost_estimate=cost(0, MIB),
        name="weight_sum",
    )(*packed).reshape(1, pieces * unit, lanes)
    near = pl.pallas_call(
        functools.partial(near_kernel, shifts),
        out_shape=sds((block_rows, chan_width, size), F32),
        in_specs=[smem()] + [vmem()] * (1 + chans),
        out_specs=vmem(),
        compiler_params=params(BIG),
        cost_estimate=cost(0, 3 * MIB),
        name="sum_near",
    )(me, own_grad, *packed)
    whole = 1 << order[-1]
    places = []
    for place in range(1 << (len(halves) - 1)):
        flip = sum(1 << bit for level, bit in enumerate(reversed(halves[1:])) if place >> level & 1)
        pair = [
            lax.ppermute(held, "dom", [(i, i ^ away) for i in range(parts)]) if away else held
            for away in (flip, flip | whole)
        ]
        places.append(pair[0].astype(F32) + pair[1].astype(F32))
    held = jnp.concatenate(places, axis=0).astype(BF)
    held, back, near = lax.optimization_barrier((held, back, near))
    grad_feats = pl.pallas_call(
        final_kernel,
        out_shape=sds((chan_width, node_count), BF),
        in_specs=[smem()] + [vmem()] * 2,
        out_specs=vmem(),
        scratch_shapes=[pltpu.VMEM((block_rows, chan_width, size), F32)],
        compiler_params=params(BIG),
        cost_estimate=cost(0, 4 * MIB),
        name="sum_returned",
    )(send, near, back)
    held = jnp.concatenate([held, lax.ppermute(held, "dom", flips[0])], axis=0)
    address = jnp.int32(0)
    for level in range(len(halves)):
        address = address * 2 + bits[level][0]
    grad_w_self, grad_w_neigh = pl.pallas_call(
        functools.partial(spread_kernel, float(node_count * parts) ** (-0.5)),
        out_shape=[sds((chan_width, f_out), F32)] * 2,
        in_specs=[smem(), vmem()],
        out_specs=[vmem()] * 2,
        compiler_params=params(BIG),
        cost_estimate=cost(0, MIB),
        name="weight_spread",
    )(address.reshape(1), held)

    return (out_h, grad_feats.T, grad_w_self, grad_w_neigh)


def solution(mesh):
    return jax.shard_map(
        per_device,
        mesh=mesh,
        in_specs=(
            P("dom", "chan"),
            P("dom", None, None, None),
            P("dom", None),
            P("dom"),
            P("dom", None, None),
            P(),
            P(),
            P(),
            P(("dom", "chan"), None),
        ),
        out_specs=(P(("dom", "chan"), None), P("dom", "chan"), P("chan", None), P("chan", None)),
        check_vma=False,
    )
```

```python
import functools

import jax
import jax.numpy as jnp
from jax import lax
from jax.experimental import pallas as pl
from jax.experimental.pallas import tpu as pltpu
from jax.sharding import PartitionSpec as P

BF = jnp.bfloat16
F32 = jnp.float32
MIB = 1 << 20
BIG = 8


def vmem():
    return pl.BlockSpec(memory_space=pltpu.VMEM)


def hbm():
    return pl.BlockSpec(memory_space=pltpu.HBM)


def smem():
    return pl.BlockSpec(memory_space=pltpu.SMEM)


def params(mib):
    return pltpu.CompilerParams(vmem_limit_bytes=mib * MIB)


def cost(flops, nbytes):
    return pl.CostEstimate(flops=flops, bytes_accessed=nbytes, transcendentals=0)


def nt_dot(left, right):
    return lax.dot_general(left, right, (((1,), (1,)), ((), ())), preferred_element_type=F32)


def nn_dot(left, right):
    return lax.dot_general(left, right, (((1,), (0,)), ((), ())), preferred_element_type=F32)


def pack_kernel(send_ref, feats_ref, out_ref, hold_ref, sems):
    dests, slots, _, size = hold_ref.shape
    copies = sems.shape[0]
    span = dests // copies
    for copy in range(copies):
        for dest in range(copy * span, (copy + 1) * span):
            for slot in range(slots):
                lane = pl.multiple_of(send_ref[slot, dest] * size, size)
                hold_ref[dest, slot] = feats_ref[:, pl.ds(lane, size)]
        place = pl.ds(copy * span, span)
        pltpu.make_async_copy(hold_ref.at[place], out_ref.at[place], sems.at[copy]).start()
    for copy in range(copies):
        place = pl.ds(copy * span, span)
        pltpu.make_async_copy(hold_ref.at[place], out_ref.at[place], sems.at[copy]).wait()


def split_kernel(me_ref, feats_ref, *refs):
    out_refs, sems = refs[:-1], refs[-1]
    chans = len(out_refs)
    width = out_refs[0].shape[1]

    def copy(shift):
        lane = pl.multiple_of(lax.rem(me_ref[0] + shift, chans) * width, width)
        return pltpu.make_async_copy(feats_ref.at[:, pl.ds(lane, width)], out_refs[shift], sems.at[shift])

    for shift in range(chans):
        copy(shift).start()
    for shift in range(chans):
        copy(shift).wait()


def join_slots(vals_ref, row):
    return jnp.concatenate([vals_ref[row, k] for k in range(vals_ref.shape[1])], axis=1)


def stream_rows(vals_ref, held_ref, sems, body, before=None, after=None):
    copies = sems.shape[0]
    span = held_ref.shape[0] // copies

    def copy(place):
        rows = pl.ds(place * span, span)
        return pltpu.make_async_copy(vals_ref.at[rows], held_ref.at[rows], sems.at[place])

    for place in range(copies):
        copy(place).start()
    if before is not None:
        before()

    def one(place, carry):
        copy(place).wait()
        for row in range(span):
            body(place * span + row)
        if after is not None:
            after(place)
        return carry

    lax.fori_loop(0, copies, one, 0)


def gather_kernel(
    cols_ref, counts_ref, feats_ref, recv_ref, vals_ref, out_ref, degree_ref, held_ref, mean_ref, sems, out_sems
):
    _, depth, size, _ = vals_ref.shape
    width = feats_ref.shape[0]
    rows = out_ref.shape[2] // size
    own = feats_ref.shape[1] // size
    ones = jnp.ones((16, size), BF)

    def body(index):
        count = counts_ref[index]
        picked = []
        for k in range(depth):
            col = cols_ref[k, index]
            lane = pl.multiple_of(jnp.minimum(col, own - 1) * size, size)
            near = feats_ref[:, pl.ds(lane, size)]
            far = recv_ref[jnp.maximum(col - own, 0)]
            block = jnp.concatenate([jnp.where(col < own, near, far), ones], axis=0)
            picked.append(jnp.where(k < count, block, jnp.zeros_like(block)))
        total = nt_dot(join_slots(held_ref, index), jnp.concatenate(picked, axis=1)).T
        group = index // rows
        place = pl.ds(pl.multiple_of(lax.rem(index, rows) * size, size), size)
        degree_ref[group, :, place] = total[width : width + 8]
        mean_ref[group, :, place] = (total[:width] / total[width : width + 1]).astype(BF)

    copies = out_sems.shape[0]
    span = mean_ref.shape[0] // copies

    def copy(place):
        groups = pl.ds(place * span, span)
        return pltpu.make_async_copy(mean_ref.at[groups], out_ref.at[groups], out_sems.at[place])

    stream_rows(vals_ref, held_ref, sems, body, after=lambda place: copy(place).start())
    for place in range(copies):
        copy(place).wait()


def self_kernel(chans, me_ref, weight_ref, bias_ref, neigh_ref, cot_ref, *refs):
    chunk_refs = refs[:chans]
    full_ref, pre_ref, neigh_turned_ref, cot_turned_ref = refs[chans:]
    neigh_turned_ref[...] = neigh_ref[...].T
    cot_turned_ref[...] = cot_ref[...].T
    height = chunk_refs[0].shape[0]
    for shift, chunk_ref in enumerate(chunk_refs):
        start = pl.multiple_of(lax.rem(me_ref[0] + (chans - shift), chans) * height, height)
        full_ref[pl.ds(start, height), :] = chunk_ref[...]
    pre_ref[...] = nn_dot(weight_ref[...].T, full_ref[...]) + bias_ref[...]


def head_kernel(me_ref, degree_ref, pre_ref, turned_ref, weight_ref, cot_ref, mean_ref, out_ref, grad_ref, scaled_ref):
    preact = pre_ref[...] + nn_dot(turned_ref[...], mean_ref[...])
    logistic = jax.nn.sigmoid(preact)
    activated = preact * logistic
    slope = logistic * (1.0 + preact * (1.0 - logistic))
    inverse = 1.0 / jnp.sqrt(jnp.mean(activated * activated, axis=0, keepdims=True) + 1e-06)
    unit = activated * inverse
    cot = cot_ref[...].astype(F32)
    grad_act = (cot - unit * jnp.mean(cot * unit, axis=0, keepdims=True)) * inverse
    grad = (grad_act * slope).astype(BF)
    out_ref[...] = unit.astype(BF)
    grad_ref[...] = grad
    mean_grad = nn_dot(weight_ref[...], grad).astype(BF).astype(F32)
    degree = degree_ref[me_ref[0], 0:1, :]
    scaled_ref[...] = (mean_grad / degree).astype(BF)


def weight_partial_kernel(me_ref, feats_ref, mean_ref, grad_ref, keep_ref, give_ref, hold_ref):
    parts, chans, unit, lanes = hold_ref.shape
    grad = grad_ref[...]
    totals = [nt_dot(feats_ref[...], grad), nt_dot(mean_ref[...], grad)]
    width = totals[0].shape[0] // chans
    halves = totals[0].shape[1] // lanes
    count = width // unit
    for which, total in enumerate(totals):
        for half in range(halves):
            place = (which * halves + half) * count
            for chan in range(chans):
                piece = total[chan * width : (chan + 1) * width, half * lanes : (half + 1) * lanes]
                hold_ref[place : place + count, chan] = piece.reshape(count, unit, lanes)
    half = parts // 2
    bit = me_ref[0]
    keep_ref[...] = hold_ref[pl.ds(bit * half, half)]
    give_ref[...] = hold_ref[pl.ds((1 - bit) * half, half)].astype(BF)


def quarter_kernel(me_ref, held_ref, recv_ref, keep_ref, *refs):
    give_refs, hold_ref = refs[:-1], refs[-1]
    span = keep_ref.shape[0]
    hold_ref[...] = held_ref[...] + recv_ref[...].astype(F32)
    keep_ref[...] = hold_ref[pl.ds(me_ref[0] * span, span)]
    for flip, give_ref in enumerate(give_refs, 1):
        give_ref[...] = hold_ref[pl.ds(lax.bitwise_xor(me_ref[0], flip) * span, span)].astype(BF)


def add_round_kernel(held_ref, *refs):
    total = held_ref[...]
    for recv_ref in refs[:-1]:
        total = total + recv_ref[...].astype(F32)
    refs[-1][...] = total.astype(BF)


def add_pair_kernel(held_ref, recv_ref, out_ref):
    out_ref[...] = (held_ref[...].astype(F32) + recv_ref[...].astype(F32)).astype(BF)


def side_kernel(chans, me_ref, weight_ref, out_ref, grad_ref, turned_ref, *refs):
    self_refs = refs[:chans]
    (hold_ref,) = refs[chans:]
    turned_ref[...] = out_ref[...].T
    hold_ref[...] = nn_dot(weight_ref[...], grad_ref[...]).astype(BF)
    height = self_refs[0].shape[0]
    for shift, self_ref in enumerate(self_refs):
        start = pl.multiple_of(lax.rem(me_ref[0] + shift, chans) * height, height)
        self_ref[...] = hold_ref[pl.ds(start, height), :]


def message_kernel(chans, me_ref, unit_ref, *refs):
    self_refs = refs[:chans]
    packed_refs = refs[chans:]
    nodes = self_refs[0].shape[1]
    units, _, unit, lanes = unit_ref.shape
    for shift, packed_ref in enumerate(packed_refs):
        dest = lax.rem(me_ref[0] + shift, chans)
        piece = unit_ref[:, dest].astype(F32).reshape(units * unit, lanes)
        packed_ref[:, :nodes] = self_refs[shift][...]
        packed_ref[: units * unit, nodes:] = piece.astype(BF)
        packed_ref[units * unit :, nodes:] = jnp.zeros_like(packed_ref[units * unit :, nodes:])


def scatter_kernel(
    cols_ref, counts_ref, vals_ref, scaled_ref, own_ref, far_ref, held_ref, hold_ref, send_ref, val_sems, sems, own_sem
):
    _, depth, size, _ = vals_ref.shape
    rows = scaled_ref.shape[2] // size
    own = own_ref.shape[0]

    def clear():
        hold_ref[...] = jnp.zeros_like(hold_ref)

    def body(index):
        count = counts_ref[index]
        place = pl.ds(pl.multiple_of(lax.rem(index, rows) * size, size), size)
        total = nn_dot(scaled_ref[index // rows, :, place], join_slots(held_ref, index))
        for k in range(depth):
            part = total[:, k * size : (k + 1) * size]
            hold_ref[cols_ref[k, index]] += jnp.where(k < count, part, jnp.zeros_like(part))

    stream_rows(vals_ref, held_ref, val_sems, body, clear)
    copies = sems.shape[0]
    span = far_ref.shape[0] // copies
    for copy in range(copies):
        send_ref[copy * span : (copy + 1) * span] = hold_ref[own + copy * span : own + (copy + 1) * span].astype(BF)
        place = pl.ds(copy * span, span)
        pltpu.make_async_copy(send_ref.at[place], far_ref.at[place], sems.at[copy]).start()
    pltpu.make_async_copy(hold_ref.at[pl.ds(0, own)], own_ref, own_sem).start()
    for copy in range(copies):
        place = pl.ds(copy * span, span)
        pltpu.make_async_copy(send_ref.at[place], far_ref.at[place], sems.at[copy]).wait()
    pltpu.make_async_copy(hold_ref.at[pl.ds(0, own)], own_ref, own_sem).wait()


def unit_kernel(*refs):
    packed_refs = refs[:-1]
    out_ref = refs[-1]
    rows, lanes = out_ref.shape
    total = packed_refs[0][:rows, -lanes:].astype(F32)
    for packed_ref in packed_refs[1:]:
        total = total + packed_ref[:rows, -lanes:].astype(F32)
    out_ref[...] = total.astype(BF)


def spread_kernel(scale, me_ref, held_ref, self_ref, neigh_ref):
    pieces, rows, lanes = held_ref.shape
    half = pieces // 2
    unit_rows = self_ref.shape[0]
    per = unit_rows // rows
    for place in range(pieces):
        value = held_ref[lax.bitwise_xor(me_ref[0], place)].astype(F32) * scale
        target = self_ref if place < half else neigh_ref
        inside = place % half
        column, row = inside // per, inside % per
        target[row * rows : (row + 1) * rows, column * lanes : (column + 1) * lanes] = value


def near_kernel(shifts, me_ref, own_ref, *refs):
    chans = len(shifts)
    packed_refs = refs[:chans]
    (out_ref,) = refs[chans:]
    blocks, _, size = out_ref.shape
    rows = blocks // chans
    for shift, packed_ref in zip(shifts, packed_refs):
        group = lax.rem(me_ref[0] + (chans - shift), chans)
        for row in range(rows):
            index = group * rows + row
            out_ref[index] = own_ref[index] + packed_ref[:, row * size : (row + 1) * size].astype(F32)


def final_kernel(send_ref, near_ref, back_ref, out_ref, hold_ref):
    slots, dests = send_ref.shape
    blocks, _, size = hold_ref.shape
    hold_ref[...] = near_ref[...]

    def one(dest, carry):
        for slot in range(slots):
            hold_ref[send_ref[slot, dest]] += back_ref[dest, slot].astype(F32)
        return carry

    lax.fori_loop(0, dests, one, 0, unroll=8)
    for block in range(blocks):
        out_ref[:, block * size : (block + 1) * size] = hold_ref[block].astype(BF)


def exchange(chunks):
    count = len(chunks)
    received = list(chunks)
    for shift in range(1, count):
        received[shift] = lax.ppermute(chunks[shift], "chan", [(i, (i + shift) % count) for i in range(count)])
    return received


def sds(shape, dtype):
    return jax.ShapeDtypeStruct(shape, dtype)


def halving_order(parts):
    count = parts.bit_length() - 1
    return [bit for bit in (0, 1, 3, 2, 4) if bit < count] + list(range(5, count))


def add_round(kernel, left, *rights):
    return pl.pallas_call(
        kernel,
        out_shape=sds(left.shape, BF),
        in_specs=[vmem()] * (1 + len(rights)),
        out_specs=vmem(),
        compiler_params=params(BIG),
        cost_estimate=cost(0, MIB),
        name="weight_add",
    )(left, *rights)


def per_device(feats, block_vals, block_cols, block_counts, send_list, w_self, w_neigh, bias, cotangent):
    node_count, chan_width = feats.shape
    block_rows, depth, size, _ = block_vals.shape
    parts = lax.axis_size("dom")
    chans = lax.axis_size("chan")
    slots = send_list.shape[2]
    f_in, f_out = w_self.shape
    nodes = node_count // chans
    rows = block_rows // chans
    table = block_rows + parts * slots
    chan = lax.axis_index("chan").astype(jnp.int32)
    part = lax.axis_index("dom").astype(jnp.int32)
    me = chan.reshape(1)
    send = send_list[0].T
    cols = block_cols.T
    feats_t = feats.T
    val_bytes = block_vals.size * 2
    vals = pltpu.with_memory_space_constraint(block_vals, pltpu.HBM)
    block_flops = 2 * block_rows * depth * size * size * chan_width
    layer_flops = 2 * f_in * f_out * nodes
    unit, lanes = 8, 128
    copies, streams = 8, 4

    outgoing = pl.pallas_call(
        pack_kernel,
        out_shape=pltpu.HBM((parts, slots, chan_width, size), BF),
        in_specs=[smem(), vmem()],
        out_specs=hbm(),
        scratch_shapes=[pltpu.VMEM((parts, slots, chan_width, size), BF), pltpu.SemaphoreType.DMA((copies,))],
        compiler_params=params(8),
        cost_estimate=cost(0, 5 * MIB),
        name="pack_outgoing",
    )(
        pltpu.with_memory_space_constraint(send, pltpu.HBM),
        pltpu.with_memory_space_constraint(feats_t, pltpu.HBM),
    )
    incoming = lax.all_to_all(outgoing, "dom", split_axis=0, concat_axis=0, tiled=True)

    feat_chunks = pl.pallas_call(
        split_kernel,
        out_shape=[pltpu.HBM((chan_width, nodes), BF)] * chans,
        in_specs=[smem(), vmem()],
        out_specs=[hbm()] * chans,
        scratch_shapes=[pltpu.SemaphoreType.DMA((chans,))],
        compiler_params=params(BIG),
        cost_estimate=cost(0, MIB),
        name="split_feats",
    )(me, feats_t)
    incoming, feat_chunks = lax.optimization_barrier((incoming, exchange(feat_chunks)))
    feat_chunks = [pltpu.with_memory_space_constraint(chunk, pltpu.HBM) for chunk in feat_chunks]
    feats_own, pre_self, neigh_turned, cot_turned = pl.pallas_call(
        functools.partial(self_kernel, chans),
        out_shape=[sds((f_in, nodes), BF), sds((f_out, nodes), F32), sds((f_out, f_in), BF), sds((f_out, nodes), BF)],
        in_specs=[smem()] + [vmem()] * (4 + chans),
        out_specs=[vmem()] * 4,
        compiler_params=params(BIG),
        cost_estimate=cost(layer_flops, 2 * MIB),
        name="self_part",
    )(me, w_self, bias.reshape(f_out, 1), w_neigh, cotangent, *feat_chunks)

    mean, degree = pl.pallas_call(
        gather_kernel,
        out_shape=[pltpu.HBM((chans, chan_width, nodes), BF), sds((chans, 8, nodes), F32)],
        in_specs=[smem(), smem()] + [vmem()] * 2 + [hbm()],
        out_specs=[hbm(), vmem()],
        scratch_shapes=[
            pltpu.VMEM(block_vals.shape, BF),
            pltpu.VMEM((chans, chan_width, nodes), BF),
            pltpu.SemaphoreType.DMA((streams,)),
            pltpu.SemaphoreType.DMA((streams,)),
        ],
        compiler_params=params(16),
        cost_estimate=cost(block_flops, val_bytes + 3 * MIB),
        name="neighbour_mean",
    )(cols, block_counts, feats_t, incoming.reshape(parts * slots, chan_width, size), vals)
    mean = lax.all_to_all(mean, "chan", split_axis=0, concat_axis=0, tiled=True).reshape(f_in, nodes)

    out_t, grad_t, scaled = pl.pallas_call(
        head_kernel,
        out_shape=[sds((f_out, nodes), BF), sds((f_out, nodes), BF), sds((f_in, nodes), BF)],
        in_specs=[smem()] + [vmem()] * 6,
        out_specs=[vmem()] * 3,
        compiler_params=params(BIG),
        cost_estimate=cost(2 * layer_flops, 4 * MIB),
        name="layer_head",
    )(me, degree, pre_self, neigh_turned, w_neigh, cot_turned, mean)
    scaled = lax.all_to_all(
        scaled.reshape(chans, chan_width, nodes), "chan", split_axis=0, concat_axis=0, tiled=True
    )

    order = halving_order(parts)
    halves, wholes = order[:3], order[3:]
    flips = [[(i, i ^ (1 << bit)) for i in range(parts)] for bit in order]
    bits = [((part >> bit) & 1).reshape(1) for bit in order]
    pieces = parts
    keep, give = pl.pallas_call(
        weight_partial_kernel,
        out_shape=[sds((pieces // 2, chans, unit, lanes), F32), sds((pieces // 2, chans, unit, lanes), BF)],
        in_specs=[smem()] + [vmem()] * 3,
        out_specs=[vmem()] * 2,
        scratch_shapes=[pltpu.VMEM((pieces, chans, unit, lanes), F32)],
        compiler_params=params(BIG),
        cost_estimate=cost(2 * layer_flops, 3 * MIB),
        name="weight_partial",
    )(bits[0], feats_own, mean, grad_t)
    pieces //= 2
    got = lax.ppermute(give, "dom", flips[0])
    quarter = (bits[1] << 1) | bits[2]
    pieces //= 4
    keep, *gives = pl.pallas_call(
        quarter_kernel,
        out_shape=[sds((pieces, chans, unit, lanes), F32)] + [sds((pieces, chans, unit, lanes), BF)] * 3,
        in_specs=[smem()] + [vmem()] * 2,
        out_specs=[vmem()] * 4,
        scratch_shapes=[pltpu.VMEM((pieces * 4, chans, unit, lanes), F32)],
        compiler_params=params(BIG),
        cost_estimate=cost(0, MIB),
        name="weight_quarter",
    )(quarter, keep, got)
    gots = []
    for flip, give in enumerate(gives, 1):
        away = (flip >> 1) << halves[1] | (flip & 1) << halves[2]
        gots.append(lax.ppermute(give, "dom", [(i, i ^ away) for i in range(parts)]))
    total = add_round(add_round_kernel, keep, *gots)
    side = pl.pallas_call(
        functools.partial(side_kernel, chans),
        out_shape=[sds((nodes, f_out), BF)] + [sds((chan_width, nodes), BF)] * chans,
        in_specs=[smem()] + [vmem()] * 3,
        out_specs=[vmem()] * (1 + chans),
        scratch_shapes=[pltpu.VMEM((f_in, nodes), BF)],
        compiler_params=params(BIG),
        cost_estimate=cost(layer_flops, 3 * MIB),
        name="side_grads",
    )(me, w_self, out_t, grad_t)
    for level in range(len(halves), len(order) - 1):
        got = lax.ppermute(total, "dom", flips[level])
        total = add_round(add_pair_kernel, total, got)
    scaled, total, side = lax.optimization_barrier((scaled, total, side))
    out_h = side[0]
    own_grad, far_grad = pl.pallas_call(
        scatter_kernel,
        out_shape=[
            pltpu.HBM((block_rows, chan_width, size), F32),
            pltpu.HBM((parts * slots, chan_width, size), BF),
        ],
        in_specs=[smem(), smem(), hbm(), vmem()],
        out_specs=[hbm(), hbm()],
        scratch_shapes=[
            pltpu.VMEM(block_vals.shape, BF),
            pltpu.VMEM((table, chan_width, size), F32),
            pltpu.VMEM((parts * slots, chan_width, size), BF),
            pltpu.SemaphoreType.DMA((streams,)),
            pltpu.SemaphoreType.DMA((copies,)),
            pltpu.SemaphoreType.DMA,
        ],
        compiler_params=params(24),
        cost_estimate=cost(block_flops, val_bytes + 4 * MIB),
        name="table_grad",
    )(cols, block_counts, vals, scaled)
    total, far_grad = lax.optimization_barrier((total, far_grad))
    back = lax.all_to_all(
        far_grad.reshape(parts, slots, chan_width, size), "dom", split_axis=0, concat_axis=0, tiled=True
    )

    packed = pl.pallas_call(
        functools.partial(message_kernel, chans),
        out_shape=[sds((chan_width, nodes + lanes), BF)] * chans,
        in_specs=[smem()] + [vmem()] * (1 + chans),
        out_specs=[vmem()] * chans,
        compiler_params=params(BIG),
        cost_estimate=cost(0, MIB),
        name="pack_messages",
    )(me, total, *side[1:])
    packed = exchange(packed)
    shifts = sorted(range(chans), key=lambda shift: -min(shift, chans - shift))
    packed = [packed[shift] for shift in shifts]
    held = pl.pallas_call(
        unit_kernel,
        out_shape=sds((pieces * unit, lanes), BF),
        in_specs=[vmem()] * chans,
        out_specs=vmem(),
        compiler_params=params(BIG),
        cost_estimate=cost(0, MIB),
        name="weight_sum",
    )(*packed).reshape(1, pieces * unit, lanes)
    near = pl.pallas_call(
        functools.partial(near_kernel, shifts),
        out_shape=sds((block_rows, chan_width, size), F32),
        in_specs=[smem()] + [vmem()] * (1 + chans),
        out_specs=vmem(),
        compiler_params=params(BIG),
        cost_estimate=cost(0, 3 * MIB),
        name="sum_near",
    )(me, own_grad, *packed)
    whole, half = 1 << order[-1], 1 << halves[-1]
    across, beside, both = (
        lax.ppermute(held, "dom", [(i, i ^ flip) for i in range(parts)]) for flip in (whole, half, whole | half)
    )
    mine = held.astype(F32) + across.astype(F32)
    other = beside.astype(F32) + both.astype(F32)
    held = jnp.concatenate([mine, other], axis=0).astype(BF)
    held, back, near = lax.optimization_barrier((held, back, near))
    grad_feats = pl.pallas_call(
        final_kernel,
        out_shape=sds((chan_width, node_count), BF),
        in_specs=[smem()] + [vmem()] * 2,
        out_specs=vmem(),
        scratch_shapes=[pltpu.VMEM((block_rows, chan_width, size), F32)],
        compiler_params=params(BIG),
        cost_estimate=cost(0, 4 * MIB),
        name="sum_returned",
    )(send, near, back)
    for level in reversed(range(len(halves) - 1)):
        held = jnp.concatenate([held, lax.ppermute(held, "dom", flips[level])], axis=0)
        if level == len(halves) - 2:
            held, grad_feats = lax.optimization_barrier((held, grad_feats))
    address = jnp.int32(0)
    for level in range(len(halves)):
        address = address * 2 + bits[level][0]
    grad_w_self, grad_w_neigh = pl.pallas_call(
        functools.partial(spread_kernel, float(node_count * parts) ** (-0.5)),
        out_shape=[sds((chan_width, f_out), F32)] * 2,
        in_specs=[smem(), vmem()],
        out_specs=[vmem()] * 2,
        compiler_params=params(BIG),
        cost_estimate=cost(0, MIB),
        name="weight_spread",
    )(address.reshape(1), held)

    return (out_h, grad_feats.T, grad_w_self, grad_w_neigh)


def solution(mesh):
    return jax.shard_map(
        per_device,
        mesh=mesh,
        in_specs=(
            P("dom", "chan"),
            P("dom", None, None, None),
            P("dom", None),
            P("dom"),
            P("dom", None, None),
            P(),
            P(),
            P(),
            P(("dom", "chan"), None),
        ),
        out_specs=(P(("dom", "chan"), None), P("dom", "chan"), P("chan", None), P("chan", None)),
        check_vma=False,
    )
```

```python
import functools

import jax
import jax.numpy as jnp
from jax import lax
from jax.experimental import pallas as pl
from jax.experimental.pallas import tpu as pltpu
from jax.sharding import PartitionSpec as P

BF = jnp.bfloat16
F32 = jnp.float32
MIB = 1 << 20
BIG = 8


def vmem():
    return pl.BlockSpec(memory_space=pltpu.VMEM)


def hbm():
    return pl.BlockSpec(memory_space=pltpu.HBM)


def smem():
    return pl.BlockSpec(memory_space=pltpu.SMEM)


def params(mib):
    return pltpu.CompilerParams(vmem_limit_bytes=mib * MIB)


def cost(flops, nbytes):
    return pl.CostEstimate(flops=flops, bytes_accessed=nbytes, transcendentals=0)


def nt_dot(left, right):
    return lax.dot_general(left, right, (((1,), (1,)), ((), ())), preferred_element_type=F32)


def nn_dot(left, right):
    return lax.dot_general(left, right, (((1,), (0,)), ((), ())), preferred_element_type=F32)


def pack_kernel(send_ref, feats_ref, out_ref, hold_ref, sems):
    dests, slots, _, size = hold_ref.shape
    copies = sems.shape[0]
    span = dests // copies
    for copy in range(copies):
        for dest in range(copy * span, (copy + 1) * span):
            for slot in range(slots):
                lane = pl.multiple_of(send_ref[slot, dest] * size, size)
                hold_ref[dest, slot] = feats_ref[:, pl.ds(lane, size)]
        place = pl.ds(copy * span, span)
        pltpu.make_async_copy(hold_ref.at[place], out_ref.at[place], sems.at[copy]).start()
    for copy in range(copies):
        place = pl.ds(copy * span, span)
        pltpu.make_async_copy(hold_ref.at[place], out_ref.at[place], sems.at[copy]).wait()


def split_kernel(me_ref, feats_ref, *refs):
    out_refs, sems = refs[:-1], refs[-1]
    chans = len(out_refs)
    width = out_refs[0].shape[1]

    def copy(shift):
        lane = pl.multiple_of(lax.rem(me_ref[0] + shift, chans) * width, width)
        return pltpu.make_async_copy(feats_ref.at[:, pl.ds(lane, width)], out_refs[shift], sems.at[shift])

    for shift in range(chans):
        copy(shift).start()
    for shift in range(chans):
        copy(shift).wait()


def join_slots(vals_ref, row):
    return jnp.concatenate([vals_ref[row, k] for k in range(vals_ref.shape[1])], axis=1)


def stream_rows(vals_ref, held_ref, sems, body, before=None, after=None):
    total = held_ref.shape[0]
    small = total // 8
    large = 2 * small

    def copy(start, span, place):
        rows = pl.ds(start, span)
        return pltpu.make_async_copy(vals_ref.at[rows], held_ref.at[rows], sems.at[place])

    heads = [(place * small, small, place) for place in range(2)]
    tails = total // large - 1
    for start, span, place in heads:
        copy(start, span, place).start()
    for place in range(tails):
        copy((place + 1) * large, large, place + 2).start()
    if before is not None:
        before()

    def work(start, span, place):
        copy(start, span, place).wait()
        for row in range(span):
            body(start + row)
        if after is not None:
            after(start, span, place)

    for start, span, place in heads:
        work(jnp.int32(start), span, place)

    def one(place, carry):
        work((place + 1) * large, large, place + 2)
        return carry

    lax.fori_loop(0, tails, one, 0)


def gather_kernel(
    cols_ref, counts_ref, feats_ref, recv_ref, vals_ref, out_ref, degree_ref, held_ref, mean_ref, sems, out_sems
):
    _, depth, size, _ = vals_ref.shape
    width = feats_ref.shape[0]
    rows = out_ref.shape[2] // size
    own = feats_ref.shape[1] // size
    ones = jnp.ones((16, size), BF)

    def body(index):
        count = counts_ref[index]
        picked = []
        for k in range(depth):
            col = cols_ref[k, index]
            lane = pl.multiple_of(jnp.minimum(col, own - 1) * size, size)
            near = feats_ref[:, pl.ds(lane, size)]
            far = recv_ref[jnp.maximum(col - own, 0)]
            block = jnp.concatenate([jnp.where(col < own, near, far), ones], axis=0)
            picked.append(jnp.where(k < count, block, jnp.zeros_like(block)))
        total = nt_dot(join_slots(held_ref, index), jnp.concatenate(picked, axis=1)).T
        group = index // rows
        place = pl.ds(pl.multiple_of(lax.rem(index, rows) * size, size), size)
        degree_ref[group, :, place] = total[width : width + 8]
        mean_ref[group, :, place] = (total[:width] / total[width : width + 1]).astype(BF)

    def copy(start, span, place):
        groups = pl.ds(start // rows, span // rows)
        return pltpu.make_async_copy(mean_ref.at[groups], out_ref.at[groups], out_sems.at[place])

    stream_rows(vals_ref, held_ref, sems, body, after=lambda *which: copy(*which).start())
    small = held_ref.shape[0] // 8
    copy(0, small, 0).wait()
    copy(small, small, 1).wait()
    for place in range(2, out_sems.shape[0]):
        copy((place - 1) * 2 * small, 2 * small, place).wait()


def self_kernel(chans, me_ref, weight_ref, bias_ref, neigh_ref, cot_ref, *refs):
    chunk_refs = refs[:chans]
    full_ref, pre_ref, neigh_turned_ref, cot_turned_ref = refs[chans:]
    neigh_turned_ref[...] = neigh_ref[...].T
    cot_turned_ref[...] = cot_ref[...].T
    height = chunk_refs[0].shape[0]
    for shift, chunk_ref in enumerate(chunk_refs):
        start = pl.multiple_of(lax.rem(me_ref[0] + (chans - shift), chans) * height, height)
        full_ref[pl.ds(start, height), :] = chunk_ref[...]
    pre_ref[...] = nn_dot(weight_ref[...].T, full_ref[...]) + bias_ref[...]


def head_kernel(me_ref, degree_ref, pre_ref, turned_ref, weight_ref, cot_ref, mean_ref, out_ref, grad_ref, scaled_ref):
    preact = pre_ref[...] + nn_dot(turned_ref[...], mean_ref[...])
    logistic = jax.nn.sigmoid(preact)
    activated = preact * logistic
    slope = logistic * (1.0 + preact * (1.0 - logistic))
    inverse = 1.0 / jnp.sqrt(jnp.mean(activated * activated, axis=0, keepdims=True) + 1e-06)
    unit = activated * inverse
    cot = cot_ref[...].astype(F32)
    grad_act = (cot - unit * jnp.mean(cot * unit, axis=0, keepdims=True)) * inverse
    grad = (grad_act * slope).astype(BF)
    out_ref[...] = unit.astype(BF)
    grad_ref[...] = grad
    mean_grad = nn_dot(weight_ref[...], grad).astype(BF).astype(F32)
    degree = degree_ref[me_ref[0], 0:1, :]
    scaled_ref[...] = (mean_grad / degree).astype(BF)


def weight_partial_kernel(me_ref, feats_ref, mean_ref, grad_ref, keep_ref, give_ref, hold_ref):
    parts, chans, unit, lanes = hold_ref.shape
    grad = grad_ref[...]
    totals = [nt_dot(feats_ref[...], grad), nt_dot(mean_ref[...], grad)]
    width = totals[0].shape[0] // chans
    halves = totals[0].shape[1] // lanes
    count = width // unit
    for which, total in enumerate(totals):
        for half in range(halves):
            place = (which * halves + half) * count
            for chan in range(chans):
                piece = total[chan * width : (chan + 1) * width, half * lanes : (half + 1) * lanes]
                hold_ref[place : place + count, chan] = piece.reshape(count, unit, lanes)
    half = parts // 2
    bit = me_ref[0]
    keep_ref[...] = hold_ref[pl.ds(bit * half, half)]
    give_ref[...] = hold_ref[pl.ds((1 - bit) * half, half)].astype(BF)


def quarter_kernel(me_ref, held_ref, recv_ref, keep_ref, *refs):
    give_refs, hold_ref = refs[:-1], refs[-1]
    span = keep_ref.shape[0]
    hold_ref[...] = held_ref[...] + recv_ref[...].astype(F32)
    keep_ref[...] = hold_ref[pl.ds(me_ref[0] * span, span)]
    for flip, give_ref in enumerate(give_refs, 1):
        give_ref[...] = hold_ref[pl.ds(lax.bitwise_xor(me_ref[0], flip) * span, span)].astype(BF)


def add_round_kernel(held_ref, *refs):
    total = held_ref[...]
    for recv_ref in refs[:-1]:
        total = total + recv_ref[...].astype(F32)
    refs[-1][...] = total.astype(BF)


def add_pair_kernel(held_ref, recv_ref, out_ref):
    out_ref[...] = (held_ref[...].astype(F32) + recv_ref[...].astype(F32)).astype(BF)


def side_kernel(chans, me_ref, weight_ref, out_ref, grad_ref, turned_ref, *refs):
    self_refs = refs[:chans]
    (hold_ref,) = refs[chans:]
    turned_ref[...] = out_ref[...].T
    hold_ref[...] = nn_dot(weight_ref[...], grad_ref[...]).astype(BF)
    height = self_refs[0].shape[0]
    for shift, self_ref in enumerate(self_refs):
        start = pl.multiple_of(lax.rem(me_ref[0] + shift, chans) * height, height)
        self_ref[...] = hold_ref[pl.ds(start, height), :]


def message_kernel(chans, me_ref, unit_ref, *refs):
    self_refs = refs[:chans]
    packed_refs = refs[chans:]
    nodes = self_refs[0].shape[1]
    units, _, unit, lanes = unit_ref.shape
    for shift, packed_ref in enumerate(packed_refs):
        dest = lax.rem(me_ref[0] + shift, chans)
        piece = unit_ref[:, dest].astype(F32).reshape(units * unit, lanes)
        packed_ref[:, :nodes] = self_refs[shift][...]
        packed_ref[: units * unit, nodes:] = piece.astype(BF)
        packed_ref[units * unit :, nodes:] = jnp.zeros_like(packed_ref[units * unit :, nodes:])


def scatter_kernel(
    cols_ref, counts_ref, vals_ref, scaled_ref, own_ref, far_ref, held_ref, hold_ref, send_ref, val_sems, sems, own_sem
):
    _, depth, size, _ = vals_ref.shape
    rows = scaled_ref.shape[2] // size
    own = own_ref.shape[0]

    def clear():
        hold_ref[...] = jnp.zeros_like(hold_ref)

    def body(index):
        count = counts_ref[index]
        place = pl.ds(pl.multiple_of(lax.rem(index, rows) * size, size), size)
        total = nn_dot(scaled_ref[index // rows, :, place], join_slots(held_ref, index))
        for k in range(depth):
            part = total[:, k * size : (k + 1) * size]
            hold_ref[cols_ref[k, index]] += jnp.where(k < count, part, jnp.zeros_like(part))

    stream_rows(vals_ref, held_ref, val_sems, body, clear)
    copies = sems.shape[0]
    span = far_ref.shape[0] // copies
    for copy in range(copies):
        send_ref[copy * span : (copy + 1) * span] = hold_ref[own + copy * span : own + (copy + 1) * span].astype(BF)
        place = pl.ds(copy * span, span)
        pltpu.make_async_copy(send_ref.at[place], far_ref.at[place], sems.at[copy]).start()
    pltpu.make_async_copy(hold_ref.at[pl.ds(0, own)], own_ref, own_sem).start()
    for copy in range(copies):
        place = pl.ds(copy * span, span)
        pltpu.make_async_copy(send_ref.at[place], far_ref.at[place], sems.at[copy]).wait()
    pltpu.make_async_copy(hold_ref.at[pl.ds(0, own)], own_ref, own_sem).wait()


def unit_kernel(*refs):
    packed_refs = refs[:-1]
    out_ref = refs[-1]
    rows, lanes = out_ref.shape
    total = packed_refs[0][:rows, -lanes:].astype(F32)
    for packed_ref in packed_refs[1:]:
        total = total + packed_ref[:rows, -lanes:].astype(F32)
    out_ref[...] = total.astype(BF)


def spread_kernel(scale, me_ref, held_ref, self_ref, neigh_ref):
    pieces, rows, lanes = held_ref.shape
    half = pieces // 2
    unit_rows = self_ref.shape[0]
    per = unit_rows // rows
    for place in range(pieces):
        away = lax.bitwise_xor(me_ref[0], place)
        first, second, third = away // 4, lax.rem(away // 2, 2), lax.rem(away, 2)
        value = held_ref[second * 4 + third * 2 + first].astype(F32) * scale
        target = self_ref if place < half else neigh_ref
        inside = place % half
        column, row = inside // per, inside % per
        target[row * rows : (row + 1) * rows, column * lanes : (column + 1) * lanes] = value


def near_kernel(shifts, me_ref, own_ref, *refs):
    chans = len(shifts)
    packed_refs = refs[:chans]
    (out_ref,) = refs[chans:]
    blocks, _, size = out_ref.shape
    rows = blocks // chans
    for shift, packed_ref in zip(shifts, packed_refs):
        group = lax.rem(me_ref[0] + (chans - shift), chans)
        for row in range(rows):
            index = group * rows + row
            out_ref[index] = own_ref[index] + packed_ref[:, row * size : (row + 1) * size].astype(F32)


def final_kernel(send_ref, near_ref, back_ref, out_ref, hold_ref):
    slots, dests = send_ref.shape
    blocks, _, size = hold_ref.shape
    hold_ref[...] = near_ref[...]

    def one(dest, carry):
        for slot in range(slots):
            hold_ref[send_ref[slot, dest]] += back_ref[dest, slot].astype(F32)
        return carry

    lax.fori_loop(0, dests, one, 0, unroll=8)
    for block in range(blocks):
        out_ref[:, block * size : (block + 1) * size] = hold_ref[block].astype(BF)


def exchange(chunks):
    count = len(chunks)
    received = list(chunks)
    for shift in range(1, count):
        received[shift] = lax.ppermute(chunks[shift], "chan", [(i, (i + shift) % count) for i in range(count)])
    return received


def sds(shape, dtype):
    return jax.ShapeDtypeStruct(shape, dtype)


def halving_order(parts):
    count = parts.bit_length() - 1
    return [bit for bit in (0, 1, 3, 2, 4) if bit < count] + list(range(5, count))


def add_round(kernel, left, *rights):
    return pl.pallas_call(
        kernel,
        out_shape=sds(left.shape, BF),
        in_specs=[vmem()] * (1 + len(rights)),
        out_specs=vmem(),
        compiler_params=params(BIG),
        cost_estimate=cost(0, MIB),
        name="weight_add",
    )(left, *rights)


def per_device(feats, block_vals, block_cols, block_counts, send_list, w_self, w_neigh, bias, cotangent):
    node_count, chan_width = feats.shape
    block_rows, depth, size, _ = block_vals.shape
    parts = lax.axis_size("dom")
    chans = lax.axis_size("chan")
    slots = send_list.shape[2]
    f_in, f_out = w_self.shape
    nodes = node_count // chans
    rows = block_rows // chans
    table = block_rows + parts * slots
    chan = lax.axis_index("chan").astype(jnp.int32)
    part = lax.axis_index("dom").astype(jnp.int32)
    me = chan.reshape(1)
    send = send_list[0].T
    cols = block_cols.T
    feats_t = feats.T
    val_bytes = block_vals.size * 2
    vals = pltpu.with_memory_space_constraint(block_vals, pltpu.HBM)
    block_flops = 2 * block_rows * depth * size * size * chan_width
    layer_flops = 2 * f_in * f_out * nodes
    unit, lanes = 8, 128
    copies, streams = 8, 5

    outgoing = pl.pallas_call(
        pack_kernel,
        out_shape=pltpu.HBM((parts, slots, chan_width, size), BF),
        in_specs=[smem(), vmem()],
        out_specs=hbm(),
        scratch_shapes=[pltpu.VMEM((parts, slots, chan_width, size), BF), pltpu.SemaphoreType.DMA((copies,))],
        compiler_params=params(8),
        cost_estimate=cost(0, 5 * MIB),
        name="pack_outgoing",
    )(
        pltpu.with_memory_space_constraint(send, pltpu.HBM),
        pltpu.with_memory_space_constraint(feats_t, pltpu.HBM),
    )
    incoming = lax.all_to_all(outgoing, "dom", split_axis=0, concat_axis=0, tiled=True)

    feat_chunks = pl.pallas_call(
        split_kernel,
        out_shape=[pltpu.HBM((chan_width, nodes), BF)] * chans,
        in_specs=[smem(), vmem()],
        out_specs=[hbm()] * chans,
        scratch_shapes=[pltpu.SemaphoreType.DMA((chans,))],
        compiler_params=params(BIG),
        cost_estimate=cost(0, MIB),
        name="split_feats",
    )(me, feats_t)
    incoming, feat_chunks = lax.optimization_barrier((incoming, exchange(feat_chunks)))
    feat_chunks = [pltpu.with_memory_space_constraint(chunk, pltpu.HBM) for chunk in feat_chunks]
    feats_own, pre_self, neigh_turned, cot_turned = pl.pallas_call(
        functools.partial(self_kernel, chans),
        out_shape=[sds((f_in, nodes), BF), sds((f_out, nodes), F32), sds((f_out, f_in), BF), sds((f_out, nodes), BF)],
        in_specs=[smem()] + [vmem()] * (4 + chans),
        out_specs=[vmem()] * 4,
        compiler_params=params(BIG),
        cost_estimate=cost(layer_flops, 2 * MIB),
        name="self_part",
    )(me, w_self, bias.reshape(f_out, 1), w_neigh, cotangent, *feat_chunks)

    mean, degree = pl.pallas_call(
        gather_kernel,
        out_shape=[pltpu.HBM((chans, chan_width, nodes), BF), sds((chans, 8, nodes), F32)],
        in_specs=[smem(), smem()] + [vmem()] * 2 + [hbm()],
        out_specs=[hbm(), vmem()],
        scratch_shapes=[
            pltpu.VMEM(block_vals.shape, BF),
            pltpu.VMEM((chans, chan_width, nodes), BF),
            pltpu.SemaphoreType.DMA((streams,)),
            pltpu.SemaphoreType.DMA((streams,)),
        ],
        compiler_params=params(16),
        cost_estimate=cost(block_flops, val_bytes + 3 * MIB),
        name="neighbour_mean",
    )(cols, block_counts, feats_t, incoming.reshape(parts * slots, chan_width, size), vals)
    mean = lax.all_to_all(mean, "chan", split_axis=0, concat_axis=0, tiled=True).reshape(f_in, nodes)

    out_t, grad_t, scaled = pl.pallas_call(
        head_kernel,
        out_shape=[sds((f_out, nodes), BF), sds((f_out, nodes), BF), sds((f_in, nodes), BF)],
        in_specs=[smem()] + [vmem()] * 6,
        out_specs=[vmem()] * 3,
        compiler_params=params(BIG),
        cost_estimate=cost(2 * layer_flops, 4 * MIB),
        name="layer_head",
    )(me, degree, pre_self, neigh_turned, w_neigh, cot_turned, mean)
    scaled = lax.all_to_all(
        scaled.reshape(chans, chan_width, nodes), "chan", split_axis=0, concat_axis=0, tiled=True
    )

    order = halving_order(parts)
    halves, wholes = order[:3], order[3:]
    flips = [[(i, i ^ (1 << bit)) for i in range(parts)] for bit in order]
    bits = [((part >> bit) & 1).reshape(1) for bit in order]
    pieces = parts
    keep, give = pl.pallas_call(
        weight_partial_kernel,
        out_shape=[sds((pieces // 2, chans, unit, lanes), F32), sds((pieces // 2, chans, unit, lanes), BF)],
        in_specs=[smem()] + [vmem()] * 3,
        out_specs=[vmem()] * 2,
        scratch_shapes=[pltpu.VMEM((pieces, chans, unit, lanes), F32)],
        compiler_params=params(BIG),
        cost_estimate=cost(2 * layer_flops, 3 * MIB),
        name="weight_partial",
    )(bits[0], feats_own, mean, grad_t)
    pieces //= 2
    got = lax.ppermute(give, "dom", flips[0])
    quarter = (bits[1] << 1) | bits[2]
    pieces //= 4
    keep, *gives = pl.pallas_call(
        quarter_kernel,
        out_shape=[sds((pieces, chans, unit, lanes), F32)] + [sds((pieces, chans, unit, lanes), BF)] * 3,
        in_specs=[smem()] + [vmem()] * 2,
        out_specs=[vmem()] * 4,
        scratch_shapes=[pltpu.VMEM((pieces * 4, chans, unit, lanes), F32)],
        compiler_params=params(BIG),
        cost_estimate=cost(0, MIB),
        name="weight_quarter",
    )(quarter, keep, got)
    gots = []
    for flip, give in enumerate(gives, 1):
        away = (flip >> 1) << halves[1] | (flip & 1) << halves[2]
        gots.append(lax.ppermute(give, "dom", [(i, i ^ away) for i in range(parts)]))
    total = add_round(add_round_kernel, keep, *gots)
    side = pl.pallas_call(
        functools.partial(side_kernel, chans),
        out_shape=[sds((nodes, f_out), BF)] + [sds((chan_width, nodes), BF)] * chans,
        in_specs=[smem()] + [vmem()] * 3,
        out_specs=[vmem()] * (1 + chans),
        scratch_shapes=[pltpu.VMEM((f_in, nodes), BF)],
        compiler_params=params(BIG),
        cost_estimate=cost(layer_flops, 3 * MIB),
        name="side_grads",
    )(me, w_self, out_t, grad_t)
    for level in range(len(halves), len(order) - 1):
        got = lax.ppermute(total, "dom", flips[level])
        total = add_round(add_pair_kernel, total, got)
    scaled, total, side = lax.optimization_barrier((scaled, total, side))
    out_h = side[0]
    own_grad, far_grad = pl.pallas_call(
        scatter_kernel,
        out_shape=[
            pltpu.HBM((block_rows, chan_width, size), F32),
            pltpu.HBM((parts * slots, chan_width, size), BF),
        ],
        in_specs=[smem(), smem(), hbm(), vmem()],
        out_specs=[hbm(), hbm()],
        scratch_shapes=[
            pltpu.VMEM(block_vals.shape, BF),
            pltpu.VMEM((table, chan_width, size), F32),
            pltpu.VMEM((parts * slots, chan_width, size), BF),
            pltpu.SemaphoreType.DMA((streams,)),
            pltpu.SemaphoreType.DMA((copies,)),
            pltpu.SemaphoreType.DMA,
        ],
        compiler_params=params(24),
        cost_estimate=cost(block_flops, val_bytes + 4 * MIB),
        name="table_grad",
    )(cols, block_counts, vals, scaled)
    total, far_grad = lax.optimization_barrier((total, far_grad))
    back = lax.all_to_all(
        far_grad.reshape(parts, slots, chan_width, size), "dom", split_axis=0, concat_axis=0, tiled=True
    )

    packed = pl.pallas_call(
        functools.partial(message_kernel, chans),
        out_shape=[sds((chan_width, nodes + lanes), BF)] * chans,
        in_specs=[smem()] + [vmem()] * (1 + chans),
        out_specs=[vmem()] * chans,
        compiler_params=params(BIG),
        cost_estimate=cost(0, MIB),
        name="pack_messages",
    )(me, total, *side[1:])
    packed = exchange(packed)
    shifts = sorted(range(chans), key=lambda shift: -min(shift, chans - shift))
    packed = [packed[shift] for shift in shifts]
    held = pl.pallas_call(
        unit_kernel,
        out_shape=sds((pieces * unit, lanes), BF),
        in_specs=[vmem()] * chans,
        out_specs=vmem(),
        compiler_params=params(BIG),
        cost_estimate=cost(0, MIB),
        name="weight_sum",
    )(*packed).reshape(1, pieces * unit, lanes)
    near = pl.pallas_call(
        functools.partial(near_kernel, shifts),
        out_shape=sds((block_rows, chan_width, size), F32),
        in_specs=[smem()] + [vmem()] * (1 + chans),
        out_specs=vmem(),
        compiler_params=params(BIG),
        cost_estimate=cost(0, 3 * MIB),
        name="sum_near",
    )(me, own_grad, *packed)
    held = jnp.concatenate([held, lax.ppermute(held, "dom", flips[0])], axis=0)
    whole, half = 1 << order[-1], 1 << halves[-1]
    across, beside, both = (
        lax.ppermute(held, "dom", [(i, i ^ flip) for i in range(parts)]) for flip in (whole, half, whole | half)
    )
    mine = held.astype(F32) + across.astype(F32)
    other = beside.astype(F32) + both.astype(F32)
    held = jnp.concatenate([mine, other], axis=0).astype(BF)
    held, back, near = lax.optimization_barrier((held.reshape(4, pieces * unit, lanes), back, near))
    grad_feats = pl.pallas_call(
        final_kernel,
        out_shape=sds((chan_width, node_count), BF),
        in_specs=[smem()] + [vmem()] * 2,
        out_specs=vmem(),
        scratch_shapes=[pltpu.VMEM((block_rows, chan_width, size), F32)],
        compiler_params=params(BIG),
        cost_estimate=cost(0, 4 * MIB),
        name="sum_returned",
    )(send, near, back)
    held = jnp.concatenate([held, lax.ppermute(held, "dom", flips[1])], axis=0)
    address = jnp.int32(0)
    for level in range(len(halves)):
        address = address * 2 + bits[level][0]
    grad_w_self, grad_w_neigh = pl.pallas_call(
        functools.partial(spread_kernel, float(node_count * parts) ** (-0.5)),
        out_shape=[sds((chan_width, f_out), F32)] * 2,
        in_specs=[smem(), vmem()],
        out_specs=[vmem()] * 2,
        compiler_params=params(BIG),
        cost_estimate=cost(0, MIB),
        name="weight_spread",
    )(address.reshape(1), held)

    return (out_h, grad_feats.T, grad_w_self, grad_w_neigh)


def solution(mesh):
    return jax.shard_map(
        per_device,
        mesh=mesh,
        in_specs=(
            P("dom", "chan"),
            P("dom", None, None, None),
            P("dom", None),
            P("dom"),
            P("dom", None, None),
            P(),
            P(),
            P(),
            P(("dom", "chan"), None),
        ),
        out_specs=(P(("dom", "chan"), None), P("dom", "chan"), P("chan", None), P("chan", None)),
        check_vma=False,
    )
```

```python
import functools

import jax
import jax.numpy as jnp
from jax import lax
from jax.experimental import pallas as pl
from jax.experimental.pallas import tpu as pltpu
from jax.sharding import PartitionSpec as P

BF = jnp.bfloat16
F32 = jnp.float32
MIB = 1 << 20
BIG = 8


def vmem():
    return pl.BlockSpec(memory_space=pltpu.VMEM)


def hbm():
    return pl.BlockSpec(memory_space=pltpu.HBM)


def smem():
    return pl.BlockSpec(memory_space=pltpu.SMEM)


def params(mib):
    return pltpu.CompilerParams(vmem_limit_bytes=mib * MIB)


def cost(flops, nbytes):
    return pl.CostEstimate(flops=flops, bytes_accessed=nbytes, transcendentals=0)


def nt_dot(left, right):
    return lax.dot_general(left, right, (((1,), (1,)), ((), ())), preferred_element_type=F32)


def nn_dot(left, right):
    return lax.dot_general(left, right, (((1,), (0,)), ((), ())), preferred_element_type=F32)


def pack_kernel(send_ref, feats_ref, out_ref, hold_ref, sems):
    dests, slots, _, size = hold_ref.shape
    copies = sems.shape[0]
    span = dests // copies
    for copy in range(copies):
        for dest in range(copy * span, (copy + 1) * span):
            for slot in range(slots):
                lane = pl.multiple_of(send_ref[slot, dest] * size, size)
                hold_ref[dest, slot] = feats_ref[:, pl.ds(lane, size)]
        place = pl.ds(copy * span, span)
        pltpu.make_async_copy(hold_ref.at[place], out_ref.at[place], sems.at[copy]).start()
    for copy in range(copies):
        place = pl.ds(copy * span, span)
        pltpu.make_async_copy(hold_ref.at[place], out_ref.at[place], sems.at[copy]).wait()


def split_kernel(me_ref, feats_ref, *refs):
    out_refs, sems = refs[:-1], refs[-1]
    chans = len(out_refs)
    width = out_refs[0].shape[1]

    def copy(shift):
        lane = pl.multiple_of(lax.rem(me_ref[0] + shift, chans) * width, width)
        return pltpu.make_async_copy(feats_ref.at[:, pl.ds(lane, width)], out_refs[shift], sems.at[shift])

    for shift in range(chans):
        copy(shift).start()
    for shift in range(chans):
        copy(shift).wait()


def join_slots(vals_ref, row):
    return jnp.concatenate([vals_ref[row, k] for k in range(vals_ref.shape[1])], axis=1)


def stream_rows(vals_ref, held_ref, sems, body, before=None, after=None):
    total = held_ref.shape[0]
    small = total // 8
    large = 2 * small

    def copy(start, span, place):
        rows = pl.ds(start, span)
        return pltpu.make_async_copy(vals_ref.at[rows], held_ref.at[rows], sems.at[place])

    heads = [(place * small, small, place) for place in range(2)]
    tails = total // large - 1
    for start, span, place in heads:
        copy(start, span, place).start()
    for place in range(tails):
        copy((place + 1) * large, large, place + 2).start()
    if before is not None:
        before()

    def work(start, span, place):
        copy(start, span, place).wait()
        for row in range(span):
            body(start + row)
        if after is not None:
            after(start, span, place)

    for start, span, place in heads:
        work(jnp.int32(start), span, place)

    def one(place, carry):
        work((place + 1) * large, large, place + 2)
        return carry

    lax.fori_loop(0, tails, one, 0)


def gather_kernel(shifts, chans, me_ref, cols_ref, counts_ref, feats_ref, recv_ref, vals_ref, *refs):
    out_refs = refs[: len(shifts)]
    degree_ref, held_ref, mean_ref, sems, out_sems = refs[len(shifts) :]
    _, rows, depth, size, _ = held_ref.shape
    width = feats_ref.shape[0]
    own = feats_ref.shape[1] // size
    ones = jnp.ones((16, size), BF)
    groups = [lax.rem(me_ref[0] + shift, chans) for shift in shifts]

    def load(place):
        return pltpu.make_async_copy(
            vals_ref.at[pl.ds(groups[place] * rows, rows)], held_ref.at[place], sems.at[place]
        )

    def store(place):
        return pltpu.make_async_copy(mean_ref.at[place], out_refs[place], out_sems.at[place])

    for place in range(len(shifts)):
        load(place).start()
    for place in range(len(shifts)):
        load(place).wait()
        for row in range(rows):
            index = groups[place] * rows + row
            count = counts_ref[index]
            picked = []
            for k in range(depth):
                col = cols_ref[k, index]
                lane = pl.multiple_of(jnp.minimum(col, own - 1) * size, size)
                near = feats_ref[:, pl.ds(lane, size)]
                far = recv_ref[jnp.maximum(col - own, 0)]
                block = jnp.concatenate([jnp.where(col < own, near, far), ones], axis=0)
                picked.append(jnp.where(k < count, block, jnp.zeros_like(block)))
            total = nt_dot(join_slots(held_ref.at[place], row), jnp.concatenate(picked, axis=1)).T
            lanes = slice(row * size, (row + 1) * size)
            mean_ref[place, :, lanes] = (total[:width] / total[width : width + 1]).astype(BF)
            if place == len(shifts) - 1:
                degree_ref[:, lanes] = total[width : width + 8]
        store(place).start()
    for place in range(len(shifts)):
        store(place).wait()


def self_kernel(chans, me_ref, weight_ref, bias_ref, neigh_ref, cot_ref, *refs):
    chunk_refs = refs[:chans]
    full_ref, pre_ref, neigh_turned_ref, cot_turned_ref = refs[chans:]
    neigh_turned_ref[...] = neigh_ref[...].T
    cot_turned_ref[...] = cot_ref[...].T
    height = chunk_refs[0].shape[0]
    for shift, chunk_ref in enumerate(chunk_refs):
        start = pl.multiple_of(lax.rem(me_ref[0] + (chans - shift), chans) * height, height)
        full_ref[pl.ds(start, height), :] = chunk_ref[...]
    pre_ref[...] = nn_dot(weight_ref[...].T, full_ref[...]) + bias_ref[...]


def head_kernel(shifts, me_ref, degree_ref, pre_ref, turned_ref, weight_ref, cot_ref, *refs):
    chans = len(shifts)
    chunk_refs = refs[:chans]
    mean_ref, out_ref, grad_ref, scaled_ref = refs[chans:]
    height = chunk_refs[0].shape[0]
    for shift, chunk_ref in zip(shifts, chunk_refs):
        start = pl.multiple_of(lax.rem(me_ref[0] + (chans - shift), chans) * height, height)
        mean_ref[pl.ds(start, height), :] = chunk_ref[...]
    preact = pre_ref[...] + nn_dot(turned_ref[...], mean_ref[...])
    logistic = jax.nn.sigmoid(preact)
    activated = preact * logistic
    slope = logistic * (1.0 + preact * (1.0 - logistic))
    inverse = 1.0 / jnp.sqrt(jnp.mean(activated * activated, axis=0, keepdims=True) + 1e-06)
    unit = activated * inverse
    cot = cot_ref[...].astype(F32)
    grad_act = (cot - unit * jnp.mean(cot * unit, axis=0, keepdims=True)) * inverse
    grad = (grad_act * slope).astype(BF)
    out_ref[...] = unit.astype(BF)
    grad_ref[...] = grad
    mean_grad = nn_dot(weight_ref[...], grad).astype(BF).astype(F32)
    degree = degree_ref[0:1, :]
    scaled_ref[...] = (mean_grad / degree).astype(BF)


def weight_partial_kernel(me_ref, feats_ref, mean_ref, grad_ref, keep_ref, give_ref, hold_ref):
    parts, chans, unit, lanes = hold_ref.shape
    grad = grad_ref[...]
    totals = [nt_dot(feats_ref[...], grad), nt_dot(mean_ref[...], grad)]
    width = totals[0].shape[0] // chans
    halves = totals[0].shape[1] // lanes
    count = width // unit
    for which, total in enumerate(totals):
        for half in range(halves):
            place = (which * halves + half) * count
            for chan in range(chans):
                piece = total[chan * width : (chan + 1) * width, half * lanes : (half + 1) * lanes]
                hold_ref[place : place + count, chan] = piece.reshape(count, unit, lanes)
    half = parts // 2
    bit = me_ref[0]
    keep_ref[...] = hold_ref[pl.ds(bit * half, half)]
    give_ref[...] = hold_ref[pl.ds((1 - bit) * half, half)].astype(BF)


def quarter_kernel(me_ref, held_ref, recv_ref, keep_ref, *refs):
    give_refs, hold_ref = refs[:-1], refs[-1]
    span = keep_ref.shape[0]
    hold_ref[...] = held_ref[...] + recv_ref[...].astype(F32)
    keep_ref[...] = hold_ref[pl.ds(me_ref[0] * span, span)]
    for flip, give_ref in enumerate(give_refs, 1):
        give_ref[...] = hold_ref[pl.ds(lax.bitwise_xor(me_ref[0], flip) * span, span)].astype(BF)


def add_round_kernel(held_ref, *refs):
    total = held_ref[...]
    for recv_ref in refs[:-1]:
        total = total + recv_ref[...].astype(F32)
    refs[-1][...] = total.astype(BF)


def add_pair_kernel(held_ref, recv_ref, out_ref):
    out_ref[...] = (held_ref[...].astype(F32) + recv_ref[...].astype(F32)).astype(BF)


def side_kernel(chans, me_ref, weight_ref, out_ref, grad_ref, turned_ref, *refs):
    self_refs = refs[:chans]
    (hold_ref,) = refs[chans:]
    turned_ref[...] = out_ref[...].T
    hold_ref[...] = nn_dot(weight_ref[...], grad_ref[...]).astype(BF)
    height = self_refs[0].shape[0]
    for shift, self_ref in enumerate(self_refs):
        start = pl.multiple_of(lax.rem(me_ref[0] + shift, chans) * height, height)
        self_ref[...] = hold_ref[pl.ds(start, height), :]


def message_kernel(chans, me_ref, unit_ref, *refs):
    self_refs = refs[:chans]
    packed_refs = refs[chans:]
    nodes = self_refs[0].shape[1]
    units, _, unit, lanes = unit_ref.shape
    for shift, packed_ref in enumerate(packed_refs):
        dest = lax.rem(me_ref[0] + shift, chans)
        piece = unit_ref[:, dest].astype(F32).reshape(units * unit, lanes)
        packed_ref[:, :nodes] = self_refs[shift][...]
        packed_ref[: units * unit, nodes:] = piece.astype(BF)
        packed_ref[units * unit :, nodes:] = jnp.zeros_like(packed_ref[units * unit :, nodes:])


def scatter_kernel(
    cols_ref, counts_ref, vals_ref, scaled_ref, own_ref, far_ref, held_ref, hold_ref, send_ref, val_sems, sems, own_sem
):
    _, depth, size, _ = vals_ref.shape
    rows = scaled_ref.shape[2] // size
    own = own_ref.shape[0]

    def clear():
        hold_ref[...] = jnp.zeros_like(hold_ref)

    def body(index):
        count = counts_ref[index]
        place = pl.ds(pl.multiple_of(lax.rem(index, rows) * size, size), size)
        total = nn_dot(scaled_ref[index // rows, :, place], join_slots(held_ref, index))
        for k in range(depth):
            part = total[:, k * size : (k + 1) * size]
            hold_ref[cols_ref[k, index]] += jnp.where(k < count, part, jnp.zeros_like(part))

    stream_rows(vals_ref, held_ref, val_sems, body, clear)
    copies = sems.shape[0]
    span = far_ref.shape[0] // copies
    for copy in range(copies):
        send_ref[copy * span : (copy + 1) * span] = hold_ref[own + copy * span : own + (copy + 1) * span].astype(BF)
        place = pl.ds(copy * span, span)
        pltpu.make_async_copy(send_ref.at[place], far_ref.at[place], sems.at[copy]).start()
    pltpu.make_async_copy(hold_ref.at[pl.ds(0, own)], own_ref, own_sem).start()
    for copy in range(copies):
        place = pl.ds(copy * span, span)
        pltpu.make_async_copy(send_ref.at[place], far_ref.at[place], sems.at[copy]).wait()
    pltpu.make_async_copy(hold_ref.at[pl.ds(0, own)], own_ref, own_sem).wait()


def unit_kernel(*refs):
    packed_refs = refs[:-1]
    out_ref = refs[-1]
    rows, lanes = out_ref.shape
    total = packed_refs[0][:rows, -lanes:].astype(F32)
    for packed_ref in packed_refs[1:]:
        total = total + packed_ref[:rows, -lanes:].astype(F32)
    out_ref[...] = total.astype(BF)


def spread_kernel(scale, me_ref, held_ref, self_ref, neigh_ref):
    pieces, rows, lanes = held_ref.shape
    half = pieces // 2
    unit_rows = self_ref.shape[0]
    per = unit_rows // rows
    for place in range(pieces):
        away = lax.bitwise_xor(me_ref[0], place)
        first, second, third = away // 4, lax.rem(away // 2, 2), lax.rem(away, 2)
        value = held_ref[second * 4 + third * 2 + first].astype(F32) * scale
        target = self_ref if place < half else neigh_ref
        inside = place % half
        column, row = inside // per, inside % per
        target[row * rows : (row + 1) * rows, column * lanes : (column + 1) * lanes] = value


def near_kernel(shifts, me_ref, own_ref, *refs):
    chans = len(shifts)
    packed_refs = refs[:chans]
    (out_ref,) = refs[chans:]
    blocks, _, size = out_ref.shape
    rows = blocks // chans
    for shift, packed_ref in zip(shifts, packed_refs):
        group = lax.rem(me_ref[0] + (chans - shift), chans)
        for row in range(rows):
            index = group * rows + row
            out_ref[index] = own_ref[index] + packed_ref[:, row * size : (row + 1) * size].astype(F32)


def final_kernel(send_ref, near_ref, back_ref, out_ref, hold_ref):
    slots, dests = send_ref.shape
    blocks, _, size = hold_ref.shape
    hold_ref[...] = near_ref[...]

    def one(dest, carry):
        for slot in range(slots):
            hold_ref[send_ref[slot, dest]] += back_ref[dest, slot].astype(F32)
        return carry

    lax.fori_loop(0, dests, one, 0, unroll=8)
    for block in range(blocks):
        out_ref[:, block * size : (block + 1) * size] = hold_ref[block].astype(BF)


def exchange(chunks, shifts=None):
    count = len(chunks)
    received = list(chunks)
    for shift in shifts or range(count):
        if shift:
            received[shift] = lax.ppermute(chunks[shift], "chan", [(i, (i + shift) % count) for i in range(count)])
    return received


def sds(shape, dtype):
    return jax.ShapeDtypeStruct(shape, dtype)


def halving_order(parts):
    count = parts.bit_length() - 1
    return [bit for bit in (0, 1, 3, 2, 4) if bit < count] + list(range(5, count))


def add_round(kernel, left, *rights):
    return pl.pallas_call(
        kernel,
        out_shape=sds(left.shape, BF),
        in_specs=[vmem()] * (1 + len(rights)),
        out_specs=vmem(),
        compiler_params=params(BIG),
        cost_estimate=cost(0, MIB),
        name="weight_add",
    )(left, *rights)


def per_device(feats, block_vals, block_cols, block_counts, send_list, w_self, w_neigh, bias, cotangent):
    node_count, chan_width = feats.shape
    block_rows, depth, size, _ = block_vals.shape
    parts = lax.axis_size("dom")
    chans = lax.axis_size("chan")
    slots = send_list.shape[2]
    f_in, f_out = w_self.shape
    nodes = node_count // chans
    rows = block_rows // chans
    table = block_rows + parts * slots
    chan = lax.axis_index("chan").astype(jnp.int32)
    part = lax.axis_index("dom").astype(jnp.int32)
    me = chan.reshape(1)
    send = send_list[0].T
    cols = block_cols.T
    feats_t = feats.T
    val_bytes = block_vals.size * 2
    vals = pltpu.with_memory_space_constraint(block_vals, pltpu.HBM)
    block_flops = 2 * block_rows * depth * size * size * chan_width
    layer_flops = 2 * f_in * f_out * nodes
    unit, lanes = 8, 128
    copies, streams = 8, 5

    outgoing = pl.pallas_call(
        pack_kernel,
        out_shape=pltpu.HBM((parts, slots, chan_width, size), BF),
        in_specs=[smem(), vmem()],
        out_specs=hbm(),
        scratch_shapes=[pltpu.VMEM((parts, slots, chan_width, size), BF), pltpu.SemaphoreType.DMA((copies,))],
        compiler_params=params(8),
        cost_estimate=cost(0, 5 * MIB),
        name="pack_outgoing",
    )(
        pltpu.with_memory_space_constraint(send, pltpu.HBM),
        pltpu.with_memory_space_constraint(feats_t, pltpu.HBM),
    )
    incoming = lax.all_to_all(outgoing, "dom", split_axis=0, concat_axis=0, tiled=True)

    feat_chunks = pl.pallas_call(
        split_kernel,
        out_shape=[pltpu.HBM((chan_width, nodes), BF)] * chans,
        in_specs=[smem(), vmem()],
        out_specs=[hbm()] * chans,
        scratch_shapes=[pltpu.SemaphoreType.DMA((chans,))],
        compiler_params=params(BIG),
        cost_estimate=cost(0, MIB),
        name="split_feats",
    )(me, feats_t)
    incoming, feat_chunks = lax.optimization_barrier((incoming, exchange(feat_chunks)))
    feat_chunks = [pltpu.with_memory_space_constraint(chunk, pltpu.HBM) for chunk in feat_chunks]
    feats_own, pre_self, neigh_turned, cot_turned = pl.pallas_call(
        functools.partial(self_kernel, chans),
        out_shape=[sds((f_in, nodes), BF), sds((f_out, nodes), F32), sds((f_out, f_in), BF), sds((f_out, nodes), BF)],
        in_specs=[smem()] + [vmem()] * (4 + chans),
        out_specs=[vmem()] * 4,
        compiler_params=params(BIG),
        cost_estimate=cost(layer_flops, 2 * MIB),
        name="self_part",
    )(me, w_self, bias.reshape(f_out, 1), w_neigh, cotangent, *feat_chunks)

    shifts = sorted(range(chans), key=lambda shift: -min(shift, chans - shift))
    mean_chunks = [None] * chans
    for part_shifts in (shifts[: chans // 2], shifts[chans // 2 :]):
        count = len(part_shifts)
        *chunks, degree = pl.pallas_call(
            functools.partial(gather_kernel, part_shifts, chans),
            out_shape=[pltpu.HBM((chan_width, nodes), BF)] * count + [sds((8, nodes), F32)],
            in_specs=[smem()] * 3 + [vmem()] * 2 + [hbm()],
            out_specs=[hbm()] * count + [vmem()],
            scratch_shapes=[
                pltpu.VMEM((count, rows, depth, size, size), BF),
                pltpu.VMEM((count, chan_width, nodes), BF),
                pltpu.SemaphoreType.DMA((count,)),
                pltpu.SemaphoreType.DMA((count,)),
            ],
            compiler_params=params(16),
            cost_estimate=cost(block_flops // 2, val_bytes // 2 + 3 * MIB),
            name="neighbour_mean",
        )(me, cols, block_counts, feats_t, incoming.reshape(parts * slots, chan_width, size), vals)
        for shift, chunk in zip(part_shifts, chunks):
            mean_chunks[shift] = chunk
    mean_chunks = exchange(mean_chunks, shifts)

    mean, out_t, grad_t, scaled = pl.pallas_call(
        functools.partial(head_kernel, shifts),
        out_shape=[sds((f_in, nodes), BF), sds((f_out, nodes), BF), sds((f_out, nodes), BF), sds((f_in, nodes), BF)],
        in_specs=[smem()] + [vmem()] * (5 + chans),
        out_specs=[vmem()] * 4,
        compiler_params=params(16),
        cost_estimate=cost(2 * layer_flops, 4 * MIB),
        name="layer_head",
    )(me, degree, pre_self, neigh_turned, w_neigh, cot_turned, *[mean_chunks[shift] for shift in shifts])
    scaled = lax.all_to_all(
        scaled.reshape(chans, chan_width, nodes), "chan", split_axis=0, concat_axis=0, tiled=True
    )

    order = halving_order(parts)
    halves, wholes = order[:3], order[3:]
    flips = [[(i, i ^ (1 << bit)) for i in range(parts)] for bit in order]
    bits = [((part >> bit) & 1).reshape(1) for bit in order]
    pieces = parts
    keep, give = pl.pallas_call(
        weight_partial_kernel,
        out_shape=[sds((pieces // 2, chans, unit, lanes), F32), sds((pieces // 2, chans, unit, lanes), BF)],
        in_specs=[smem()] + [vmem()] * 3,
        out_specs=[vmem()] * 2,
        scratch_shapes=[pltpu.VMEM((pieces, chans, unit, lanes), F32)],
        compiler_params=params(BIG),
        cost_estimate=cost(2 * layer_flops, 3 * MIB),
        name="weight_partial",
    )(bits[0], feats_own, mean, grad_t)
    pieces //= 2
    got = lax.ppermute(give, "dom", flips[0])
    quarter = (bits[1] << 1) | bits[2]
    pieces //= 4
    keep, *gives = pl.pallas_call(
        quarter_kernel,
        out_shape=[sds((pieces, chans, unit, lanes), F32)] + [sds((pieces, chans, unit, lanes), BF)] * 3,
        in_specs=[smem()] + [vmem()] * 2,
        out_specs=[vmem()] * 4,
        scratch_shapes=[pltpu.VMEM((pieces * 4, chans, unit, lanes), F32)],
        compiler_params=params(BIG),
        cost_estimate=cost(0, MIB),
        name="weight_quarter",
    )(quarter, keep, got)
    gots = []
    for flip, give in enumerate(gives, 1):
        away = (flip >> 1) << halves[1] | (flip & 1) << halves[2]
        gots.append(lax.ppermute(give, "dom", [(i, i ^ away) for i in range(parts)]))
    total = add_round(add_round_kernel, keep, *gots)
    side = pl.pallas_call(
        functools.partial(side_kernel, chans),
        out_shape=[sds((nodes, f_out), BF)] + [sds((chan_width, nodes), BF)] * chans,
        in_specs=[smem()] + [vmem()] * 3,
        out_specs=[vmem()] * (1 + chans),
        scratch_shapes=[pltpu.VMEM((f_in, nodes), BF)],
        compiler_params=params(BIG),
        cost_estimate=cost(layer_flops, 3 * MIB),
        name="side_grads",
    )(me, w_self, out_t, grad_t)
    for level in range(len(halves), len(order) - 1):
        got = lax.ppermute(total, "dom", flips[level])
        total = add_round(add_pair_kernel, total, got)
    scaled, total, side = lax.optimization_barrier((scaled, total, side))
    out_h = side[0]
    own_grad, far_grad = pl.pallas_call(
        scatter_kernel,
        out_shape=[
            pltpu.HBM((block_rows, chan_width, size), F32),
            pltpu.HBM((parts * slots, chan_width, size), BF),
        ],
        in_specs=[smem(), smem(), hbm(), vmem()],
        out_specs=[hbm(), hbm()],
        scratch_shapes=[
            pltpu.VMEM(block_vals.shape, BF),
            pltpu.VMEM((table, chan_width, size), F32),
            pltpu.VMEM((parts * slots, chan_width, size), BF),
            pltpu.SemaphoreType.DMA((streams,)),
            pltpu.SemaphoreType.DMA((copies,)),
            pltpu.SemaphoreType.DMA,
        ],
        compiler_params=params(24),
        cost_estimate=cost(block_flops, val_bytes + 4 * MIB),
        name="table_grad",
    )(cols, block_counts, vals, scaled)
    total, far_grad = lax.optimization_barrier((total, far_grad))
    back = lax.all_to_all(
        far_grad.reshape(parts, slots, chan_width, size), "dom", split_axis=0, concat_axis=0, tiled=True
    )

    packed = pl.pallas_call(
        functools.partial(message_kernel, chans),
        out_shape=[sds((chan_width, nodes + lanes), BF)] * chans,
        in_specs=[smem()] + [vmem()] * (1 + chans),
        out_specs=[vmem()] * chans,
        compiler_params=params(BIG),
        cost_estimate=cost(0, MIB),
        name="pack_messages",
    )(me, total, *side[1:])
    packed = exchange(packed)
    shifts = sorted(range(chans), key=lambda shift: -min(shift, chans - shift))
    packed = [packed[shift] for shift in shifts]
    held = pl.pallas_call(
        unit_kernel,
        out_shape=sds((pieces * unit, lanes), BF),
        in_specs=[vmem()] * chans,
        out_specs=vmem(),
        compiler_params=params(BIG),
        cost_estimate=cost(0, MIB),
        name="weight_sum",
    )(*packed).reshape(1, pieces * unit, lanes)
    near = pl.pallas_call(
        functools.partial(near_kernel, shifts),
        out_shape=sds((block_rows, chan_width, size), F32),
        in_specs=[smem()] + [vmem()] * (1 + chans),
        out_specs=vmem(),
        compiler_params=params(BIG),
        cost_estimate=cost(0, 3 * MIB),
        name="sum_near",
    )(me, own_grad, *packed)
    held, near = lax.optimization_barrier((held, near))
    held = jnp.concatenate([held, lax.ppermute(held, "dom", flips[0])], axis=0)
    whole, half = 1 << order[-1], 1 << halves[-1]
    across, beside, both = (
        lax.ppermute(held, "dom", [(i, i ^ flip) for i in range(parts)]) for flip in (whole, half, whole | half)
    )
    mine = held.astype(F32) + across.astype(F32)
    other = beside.astype(F32) + both.astype(F32)
    held = jnp.concatenate([mine, other], axis=0).astype(BF)
    held, back, near = lax.optimization_barrier((held.reshape(4, pieces * unit, lanes), back, near))
    grad_feats = pl.pallas_call(
        final_kernel,
        out_shape=sds((chan_width, node_count), BF),
        in_specs=[smem()] + [vmem()] * 2,
        out_specs=vmem(),
        scratch_shapes=[pltpu.VMEM((block_rows, chan_width, size), F32)],
        compiler_params=params(BIG),
        cost_estimate=cost(0, 4 * MIB),
        name="sum_returned",
    )(send, near, back)
    held = jnp.concatenate([held, lax.ppermute(held, "dom", flips[1])], axis=0)
    address = jnp.int32(0)
    for level in range(len(halves)):
        address = address * 2 + bits[level][0]
    grad_w_self, grad_w_neigh = pl.pallas_call(
        functools.partial(spread_kernel, float(node_count * parts) ** (-0.5)),
        out_shape=[sds((chan_width, f_out), F32)] * 2,
        in_specs=[smem(), vmem()],
        out_specs=[vmem()] * 2,
        compiler_params=params(BIG),
        cost_estimate=cost(0, MIB),
        name="weight_spread",
    )(address.reshape(1), held)

    return (out_h, grad_feats.T, grad_w_self, grad_w_neigh)


def solution(mesh):
    return jax.shard_map(
        per_device,
        mesh=mesh,
        in_specs=(
            P("dom", "chan"),
            P("dom", None, None, None),
            P("dom", None),
            P("dom"),
            P("dom", None, None),
            P(),
            P(),
            P(),
            P(("dom", "chan"), None),
        ),
        out_specs=(P(("dom", "chan"), None), P("dom", "chan"), P("chan", None), P("chan", None)),
        check_vma=False,
    )
```

```python
import functools

import jax
import jax.numpy as jnp
from jax import lax
from jax.experimental import pallas as pl
from jax.experimental.pallas import tpu as pltpu
from jax.sharding import PartitionSpec as P

BF = jnp.bfloat16
F32 = jnp.float32
MIB = 1 << 20
BIG = 8


def vmem():
    return pl.BlockSpec(memory_space=pltpu.VMEM)


def hbm():
    return pl.BlockSpec(memory_space=pltpu.HBM)


def smem():
    return pl.BlockSpec(memory_space=pltpu.SMEM)


def params(mib):
    return pltpu.CompilerParams(vmem_limit_bytes=mib * MIB)


def cost(flops, nbytes):
    return pl.CostEstimate(flops=flops, bytes_accessed=nbytes, transcendentals=0)


def nt_dot(left, right):
    return lax.dot_general(left, right, (((1,), (1,)), ((), ())), preferred_element_type=F32)


def nn_dot(left, right):
    return lax.dot_general(left, right, (((1,), (0,)), ((), ())), preferred_element_type=F32)


def pack_kernel(send_ref, feats_ref, out_ref, hold_ref, sems):
    dests, slots, _, size = hold_ref.shape
    copies = sems.shape[0]
    span = dests // copies
    for copy in range(copies):
        for dest in range(copy * span, (copy + 1) * span):
            for slot in range(slots):
                lane = pl.multiple_of(send_ref[slot, dest] * size, size)
                hold_ref[dest, slot] = feats_ref[:, pl.ds(lane, size)]
        place = pl.ds(copy * span, span)
        pltpu.make_async_copy(hold_ref.at[place], out_ref.at[place], sems.at[copy]).start()
    for copy in range(copies):
        place = pl.ds(copy * span, span)
        pltpu.make_async_copy(hold_ref.at[place], out_ref.at[place], sems.at[copy]).wait()


def split_kernel(me_ref, feats_ref, *refs):
    out_refs, sems = refs[:-1], refs[-1]
    chans = len(out_refs)
    width = out_refs[0].shape[1]

    def copy(shift):
        lane = pl.multiple_of(lax.rem(me_ref[0] + shift, chans) * width, width)
        return pltpu.make_async_copy(feats_ref.at[:, pl.ds(lane, width)], out_refs[shift], sems.at[shift])

    for shift in range(chans):
        copy(shift).start()
    for shift in range(chans):
        copy(shift).wait()


def join_slots(vals_ref, row):
    return jnp.concatenate([vals_ref[row, k] for k in range(vals_ref.shape[1])], axis=1)


def stream_rows(vals_ref, held_ref, sems, body, before=None, after=None):
    total = held_ref.shape[0]
    small = total // 8
    large = 2 * small

    def copy(start, span, place):
        rows = pl.ds(start, span)
        return pltpu.make_async_copy(vals_ref.at[rows], held_ref.at[rows], sems.at[place])

    heads = [(place * small, small, place) for place in range(2)]
    tails = total // large - 1
    for start, span, place in heads:
        copy(start, span, place).start()
    for place in range(tails):
        copy((place + 1) * large, large, place + 2).start()
    if before is not None:
        before()

    def work(start, span, place):
        copy(start, span, place).wait()
        for row in range(span):
            body(start + row)
        if after is not None:
            after(start, span, place)

    for start, span, place in heads:
        work(jnp.int32(start), span, place)

    def one(place, carry):
        work((place + 1) * large, large, place + 2)
        return carry

    lax.fori_loop(0, tails, one, 0)


def gather_kernel(
    cols_ref, counts_ref, feats_ref, recv_ref, vals_ref, out_ref, degree_ref, held_ref, mean_ref, sems, out_sems
):
    _, depth, size, _ = vals_ref.shape
    width = feats_ref.shape[0]
    rows = out_ref.shape[2] // size
    own = feats_ref.shape[1] // size
    ones = jnp.ones((16, size), BF)

    def body(index):
        count = counts_ref[index]
        picked = []
        for k in range(depth):
            col = cols_ref[k, index]
            lane = pl.multiple_of(jnp.minimum(col, own - 1) * size, size)
            near = feats_ref[:, pl.ds(lane, size)]
            far = recv_ref[jnp.maximum(col - own, 0)]
            block = jnp.concatenate([jnp.where(col < own, near, far), ones], axis=0)
            picked.append(jnp.where(k < count, block, jnp.zeros_like(block)))
        total = nt_dot(join_slots(held_ref, index), jnp.concatenate(picked, axis=1)).T
        group = index // rows
        place = pl.ds(pl.multiple_of(lax.rem(index, rows) * size, size), size)
        degree_ref[group, :, place] = total[width : width + 8]
        mean_ref[group, :, place] = (total[:width] / total[width : width + 1]).astype(BF)

    def copy(start, span, place):
        groups = pl.ds(start // rows, span // rows)
        return pltpu.make_async_copy(mean_ref.at[groups], out_ref.at[groups], out_sems.at[place])

    stream_rows(vals_ref, held_ref, sems, body, after=lambda *which: copy(*which).start())
    small = held_ref.shape[0] // 8
    copy(0, small, 0).wait()
    copy(small, small, 1).wait()
    for place in range(2, out_sems.shape[0]):
        copy((place - 1) * 2 * small, 2 * small, place).wait()


def self_kernel(chans, me_ref, weight_ref, bias_ref, neigh_ref, cot_ref, *refs):
    chunk_refs = refs[:chans]
    full_ref, pre_ref, neigh_turned_ref, cot_turned_ref = refs[chans:]
    neigh_turned_ref[...] = neigh_ref[...].T
    cot_turned_ref[...] = cot_ref[...].T
    height = chunk_refs[0].shape[0]
    for shift, chunk_ref in enumerate(chunk_refs):
        start = pl.multiple_of(lax.rem(me_ref[0] + (chans - shift), chans) * height, height)
        full_ref[pl.ds(start, height), :] = chunk_ref[...]
    pre_ref[...] = nn_dot(weight_ref[...].T, full_ref[...]) + bias_ref[...]


def head_kernel(me_ref, degree_ref, pre_ref, turned_ref, weight_ref, cot_ref, mean_ref, out_ref, grad_ref, scaled_ref):
    preact = pre_ref[...] + nn_dot(turned_ref[...], mean_ref[...])
    logistic = jax.nn.sigmoid(preact)
    activated = preact * logistic
    slope = logistic * (1.0 + preact * (1.0 - logistic))
    inverse = 1.0 / jnp.sqrt(jnp.mean(activated * activated, axis=0, keepdims=True) + 1e-06)
    unit = activated * inverse
    cot = cot_ref[...].astype(F32)
    grad_act = (cot - unit * jnp.mean(cot * unit, axis=0, keepdims=True)) * inverse
    grad = (grad_act * slope).astype(BF)
    out_ref[...] = unit.astype(BF)
    grad_ref[...] = grad
    mean_grad = nn_dot(weight_ref[...], grad).astype(BF).astype(F32)
    degree = degree_ref[me_ref[0], 0:1, :]
    scaled_ref[...] = (mean_grad / degree).astype(BF)


def weight_partial_kernel(me_ref, feats_ref, mean_ref, grad_ref, keep_ref, give_ref, hold_ref):
    parts, chans, unit, lanes = hold_ref.shape
    grad = grad_ref[...]
    totals = [nt_dot(feats_ref[...], grad), nt_dot(mean_ref[...], grad)]
    width = totals[0].shape[0] // chans
    halves = totals[0].shape[1] // lanes
    count = width // unit
    for which, total in enumerate(totals):
        for half in range(halves):
            place = (which * halves + half) * count
            for chan in range(chans):
                piece = total[chan * width : (chan + 1) * width, half * lanes : (half + 1) * lanes]
                hold_ref[place : place + count, chan] = piece.reshape(count, unit, lanes)
    half = parts // 2
    bit = me_ref[0]
    keep_ref[...] = hold_ref[pl.ds(bit * half, half)]
    give_ref[...] = hold_ref[pl.ds((1 - bit) * half, half)].astype(BF)


def quarter_kernel(me_ref, held_ref, recv_ref, keep_ref, *refs):
    give_refs, hold_ref = refs[:-1], refs[-1]
    span = keep_ref.shape[0]
    hold_ref[...] = held_ref[...] + recv_ref[...].astype(F32)
    keep_ref[...] = hold_ref[pl.ds(me_ref[0] * span, span)]
    for flip, give_ref in enumerate(give_refs, 1):
        give_ref[...] = hold_ref[pl.ds(lax.bitwise_xor(me_ref[0], flip) * span, span)].astype(BF)


def add_round_kernel(held_ref, *refs):
    total = held_ref[...]
    for recv_ref in refs[:-1]:
        total = total + recv_ref[...].astype(F32)
    refs[-1][...] = total.astype(BF)


def add_pair_kernel(held_ref, recv_ref, out_ref):
    out_ref[...] = (held_ref[...].astype(F32) + recv_ref[...].astype(F32)).astype(BF)


def side_kernel(chans, me_ref, weight_ref, out_ref, grad_ref, turned_ref, *refs):
    self_refs = refs[:chans]
    (hold_ref,) = refs[chans:]
    turned_ref[...] = out_ref[...].T
    hold_ref[...] = nn_dot(weight_ref[...], grad_ref[...]).astype(BF)
    height = self_refs[0].shape[0]
    for shift, self_ref in enumerate(self_refs):
        start = pl.multiple_of(lax.rem(me_ref[0] + shift, chans) * height, height)
        self_ref[...] = hold_ref[pl.ds(start, height), :]


def message_kernel(chans, me_ref, unit_ref, *refs):
    self_refs = refs[:chans]
    packed_refs = refs[chans:]
    nodes = self_refs[0].shape[1]
    units, _, unit, lanes = unit_ref.shape
    for shift, packed_ref in enumerate(packed_refs):
        dest = lax.rem(me_ref[0] + shift, chans)
        piece = unit_ref[:, dest].astype(F32).reshape(units * unit, lanes)
        packed_ref[:, :nodes] = self_refs[shift][...]
        packed_ref[: units * unit, nodes:] = piece.astype(BF)
        packed_ref[units * unit :, nodes:] = jnp.zeros_like(packed_ref[units * unit :, nodes:])


def scatter_kernel(
    cols_ref, counts_ref, vals_ref, scaled_ref, own_ref, far_ref, held_ref, hold_ref, send_ref, val_sems, sems, own_sem
):
    _, depth, size, _ = vals_ref.shape
    rows = scaled_ref.shape[2] // size
    own = own_ref.shape[0]

    def clear():
        hold_ref[...] = jnp.zeros_like(hold_ref)

    def body(index):
        count = counts_ref[index]
        place = pl.ds(pl.multiple_of(lax.rem(index, rows) * size, size), size)
        total = nn_dot(scaled_ref[index // rows, :, place], join_slots(held_ref, index))
        for k in range(depth):
            part = total[:, k * size : (k + 1) * size]
            hold_ref[cols_ref[k, index]] += jnp.where(k < count, part, jnp.zeros_like(part))

    stream_rows(vals_ref, held_ref, val_sems, body, clear)
    copies = sems.shape[0]
    span = far_ref.shape[0] // copies
    for copy in range(copies):
        send_ref[copy * span : (copy + 1) * span] = hold_ref[own + copy * span : own + (copy + 1) * span].astype(BF)
        place = pl.ds(copy * span, span)
        pltpu.make_async_copy(send_ref.at[place], far_ref.at[place], sems.at[copy]).start()
    pltpu.make_async_copy(hold_ref.at[pl.ds(0, own)], own_ref, own_sem).start()
    for copy in range(copies):
        place = pl.ds(copy * span, span)
        pltpu.make_async_copy(send_ref.at[place], far_ref.at[place], sems.at[copy]).wait()
    pltpu.make_async_copy(hold_ref.at[pl.ds(0, own)], own_ref, own_sem).wait()


def unit_kernel(*refs):
    packed_refs = refs[:-1]
    out_ref = refs[-1]
    rows, lanes = out_ref.shape
    total = packed_refs[0][:rows, -lanes:].astype(F32)
    for packed_ref in packed_refs[1:]:
        total = total + packed_ref[:rows, -lanes:].astype(F32)
    out_ref[...] = total.astype(BF)


def spread_kernel(scale, me_ref, held_ref, self_ref, neigh_ref):
    pieces, rows, lanes = held_ref.shape
    half = pieces // 2
    unit_rows = self_ref.shape[0]
    per = unit_rows // rows
    for place in range(pieces):
        away = lax.bitwise_xor(me_ref[0], place)
        first, second, third = away // 4, lax.rem(away // 2, 2), lax.rem(away, 2)
        value = held_ref[second * 4 + third * 2 + first].astype(F32) * scale
        target = self_ref if place < half else neigh_ref
        inside = place % half
        column, row = inside // per, inside % per
        target[row * rows : (row + 1) * rows, column * lanes : (column + 1) * lanes] = value


def near_kernel(shifts, me_ref, own_ref, *refs):
    chans = len(shifts)
    packed_refs = refs[:chans]
    (out_ref,) = refs[chans:]
    blocks, _, size = out_ref.shape
    rows = blocks // chans
    for shift, packed_ref in zip(shifts, packed_refs):
        group = lax.rem(me_ref[0] + (chans - shift), chans)
        for row in range(rows):
            index = group * rows + row
            out_ref[index] = own_ref[index] + packed_ref[:, row * size : (row + 1) * size].astype(F32)


def final_kernel(send_ref, near_ref, back_ref, out_ref, hold_ref):
    slots, dests = send_ref.shape
    blocks, _, size = hold_ref.shape
    hold_ref[...] = near_ref[...]

    def one(dest, carry):
        for slot in range(slots):
            hold_ref[send_ref[slot, dest]] += back_ref[dest, slot].astype(F32)
        return carry

    lax.fori_loop(0, dests, one, 0, unroll=8)
    for block in range(blocks):
        out_ref[:, block * size : (block + 1) * size] = hold_ref[block].astype(BF)


def exchange(chunks):
    count = len(chunks)
    received = list(chunks)
    for shift in range(1, count):
        received[shift] = lax.ppermute(chunks[shift], "chan", [(i, (i + shift) % count) for i in range(count)])
    return received


def sds(shape, dtype):
    return jax.ShapeDtypeStruct(shape, dtype)


def halving_order(parts):
    count = parts.bit_length() - 1
    return [bit for bit in (0, 1, 3, 2, 4) if bit < count] + list(range(5, count))


def add_round(kernel, left, *rights):
    return pl.pallas_call(
        kernel,
        out_shape=sds(left.shape, BF),
        in_specs=[vmem()] * (1 + len(rights)),
        out_specs=vmem(),
        compiler_params=params(BIG),
        cost_estimate=cost(0, MIB),
        name="weight_add",
    )(left, *rights)


def per_device(feats, block_vals, block_cols, block_counts, send_list, w_self, w_neigh, bias, cotangent):
    node_count, chan_width = feats.shape
    block_rows, depth, size, _ = block_vals.shape
    parts = lax.axis_size("dom")
    chans = lax.axis_size("chan")
    slots = send_list.shape[2]
    f_in, f_out = w_self.shape
    nodes = node_count // chans
    rows = block_rows // chans
    table = block_rows + parts * slots
    chan = lax.axis_index("chan").astype(jnp.int32)
    part = lax.axis_index("dom").astype(jnp.int32)
    me = chan.reshape(1)
    send = send_list[0].T
    cols = block_cols.T
    feats_t = feats.T
    val_bytes = block_vals.size * 2
    vals = pltpu.with_memory_space_constraint(block_vals, pltpu.HBM)
    block_flops = 2 * block_rows * depth * size * size * chan_width
    layer_flops = 2 * f_in * f_out * nodes
    unit, lanes = 8, 128
    copies, streams = 8, 5

    outgoing = pl.pallas_call(
        pack_kernel,
        out_shape=pltpu.HBM((parts, slots, chan_width, size), BF),
        in_specs=[smem(), vmem()],
        out_specs=hbm(),
        scratch_shapes=[pltpu.VMEM((parts, slots, chan_width, size), BF), pltpu.SemaphoreType.DMA((copies,))],
        compiler_params=params(8),
        cost_estimate=cost(0, 5 * MIB),
        name="pack_outgoing",
    )(
        pltpu.with_memory_space_constraint(send, pltpu.HBM),
        pltpu.with_memory_space_constraint(feats_t, pltpu.HBM),
    )
    incoming = lax.all_to_all(outgoing, "dom", split_axis=0, concat_axis=0, tiled=True)

    feat_chunks = pl.pallas_call(
        split_kernel,
        out_shape=[pltpu.HBM((chan_width, nodes), BF)] * chans,
        in_specs=[smem(), vmem()],
        out_specs=[hbm()] * chans,
        scratch_shapes=[pltpu.SemaphoreType.DMA((chans,))],
        compiler_params=params(BIG),
        cost_estimate=cost(0, MIB),
        name="split_feats",
    )(me, feats_t)
    incoming, feat_chunks = lax.optimization_barrier((incoming, exchange(feat_chunks)))
    feat_chunks = [pltpu.with_memory_space_constraint(chunk, pltpu.HBM) for chunk in feat_chunks]
    feats_own, pre_self, neigh_turned, cot_turned = pl.pallas_call(
        functools.partial(self_kernel, chans),
        out_shape=[sds((f_in, nodes), BF), sds((f_out, nodes), F32), sds((f_out, f_in), BF), sds((f_out, nodes), BF)],
        in_specs=[smem()] + [vmem()] * (4 + chans),
        out_specs=[vmem()] * 4,
        compiler_params=params(BIG),
        cost_estimate=cost(layer_flops, 2 * MIB),
        name="self_part",
    )(me, w_self, bias.reshape(f_out, 1), w_neigh, cotangent, *feat_chunks)

    mean, degree = pl.pallas_call(
        gather_kernel,
        out_shape=[pltpu.HBM((chans, chan_width, nodes), BF), sds((chans, 8, nodes), F32)],
        in_specs=[smem(), smem()] + [vmem()] * 2 + [hbm()],
        out_specs=[hbm(), vmem()],
        scratch_shapes=[
            pltpu.VMEM(block_vals.shape, BF),
            pltpu.VMEM((chans, chan_width, nodes), BF),
            pltpu.SemaphoreType.DMA((streams,)),
            pltpu.SemaphoreType.DMA((streams,)),
        ],
        compiler_params=params(16),
        cost_estimate=cost(block_flops, val_bytes + 3 * MIB),
        name="neighbour_mean",
    )(cols, block_counts, feats_t, incoming.reshape(parts * slots, chan_width, size), vals)
    mean = lax.all_to_all(mean, "chan", split_axis=0, concat_axis=0, tiled=True).reshape(f_in, nodes)

    out_t, grad_t, scaled = pl.pallas_call(
        head_kernel,
        out_shape=[sds((f_out, nodes), BF), sds((f_out, nodes), BF), sds((f_in, nodes), BF)],
        in_specs=[smem()] + [vmem()] * 6,
        out_specs=[vmem()] * 3,
        compiler_params=params(BIG),
        cost_estimate=cost(2 * layer_flops, 4 * MIB),
        name="layer_head",
    )(me, degree, pre_self, neigh_turned, w_neigh, cot_turned, mean)
    scaled = lax.all_to_all(
        scaled.reshape(chans, chan_width, nodes), "chan", split_axis=0, concat_axis=0, tiled=True
    )

    order = halving_order(parts)
    halves, wholes = order[:3], order[3:]
    flips = [[(i, i ^ (1 << bit)) for i in range(parts)] for bit in order]
    bits = [((part >> bit) & 1).reshape(1) for bit in order]
    pieces = parts
    keep, give = pl.pallas_call(
        weight_partial_kernel,
        out_shape=[sds((pieces // 2, chans, unit, lanes), F32), sds((pieces // 2, chans, unit, lanes), BF)],
        in_specs=[smem()] + [vmem()] * 3,
        out_specs=[vmem()] * 2,
        scratch_shapes=[pltpu.VMEM((pieces, chans, unit, lanes), F32)],
        compiler_params=params(BIG),
        cost_estimate=cost(2 * layer_flops, 3 * MIB),
        name="weight_partial",
    )(bits[0], feats_own, mean, grad_t)
    pieces //= 2
    got = lax.ppermute(give, "dom", flips[0])
    quarter = (bits[1] << 1) | bits[2]
    pieces //= 4
    keep, *gives = pl.pallas_call(
        quarter_kernel,
        out_shape=[sds((pieces, chans, unit, lanes), F32)] + [sds((pieces, chans, unit, lanes), BF)] * 3,
        in_specs=[smem()] + [vmem()] * 2,
        out_specs=[vmem()] * 4,
        scratch_shapes=[pltpu.VMEM((pieces * 4, chans, unit, lanes), F32)],
        compiler_params=params(BIG),
        cost_estimate=cost(0, MIB),
        name="weight_quarter",
    )(quarter, keep, got)
    gots = []
    for flip, give in enumerate(gives, 1):
        away = (flip >> 1) << halves[1] | (flip & 1) << halves[2]
        gots.append(lax.ppermute(give, "dom", [(i, i ^ away) for i in range(parts)]))
    total = add_round(add_round_kernel, keep, *gots)
    side = pl.pallas_call(
        functools.partial(side_kernel, chans),
        out_shape=[sds((nodes, f_out), BF)] + [sds((chan_width, nodes), BF)] * chans,
        in_specs=[smem()] + [vmem()] * 3,
        out_specs=[vmem()] * (1 + chans),
        scratch_shapes=[pltpu.VMEM((f_in, nodes), BF)],
        compiler_params=params(BIG),
        cost_estimate=cost(layer_flops, 3 * MIB),
        name="side_grads",
    )(me, w_self, out_t, grad_t)
    for level in range(len(halves), len(order) - 1):
        got = lax.ppermute(total, "dom", flips[level])
        total = add_round(add_pair_kernel, total, got)
    scaled, total, side = lax.optimization_barrier((scaled, total, side))
    out_h = side[0]
    own_grad, far_grad = pl.pallas_call(
        scatter_kernel,
        out_shape=[
            pltpu.HBM((block_rows, chan_width, size), F32),
            pltpu.HBM((parts * slots, chan_width, size), BF),
        ],
        in_specs=[smem(), smem(), hbm(), vmem()],
        out_specs=[hbm(), hbm()],
        scratch_shapes=[
            pltpu.VMEM(block_vals.shape, BF),
            pltpu.VMEM((table, chan_width, size), F32),
            pltpu.VMEM((parts * slots, chan_width, size), BF),
            pltpu.SemaphoreType.DMA((streams,)),
            pltpu.SemaphoreType.DMA((copies,)),
            pltpu.SemaphoreType.DMA,
        ],
        compiler_params=params(24),
        cost_estimate=cost(block_flops, val_bytes + 4 * MIB),
        name="table_grad",
    )(cols, block_counts, vals, scaled)
    total, far_grad = lax.optimization_barrier((total, far_grad))
    back = lax.all_to_all(
        far_grad.reshape(parts, slots, chan_width, size), "dom", split_axis=0, concat_axis=0, tiled=True
    )

    packed = pl.pallas_call(
        functools.partial(message_kernel, chans),
        out_shape=[sds((chan_width, nodes + lanes), BF)] * chans,
        in_specs=[smem()] + [vmem()] * (1 + chans),
        out_specs=[vmem()] * chans,
        compiler_params=params(BIG),
        cost_estimate=cost(0, MIB),
        name="pack_messages",
    )(me, total, *side[1:])
    packed = exchange(packed)
    shifts = sorted(range(chans), key=lambda shift: -min(shift, chans - shift))
    packed = [packed[shift] for shift in shifts]
    held = pl.pallas_call(
        unit_kernel,
        out_shape=sds((pieces * unit, lanes), BF),
        in_specs=[vmem()] * chans,
        out_specs=vmem(),
        compiler_params=params(BIG),
        cost_estimate=cost(0, MIB),
        name="weight_sum",
    )(*packed).reshape(1, pieces * unit, lanes)
    near = pl.pallas_call(
        functools.partial(near_kernel, shifts),
        out_shape=sds((block_rows, chan_width, size), F32),
        in_specs=[smem()] + [vmem()] * (1 + chans),
        out_specs=vmem(),
        compiler_params=params(BIG),
        cost_estimate=cost(0, 3 * MIB),
        name="sum_near",
    )(me, own_grad, *packed)
    held, near = lax.optimization_barrier((held, near))
    held = jnp.concatenate([held, lax.ppermute(held, "dom", flips[0])], axis=0)
    whole, half = 1 << order[-1], 1 << halves[-1]
    across, beside, both = (
        lax.ppermute(held, "dom", [(i, i ^ flip) for i in range(parts)]) for flip in (whole, half, whole | half)
    )
    mine = held.astype(F32) + across.astype(F32)
    other = beside.astype(F32) + both.astype(F32)
    held = jnp.concatenate([mine, other], axis=0).astype(BF)
    held, back, near = lax.optimization_barrier((held.reshape(4, pieces * unit, lanes), back, near))
    grad_feats = pl.pallas_call(
        final_kernel,
        out_shape=sds((chan_width, node_count), BF),
        in_specs=[smem()] + [vmem()] * 2,
        out_specs=vmem(),
        scratch_shapes=[pltpu.VMEM((block_rows, chan_width, size), F32)],
        compiler_params=params(BIG),
        cost_estimate=cost(0, 4 * MIB),
        name="sum_returned",
    )(send, near, back)
    held = jnp.concatenate([held, lax.ppermute(held, "dom", flips[1])], axis=0)
    address = jnp.int32(0)
    for level in range(len(halves)):
        address = address * 2 + bits[level][0]
    grad_w_self, grad_w_neigh = pl.pallas_call(
        functools.partial(spread_kernel, float(node_count * parts) ** (-0.5)),
        out_shape=[sds((chan_width, f_out), F32)] * 2,
        in_specs=[smem(), vmem()],
        out_specs=[vmem()] * 2,
        compiler_params=params(BIG),
        cost_estimate=cost(0, MIB),
        name="weight_spread",
    )(address.reshape(1), held)

    return (out_h, grad_feats.T, grad_w_self, grad_w_neigh)


def solution(mesh):
    return jax.shard_map(
        per_device,
        mesh=mesh,
        in_specs=(
            P("dom", "chan"),
            P("dom", None, None, None),
            P("dom", None),
            P("dom"),
            P("dom", None, None),
            P(),
            P(),
            P(),
            P(("dom", "chan"), None),
        ),
        out_specs=(P(("dom", "chan"), None), P("dom", "chan"), P("chan", None), P("chan", None)),
        check_vma=False,
    )
```
